512 devices in a mesh: elem: 128 (over y, z, core), sub: 4 (over x).
Axes of the slice: x: 4, y: 8, z: 8, core: 2. Of those that a mesh axis runs over, the one named last changes fastest.
Arguments:
- velocity: float32 [2, 8, 512, 128, 128], P(None, None, ('elem', 'sub')), may hold values from -12 to 12
- thickness: float32 [8, 512, 128, 128], P(None, ('elem', 'sub')), may hold values from 0.5 to 1.5
- coriolis: float32 [512, 128, 128], P(('elem', 'sub')), may hold values from 4 to 16
- elem_mass: float32 [512, 32, 32], P(('elem', 'sub')), may hold values from 0.25 to 4
- block_owner: int32 [4, 128], replicated, may hold values from 0 to 511, as said below
Outputs:
- new_velocity: float32 [2, 8, 512, 128, 128], P(None, None, ('elem', 'sub'))
- new_thickness: float32 [8, 512, 128, 128], P(None, ('elem', 'sub'))
The draws below stay inside these ranges and needn't reach their ends.
Inputs may be any that keep to these rules, and one draw needn't show every extreme that they name: `block_owner`: every block index appears once. Each aligned run of 16 block indices (a square run s) fills a 4 x 4 square of blocks whose first column is a multiple of 4, in an order along which successive indices share an edge; the square of run s + 1 lies directly right of that of run s (columns wrap around). Each aligned run of 4 indices (one index of elem) fills a 2 x 2 square whose first row and column are even.
All inputs are finite; a program needn't handle non-finite values.
Results may differ from the reference program's by a relative error of at most 0.0003.
Values sent between devices are 32-bit elements; how exact they have to be, the bound alone decides.
No kernel may reach another device: no remote copies, remote signals or barrier semaphores. Data moves between devices by JAX's collectives and lax.ppermute only.
A program may use at most 64 MiB of HBM per device.

```python
import math
import jax
import jax.numpy as jnp
import numpy as np
from jax import lax

ELEM_SIDE = 32
LEVELS = 8
BLOCK_NODES = 128
BLOCK_ROWS = 4
BLOCK_COLS = 128
DEVICES = 512


def draw_velocity(key, part):
    key = jax.random.fold_in(key, 11)
    block_total = BLOCK_ROWS * BLOCK_COLS
    dims_all = (2, LEVELS, block_total, 4 * ELEM_SIDE, 4 * ELEM_SIDE)
    position = jnp.arange(block_total, dtype=jnp.float32) / (block_total - 1)
    strength = 1.0 + 2.0 * position
    values = jax.random.truncated_normal(key, -4.0, 4.0, dims_all, jnp.float32)
    return values * strength[None, None, :, None, None]


def draw_block_owner(key, part):
    key = jax.random.fold_in(key, 23)
    flip_key, offset_key = jax.random.split(key)
    squares = BLOCK_COLS // 4
    curve_x = jnp.array([0, 0, 1, 1, 2, 3, 3, 2, 2, 3, 3, 2, 1, 1, 0, 0], jnp.int32)
    curve_y = jnp.array([0, 1, 1, 0, 0, 0, 1, 1, 2, 2, 3, 3, 3, 2, 2, 3], jnp.int32)
    flip_bits = jax.random.randint(flip_key, (squares, 3), 0, 2)
    offset_cols = jax.random.randint(offset_key, (), 0, squares)
    mirror_x = jnp.where(flip_bits[:, 0:1] == 1, 3 - curve_x[None, :], curve_x[None, :])
    mirror_y = jnp.where(flip_bits[:, 1:2] == 1, 3 - curve_y[None, :], curve_y[None, :])
    place_x = jnp.where(flip_bits[:, 2:3] == 1, mirror_y, mirror_x)
    place_y = jnp.where(flip_bits[:, 2:3] == 1, mirror_x, mirror_y)
    column = (4 * (jnp.arange(squares, dtype=jnp.int32)[:, None] + offset_cols) + place_x) % (4 * squares)
    owners = jnp.arange(squares, dtype=jnp.int32)[:, None] * 16 + jnp.arange(16, dtype=jnp.int32)[None, :]
    return jnp.zeros((4, 4 * squares), jnp.int32).at[place_y.reshape(-1), column.reshape(-1)].set(owners.reshape(-1))


def block_scale(own_key, shape, cuts, low, largest):
    level = 1.0
    for dim, blocks in cuts:
        steps = jax.random.uniform(jax.random.fold_in(jax.random.fold_in(own_key, 6), dim), (blocks,), jnp.float32, low / len(cuts), largest / len(cuts))
        level = level * jnp.repeat(jnp.exp(steps), shape[dim] // blocks).reshape((-1,) + (1,) * (len(shape) - 1 - dim))
    return level


def setup_inputs(seed: int = 0) -> dict:
    arg_keys = jax.random.split(jax.random.key(seed), 6)
    velocity = draw_velocity(jax.random.fold_in(arg_keys[5], 71), 0)
    thickness = jnp.clip(0.5 + 1.0 * jax.random.uniform(arg_keys[1], (LEVELS, DEVICES, BLOCK_NODES, BLOCK_NODES), jnp.float32) ** block_scale(arg_keys[1], (LEVELS, DEVICES, BLOCK_NODES, BLOCK_NODES), ((1, 512),), -0.2, 0.2), 0.5, 1.5)
    coriolis = jnp.clip(4.0 + 12.0 * jax.random.uniform(arg_keys[2], (DEVICES, BLOCK_NODES, BLOCK_NODES), jnp.float32) ** block_scale(arg_keys[2], (DEVICES, BLOCK_NODES, BLOCK_NODES), ((0, 512),), -0.2, 0.2), 4.0, 16.0)
    elem_mass = jnp.clip(jnp.exp(math.log(4.0) - 2.7725887 * jax.random.uniform(arg_keys[3], (DEVICES, ELEM_SIDE, ELEM_SIDE), jnp.float32) ** block_scale(arg_keys[3], (DEVICES, ELEM_SIDE, ELEM_SIDE), ((0, 512),), -0.2, 0.2)), 0.25, 4.0)
    block_owner = draw_block_owner(jax.random.fold_in(arg_keys[5], 71), 0)
    return {"velocity": velocity, "thickness": thickness, "coriolis": coriolis, "elem_mass": elem_mass, "block_owner": block_owner}


gravity = 1.0
courant = 0.1
hyper_coef = 0.002

def gll_tables():
    points = [-1.0, -1.0 / math.sqrt(5.0), 1.0 / math.sqrt(5.0), 1.0]
    weights = np.array([1.0 / 6.0, 5.0 / 6.0, 5.0 / 6.0, 1.0 / 6.0])
    spread = [math.prod([points[target] - points[others] for others in range(4) if others != target]) for target in range(4)]
    derivative = np.zeros((4, 4))
    for target in range(4):
        for source in range(4):
            if target == source:
                derivative[target, source] = sum((1.0 / (points[target] - points[others]) for others in range(4) if others != target))
            else:
                derivative[target, source] = spread[target] / (spread[source] * (points[target] - points[source]))
    return (weights, 2.0 * derivative)

def shared_sum(surface):
    col_phase = jnp.arange(surface.shape[-1]) % 4
    row_phase = (jnp.arange(surface.shape[-2]) % 4)[:, None]
    across = surface + jnp.where(col_phase == 0, jnp.roll(surface, 1, axis=-1), 0.0) + jnp.where(col_phase == 3, jnp.roll(surface, -1, axis=-1), 0.0)
    blank_row = jnp.zeros_like(across[..., :1, :])
    below_row = jnp.concatenate([blank_row, across[..., :-1, :]], axis=-2)
    above_row = jnp.concatenate([across[..., 1:, :], blank_row], axis=-2)
    return across + jnp.where(row_phase == 0, below_row, 0.0) + jnp.where(row_phase == 3, above_row, 0.0)

def reference(velocity, thickness, coriolis, elem_mass, block_owner):
    weights, derivative = gll_tables()
    derivative = jnp.asarray(derivative, jnp.float32)
    rows_b, cols_b = block_owner.shape
    width_nodes = velocity.shape[-1]
    flat_owner = block_owner.reshape(-1)
    order_back = jnp.argsort(flat_owner).astype(jnp.int32)

    def to_grid(blocks):
        leading = blocks.shape[:-3]
        picked = jnp.take(blocks, flat_owner, axis=-3)
        picked = picked.reshape(leading + (rows_b, cols_b, width_nodes, width_nodes))
        picked = jnp.swapaxes(picked, -3, -2)
        return picked.reshape(leading + (rows_b * width_nodes, cols_b * width_nodes))

    def to_blocks(surface):
        leading = surface.shape[:-2]
        pieces = surface.reshape(leading + (rows_b, width_nodes, cols_b, width_nodes))
        pieces = jnp.swapaxes(pieces, -3, -2).reshape(leading + (rows_b * cols_b, width_nodes, width_nodes))
        return jnp.take(pieces, order_back, axis=-3)

    def along_x(surface):
        dims_all = surface.shape
        blocked = surface.reshape(dims_all[:-1] + (dims_all[-1] // 4, 4))
        result = jnp.einsum('...ej,ij->...ei', blocked, derivative, precision=lax.Precision.HIGHEST)
        return result.reshape(dims_all)

    def along_y(surface):
        dims_all = surface.shape
        blocked = surface.reshape(dims_all[:-2] + (dims_all[-2] // 4, 4, dims_all[-1]))
        result = jnp.einsum('...ejx,ij->...eix', blocked, derivative, precision=lax.Precision.HIGHEST)
        return result.reshape(dims_all)

    def laplace(surface):
        return along_x(along_x(surface)) + along_y(along_y(surface))
    node_weight = jnp.tile(jnp.asarray(weights, jnp.float32), width_nodes // 4)
    node_mass = jnp.repeat(jnp.repeat(elem_mass, 4, -2), 4, -1) * node_weight[:, None] * node_weight[None, :]
    mass_grid = to_grid(node_mass)
    mass_total = shared_sum(mass_grid)
    rotation = to_grid(coriolis)
    east_west = to_grid(velocity[0])
    north_south = to_grid(velocity[1])
    height = to_grid(thickness)
    top_speed = jnp.max(jnp.sqrt(east_west * east_west + north_south * north_south) + jnp.sqrt(gravity * height))
    time_step = courant / top_speed

    def one_level(quantities):
        level_u, level_v, level_h = quantities
        vorticity = along_x(level_v) - along_y(level_u)
        energy = 0.5 * (level_u * level_u + level_v * level_v) + gravity * level_h
        absolute = vorticity + rotation
        tendencies = (absolute * level_v - along_x(energy), -absolute * level_u - along_y(energy), -(along_x(level_h * level_u) + along_y(level_h * level_v)))
        smoothed = [shared_sum(laplace(quantity) * mass_grid) / mass_total for quantity in quantities]
        increments = [shared_sum((tendencies[component] - hyper_coef * laplace(smoothed[component])) * mass_grid) / mass_total for component in range(3)]
        return tuple((quantities[component] + time_step * increments[component] for component in range(3)))
    new_u, new_v, new_h = lax.map(one_level, (east_west, north_south, height))
    return (to_blocks(jnp.stack([new_u, new_v], 0)), to_blocks(new_h))
```

```python
import functools
import math

import jax
import jax.numpy as jnp
import numpy as np
from jax import lax
from jax.experimental import pallas as pl
from jax.experimental.pallas import tpu as pltpu
from jax.sharding import PartitionSpec as P

courant = 0.1
hyper_coef = 0.002
axes = ("elem", "sub")
f32 = jnp.float32
HIGH = lax.Precision.HIGHEST
RIGHT, LEFT, UPPER, LOWER = range(4)
steps8 = ((0, 1), (0, -1), (1, 0), (-1, 0), (1, 1), (1, -1), (-1, 1), (-1, -1))


def gll_tables():
    points = [-1.0, -1.0 / math.sqrt(5.0), 1.0 / math.sqrt(5.0), 1.0]
    weights = np.array([1.0 / 6.0, 5.0 / 6.0, 5.0 / 6.0, 1.0 / 6.0])
    spread = [
        math.prod([points[target] - points[others] for others in range(4) if others != target])
        for target in range(4)
    ]
    derivative = np.zeros((4, 4))
    for target in range(4):
        for source in range(4):
            if target == source:
                derivative[target, source] = sum(
                    1.0 / (points[target] - points[others]) for others in range(4) if others != target
                )
            else:
                derivative[target, source] = spread[target] / (
                    spread[source] * (points[target] - points[source])
                )
    return weights, 2.0 * derivative


WEIGHTS, FIRST = gll_tables()
SECOND = FIRST @ FIRST
CENTRE = float(SECOND[0, 0])


def offset_rows(table):
    rows = np.zeros((7, 4))
    for shift in range(-3, 4):
        for target in range(4):
            if 0 <= target + shift < 4:
                rows[shift + 3, target] = table[target, target + shift]
    return rows


def constant_tables():
    along_x = np.stack([np.kron(np.eye(32), FIRST.T), np.kron(np.eye(32), SECOND.T)])
    expand = np.kron(np.eye(32), WEIGHTS[:, None])
    tiles = np.zeros((27, 8, 128))
    for base, table in ((0, FIRST), (7, SECOND)):
        tiles[base : base + 7] = np.tile(offset_rows(table), (1, 2))[:, :, None]
    tiles[14:21] = np.tile(offset_rows(SECOND), (1, 32))[:, None, :]
    arm_low = np.array([0.0, SECOND[0, 1], SECOND[0, 2], SECOND[0, 3]])
    arm_high = np.array([SECOND[3, 0], SECOND[3, 1], SECOND[3, 2], 0.0])
    tiles[21] = np.tile(arm_low, 32)[None]
    tiles[22] = np.tile(arm_high, 32)[None]
    high = np.array([-hyper_coef * WEIGHTS[a] / WEIGHTS[3] * SECOND[a, 3] for a in range(4)])
    low = np.array([-hyper_coef * WEIGHTS[a] / WEIGHTS[0] * SECOND[a, 0] for a in range(4)])
    tiles[23] = np.concatenate([[0.0, 0.0, 0.0, high[0]], high])[:, None]
    tiles[24] = np.concatenate([low, [low[3], 0.0, 0.0, 0.0]])[:, None]
    across = np.zeros(128)
    across[:5] = [*low, low[3]]
    across[123:] = [high[0], *high]
    tiles[25] = across[None]
    ends = np.zeros(128)
    ends[0] = ends[127] = 1.0
    tiles[26] = ends[None]
    return (
        jnp.asarray(along_x, f32),
        jnp.asarray(expand, f32),
        jnp.asarray(expand.T, f32),
        jnp.asarray(tiles, f32),
    )


def lane_index(rows):
    return lax.broadcasted_iota(jnp.int32, (rows, 128), 1)


def turn(values, steps, axis=1):
    steps = steps % values.shape[axis]
    return values if steps == 0 else pltpu.roll(values, steps, axis)


def share_lanes(values):
    lane = lane_index(values.shape[0])
    first = (lane % 4 == 0) & (lane > 0)
    last = (lane % 4 == 3) & (lane < 127)
    return values + jnp.where(first, turn(values, 1), jnp.where(last, turn(values, 127), 0.0))


def share_rows(values):
    row = lax.broadcasted_iota(jnp.int32, values.shape, 0)
    first = (row % 4 == 0) & (row > 0)
    last = (row % 4 == 3) & (row < 127)
    return values + jnp.where(
        first, turn(values, 1, 0), jnp.where(last, turn(values, 127, 0), 0.0)
    )


def share_block(values):
    return share_rows(share_lanes(values))


def along_rows(values, tiles_ref, base):
    grouped = values.reshape(16, 8, 128)
    total = grouped * tiles_ref[base + 3][None]
    for shift in (-3, -2, -1, 1, 2, 3):
        total = total + pltpu.roll(grouped, (-shift) % 8, 1) * tiles_ref[base + 3 + shift][None]
    return total.reshape(128, 128)


def second_lanes(values, tiles_ref):
    total = values * tiles_ref[17, 0:1]
    for shift in (-3, -2, -1, 1, 2, 3):
        total = total + turn(values, -shift) * tiles_ref[17 + shift, 0:1]
    return total


def pack_end(lines, at_high):
    lane = lane_index(8)
    start = 124 if at_high else 0
    packed = jnp.zeros((8, 128), f32)
    for part in range(3):
        moved = turn(lines[8 * part : 8 * part + 8], 4 * part - start)
        packed = jnp.where(lane // 4 == part, moved, packed)
    return packed


def pack_mass(line, at_high):
    lane = lane_index(8)
    start = 124 if at_high else 0
    wide = jnp.broadcast_to(line, (8, 128))
    packed = jnp.zeros((8, 128), f32)
    for part in range(3):
        packed = jnp.where(lane // 4 == 6 + part, turn(wide, 24 + 4 * part - start), packed)
    return packed


def fold_line(line):
    lane = lane_index(8)
    row = lax.broadcasted_iota(jnp.int32, (8, 128), 0)
    wide = jnp.broadcast_to(line, (8, 128))
    folded = jnp.zeros((8, 128), f32)
    for part in range(4):
        folded = jnp.where((row == part) & (lane // 32 == 2), turn(wide, 64 - 32 * part), folded)
    return folded


def unfold_line(tile):
    lane = lane_index(1)
    line = jnp.zeros((1, 128), f32)
    for part in range(4):
        line = jnp.where(lane // 32 == part, turn(tile[part : part + 1], 32 * part - 64), line)
    return line


def find_tables(device, owner_ref, table_ref, cols_b):
    square = device // 16
    squares = cols_b // 4
    place = jnp.zeros((48, 128), f32)
    index = lax.broadcasted_iota(jnp.int32, (48, 1), 0)
    wanted = ((square + index // 16 + squares - 1) % squares) * 16 + index % 16
    lane = lane_index(1)
    own = jnp.zeros((1, 128), f32)
    for row in range(4):
        line = owner_ref[row : row + 1, :]
        code = (128 * row + lane).astype(f32)
        place = place + jnp.where(line == wanted, code, 0.0)
        own = own + jnp.where(line == device, code, 0.0)
    place = jnp.sum(place, axis=1, keepdims=True).astype(jnp.int32)
    own = jnp.sum(own, axis=1, keepdims=True).astype(jnp.int32)
    own_row, own_col = own // 128, own % 128
    rows, cols = place // 128, place % 128
    member = device % 16
    here_rows, here_cols = rows[16:32], cols[16:32]
    down, over = here_rows - own_row, here_cols - own_col
    inside = jnp.full((16, 1), 8, jnp.int32)
    for number, (step_y, step_x) in enumerate(steps8):
        inside = jnp.where((down == step_y) & (over == step_x), number, inside)
    table_ref[0:16, :] = jnp.broadcast_to(inside, (16, 128))
    crossing = jnp.full((16, 1), 6, jnp.int32)
    sixteen = lax.broadcasted_iota(jnp.int32, (16, 1), 0)
    for side, start, step_x in ((0, 32, 1), (1, 0, -1)):
        picked = sixteen == member
        their = jnp.sum(
            jnp.where(picked, place[start : start + 16], 0).astype(f32), axis=0, keepdims=True
        ).astype(jnp.int32)
        their_row, their_col = their // 128, their % 128
        beside = their_col == (here_cols + step_x + cols_b) % cols_b
        for number, step_y in enumerate((0, 1, -1)):
            crossing = jnp.where(
                beside & (here_rows - their_row == step_y), 3 * side + number, crossing
            )
    table_ref[16:32, :] = jnp.broadcast_to(crossing, (16, 128))
    way = lax.broadcasted_iota(jnp.int32, (8, 1), 0)
    step_y = jnp.zeros((8, 1), jnp.int32)
    step_x = jnp.zeros((8, 1), jnp.int32)
    for number, (along_y, along_x) in enumerate(steps8):
        step_y = jnp.where(way == number, along_y, step_y)
        step_x = jnp.where(way == number, along_x, step_x)
    near_row = own_row + step_y
    near_col = (own_col + step_x + cols_b) % cols_b
    found = jnp.zeros((8, 128), f32)
    for row in range(4):
        line = owner_ref[row : row + 1, :].astype(f32)
        found = found + jnp.where((near_row == row) & (near_col == lane), line, 0.0)
    found = jnp.sum(found, axis=1, keepdims=True).astype(jnp.int32)
    there = (near_row >= 0) & (near_row < 4)
    slot = 2 * (found % 16) + jnp.where(found // 16 == square, 0, 1)
    table_ref[32:40, :] = jnp.broadcast_to(slot, (8, 128))
    table_ref[40:48, :] = jnp.broadcast_to(there.astype(jnp.int32), (8, 128))


def first_kernel(
    cols_b, device_ref, owner_ref, velocity_ref, height_ref, coriolis_ref, elem_mass_ref,
    along_x_ref, expand_ref, expand_t_ref, tiles_ref,
    partial_ref, side_ref, upright_ref, mass_ref, table_ref, top_ref,
    node_mass, inner_inverse, columns, turned, upper_lower,
):
    level = pl.program_id(0)
    lane = lane_index(128)

    @pl.when(level == 0)
    def _():
        rows = jnp.dot(
            expand_ref[...], elem_mass_ref[0], precision=HIGH, preferred_element_type=f32
        )
        mass = jnp.dot(rows, expand_t_ref[...], precision=HIGH, preferred_element_type=f32)
        node_mass[...] = mass
        local_mass = share_block(mass)
        mass_ref[...] = local_mass
        row = lax.broadcasted_iota(jnp.int32, (128, 128), 0)
        inner = (row > 0) & (row < 127) & (lane > 0) & (lane < 127)
        inner_inverse[...] = jnp.where(inner, 1.0 / local_mass, 0.0)
        columns[...] = jnp.where(lane // 2 == 48, turn(mass, 97), 0.0)
        find_tables(device_ref[0], owner_ref, table_ref, cols_b)
        top_ref[...] = jnp.zeros_like(top_ref)

    mass = node_mass[...]
    east = velocity_ref[0, 0]
    north = velocity_ref[1, 0]
    height = height_ref[0]
    squared = east * east + north * north
    energy = 0.5 * squared + height
    speed = jnp.max(jnp.sqrt(squared) + jnp.sqrt(height))
    top_ref[...] = jnp.maximum(top_ref[...], speed)
    flux_x, flux_y = height * east, height * north
    first_x = jnp.dot(
        jnp.concatenate([north, energy, flux_x], 0), along_x_ref[0],
        precision=HIGH, preferred_element_type=f32,
    )
    second_x = jnp.dot(
        jnp.concatenate([east, north, height], 0), along_x_ref[1],
        precision=HIGH, preferred_element_type=f32,
    )
    absolute = first_x[:128] - along_rows(east, tiles_ref, 0) + coriolis_ref[0]
    tendencies = (
        absolute * north - first_x[128:256],
        -absolute * east - along_rows(energy, tiles_ref, 0),
        -(first_x[256:] + along_rows(flux_y, tiles_ref, 0)),
    )
    smoothed = []
    for part, values in enumerate((east, north, height)):
        lap = second_x[128 * part : 128 * part + 128] + along_rows(values, tiles_ref, 7)
        local = share_block(lap * mass)
        place = 8 * part + level
        upper_lower[0, pl.ds(place, 1), :] = local[127:128]
        upper_lower[1, pl.ds(place, 1), :] = local[0:1]
        columns[...] = jnp.where(
            lane // 2 == place, pltpu.roll(local, 2 * place + 1, 1), columns[...]
        )
        smoothed.append(local * inner_inverse[...])
    second_x = jnp.dot(
        jnp.concatenate(smoothed, 0), along_x_ref[1], precision=HIGH, preferred_element_type=f32
    )
    for part in range(3):
        lap = second_x[128 * part : 128 * part + 128] + along_rows(smoothed[part], tiles_ref, 7)
        local = share_block((tendencies[part] - hyper_coef * lap) * mass)
        partial_ref[part, 0] = local
        place = 24 + 8 * part + level
        upper_lower[0, pl.ds(place, 1), :] = local[127:128]
        upper_lower[1, pl.ds(place, 1), :] = local[0:1]
        columns[...] = jnp.where(
            lane // 2 == place, pltpu.roll(local, 2 * place + 1, 1), columns[...]
        )

    @pl.when(level == 7)
    def _():
        turned[...] = jnp.transpose(columns[...])
        for place in range(48):
            side_ref[0, place : place + 1, :] = turned[2 * place : 2 * place + 1, :]
            side_ref[1, place : place + 1, :] = turned[2 * place + 1 : 2 * place + 2, :]
        mass_lines = (
            turned[96:97, :], turned[97:98, :], node_mass[127:128, :], node_mass[0:1, :],
        )
        smooth_lines = (
            side_ref[0, 0:24, :], side_ref[1, 0:24, :], upper_lower[0, 0:24, :], upper_lower[1, 0:24, :],
        )
        change_lines = {
            UPPER: upper_lower[0, 24:48, :], LOWER: upper_lower[1, 24:48, :],
        }
        ends = {}
        for side in range(4):
            local_mass = share_lanes(mass_lines[side])
            for high in (False, True):
                ends[side, high] = pack_end(smooth_lines[side], high) + pack_mass(local_mass, high)
        upright_ref[0, 0:48, :] = upper_lower[0, 0:48, :]
        upright_ref[1, 0:48, :] = upper_lower[1, 0:48, :]
        extras = (
            ends[UPPER, True] + turn(ends[LOWER, True], 12),
            ends[UPPER, False] + turn(ends[LOWER, False], 12),
            ends[LEFT, True] + turn(ends[RIGHT, True], 12),
            ends[LEFT, False] + turn(ends[RIGHT, False], 12),
        )
        for side in range(4):
            tile = extras[side] + fold_line(mass_lines[side])
            if side < 2:
                side_ref[side, 48:56, :] = tile
            else:
                upright_ref[side - 2, 48:56, :] = tile
        for across, sideways in ((RIGHT, True), (LEFT, False)):
            for number, (along, upward) in enumerate(((UPPER, True), (LOWER, False))):
                tile = ends[along, sideways] + turn(ends[across, upward], 12)
                tile = tile + turn(pack_end(change_lines[along], sideways), 48)
                side_ref[across, 56 + 8 * number : 64 + 8 * number, :] = tile


def pack_kernel(table_ref, side_ref, upright_ref, ahead_ref, behind_ref, tops_ref, send_ref):
    lane = lane_index(8)
    top = jnp.max(tops_ref[...])
    for place in range(16):
        message = table_ref[place, 0]

        @pl.when(message < 2)
        def _():
            send_ref[2 * place] = side_ref[jnp.minimum(message, 1), 0:56, :]

        @pl.when((message >= 2) & (message < 4))
        def _():
            send_ref[2 * place] = upright_ref[jnp.clip(message - 2, 0, 1)]

        for corner, (side, row) in enumerate(((0, 56), (1, 56), (0, 64), (1, 64))):

            @pl.when(message == 4 + corner)
            def _(side=side, row=row):
                send_ref[2 * place, 48:56, :] = side_ref[side, row : row + 8, :]

        send_ref[2 * place, 48:56, :] = jnp.where(lane >= 96, top, send_ref[2 * place, 48:56, :])
        crossing = table_ref[16 + place, 0]
        for base, ref in ((0, ahead_ref), (3, behind_ref)):

            @pl.when(crossing == base)
            def _(ref=ref):
                send_ref[2 * place + 1] = ref[0:56, :]

            @pl.when(crossing == base + 1)
            def _(ref=ref):
                send_ref[2 * place + 1, 48:56, :] = ref[56:64, :]

            @pl.when(crossing == base + 2)
            def _(ref=ref):
                send_ref[2 * place + 1, 48:56, :] = ref[64:72, :]


def edge_terms(table_ref, side_ref, upright_ref, received_ref, tiles_ref):
    lane = lane_index(1)

    def message(way, start, stop):
        values = received_ref[table_ref[32 + way, 0], start:stop, :]
        return jnp.where(table_ref[40 + way, 0] > 0, values, 0.0)

    own = (
        side_ref[0, 0:24, :], side_ref[1, 0:24, :], upright_ref[0, 0:24, :], upright_ref[1, 0:24, :],
    )
    own_mass = (
        unfold_line(side_ref[0, 48:56, :]), unfold_line(side_ref[1, 48:56, :]),
        unfold_line(upright_ref[0, 48:56, :]), unfold_line(upright_ref[1, 48:56, :]),
    )
    near = [message(side, 0, 24) for side in range(4)]
    change = [message(side, 24, 48) for side in range(4)]
    extra = [message(side, 48, 56) for side in range(4)]
    mass = [unfold_line(extra[side]) for side in range(4)]
    shared_mass = [share_lanes(mass[side]) for side in range(4)]
    total = [own[side] + near[side] for side in range(4)]
    total_mass = [share_lanes(own_mass[side]) + shared_mass[side] for side in range(4)]
    corners = []
    for along in (UPPER, LOWER):
        for across in (RIGHT, LEFT):
            corner = 4 + 2 * (along - UPPER) + across
            at_x = 127 if across == RIGHT else 0
            at_y = 127 if along == UPPER else 0
            tile = message(corner, 48, 56)
            end_x = 0 if across == RIGHT else 3

            def spread_out(packed, start, at_x=at_x):
                return jnp.concatenate(
                    [turn(packed, at_x - start - 4 * part) for part in range(3)], 0
                )

            far = spread_out(tile, end_x)
            far_mass = turn(tile, at_x - 24 - end_x)[0:1]
            corners.append((along, across, at_x, at_y, tile, far_mass, spread_out))
            on_x, on_y = lane == at_x, lane == at_y
            total[along] = total[along] + jnp.where(
                on_x, turn(near[across], at_x - at_y) + far, 0.0
            )
            total_mass[along] = total_mass[along] + jnp.where(
                on_x, turn(mass[across], at_x - at_y) + far_mass, 0.0
            )
            total[across] = total[across] + jnp.where(
                on_y, turn(near[along] + far, at_y - at_x), 0.0
            )
            total_mass[across] = total_mass[across] + jnp.where(
                on_y, turn(mass[along] + far_mass, at_y - at_x), 0.0
            )
    smooth = [total[side] / total_mass[side] for side in range(4)]
    curve = [second_lanes(smooth[side], tiles_ref) for side in range(4)]
    added = [
        change[side]
        - hyper_coef
        * (shared_mass[side] * CENTRE * smooth[side] + share_lanes(mass[side] * curve[side]))
        for side in range(4)
    ]

    def arm(beside, diagonal, coefs):
        both = beside + diagonal
        weight = turn(both, -24)
        value = jnp.where(weight > 0.0, both / jnp.where(weight > 0.0, weight, 1.0), 0.0) * coefs
        value = value + turn(value, -1)
        return value + turn(value, -2)

    for along, across, at_x, at_y, tile, far_mass, spread_out in corners:
        beside = extra[across] if along == UPPER else turn(extra[across], -12)
        arm_x = spread_out(arm(beside, tile, tiles_ref[21 if across == RIGHT else 22]), 0)
        beside = extra[along] if across == LEFT else turn(extra[along], -12)
        arm_y = spread_out(
            arm(beside, turn(tile, -12), tiles_ref[21 if along == UPPER else 22]), 0
        )
        middle = CENTRE * smooth[along]
        arm_x, arm_y = arm_x + middle, arm_y + middle
        own_x = curve[along]
        own_y = turn(curve[across], at_x - at_y)
        mass_x = turn(mass[across], at_x - at_y)
        end_x = 0 if across == RIGHT else 3
        value = (
            turn(change[across], at_x - at_y) + change[along] + spread_out(tile, 48 + end_x)
        ) - hyper_coef * (
            mass_x * (arm_x + own_y) + mass[along] * (own_x + arm_y) + far_mass * (arm_x + arm_y)
        )
        added[along] = jnp.where(lane == at_x, value, added[along])
    ends = (lane == 0) | (lane == 127)
    plain, edge = [], []
    for side in range(4):
        line = smooth[side] if side >= UPPER else jnp.where(ends, 0.0, smooth[side])
        outside = added[side] if side >= UPPER else jnp.where(ends, 0.0, added[side])
        bend = curve[side] if side >= UPPER else second_lanes(line, tiles_ref)
        plain.append(share_lanes(own_mass[side] * line))
        edge.append(outside - hyper_coef * share_lanes(own_mass[side] * bend))
    return plain, edge, total_mass


def last_kernel(
    table_ref, side_ref, upright_ref, received_ref, tiles_ref, mass_ref,
    velocity_ref, height_ref, partial_ref, new_velocity_ref, new_height_ref,
    rows, columns, inverse,
):
    level = pl.program_id(0)
    lane = lane_index(128)

    @pl.when(level == 0)
    def _():
        plain, edge, total_mass = edge_terms(
            table_ref, side_ref, upright_ref, received_ref, tiles_ref
        )
        rows[0] = plain[UPPER]
        rows[1] = plain[LOWER]
        rows[2] = edge[UPPER]
        rows[3] = edge[LOWER]
        stacked = jnp.concatenate(
            [plain[LEFT], plain[RIGHT], edge[LEFT], edge[RIGHT]]
            + [jnp.broadcast_to(total_mass[side], (16, 128)) for side in (LEFT, RIGHT)],
            0,
        )
        columns[...] = jnp.transpose(stacked)
        sides = columns[...]
        mass = mass_ref[...]
        mass = jnp.where(lane == 0, sides[:, 96:97], mass)
        mass = jnp.where(lane == 127, sides[:, 112:113], mass)
        row = lax.broadcasted_iota(jnp.int32, (128, 128), 0)
        mass = jnp.where(row == 127, total_mass[UPPER], mass)
        mass = jnp.where(row == 0, total_mass[LOWER], mass)
        top = jnp.zeros((8, 128), f32)
        for place in range(16):
            top = jnp.maximum(top, received_ref[2 * place, 48:56, :])
        top = jnp.max(jnp.where(lane_index(8) >= 96, top, 0.0))
        inverse[...] = (courant / top) / mass

    moved = pltpu.roll(columns[...], (128 - level) % 128, 1)
    factor = inverse[...]
    left = lane < 64
    across = tiles_ref[25, 0:1]
    ends = tiles_ref[26, 0:1]
    for part in range(3):
        start = 8 * part
        plain = jnp.where(left, moved[:, start : start + 1], moved[:, start + 24 : start + 25])
        edge = jnp.where(left, moved[:, start + 48 : start + 49], moved[:, start + 72 : start + 73])
        value = partial_ref[part, 0] + across * plain + ends * edge
        place = pl.ds(start + level, 1)
        upper = tiles_ref[23] * rows[0, place, :]
        lower = tiles_ref[24] * rows[1, place, :]
        row = lax.broadcasted_iota(jnp.int32, (8, 128), 0)
        upper = upper + jnp.where(row == 7, rows[2, place, :], 0.0)
        lower = lower + jnp.where(row == 0, rows[3, place, :], 0.0)
        value = jnp.concatenate([value[:8] + lower, value[8:120], value[120:] + upper], 0)
        if part < 2:
            new_velocity_ref[part, 0] = velocity_ref[part, 0] + factor * value
        else:
            new_height_ref[0] = height_ref[0] + factor * value


def whole(shape, space=None):
    if space is None:
        return pl.BlockSpec(shape, lambda level: (0,) * len(shape))
    return pl.BlockSpec(memory_space=space)


def per_device(velocity, thickness, coriolis, elem_mass, block_owner):
    cols_b = block_owner.shape[1]
    count = 4 * cols_b
    velocity = velocity[:, :, 0]
    thickness = thickness[:, 0]
    along_x, expand, expand_t, tiles = constant_tables()
    device = (lax.axis_index("elem") * lax.axis_size("sub") + lax.axis_index("sub")).reshape(1)
    if cols_b < 128:
        block_owner = jnp.pad(block_owner, ((0, 0), (0, 128 - cols_b)), constant_values=-1)
    pair = pl.BlockSpec((2, 1, 128, 128), lambda level: (0, level, 0, 0))
    single = pl.BlockSpec((1, 128, 128), lambda level: (level, 0, 0))
    triple = pl.BlockSpec((3, 1, 128, 128), lambda level: (0, level, 0, 0))
    shape = jax.ShapeDtypeStruct
    params = pltpu.CompilerParams(
        dimension_semantics=("arbitrary",), vmem_limit_bytes=32 * 1024 * 1024
    )
    partial, side, upright, local_mass, table, top = pl.pallas_call(
        functools.partial(first_kernel, cols_b),
        grid=(8,),
        in_specs=[
            whole((1,), pltpu.SMEM), whole((4, 128)), pair, single, whole((1, 128, 128)),
            whole((1, 32, 32)), whole((2, 128, 128)), whole((128, 32)), whole((32, 128)),
            whole((27, 8, 128)),
        ],
        out_specs=[
            triple, whole((2, 72, 128)), whole((2, 56, 128)), whole((128, 128)), whole((48, 128)),
            whole((32, 128)),
        ],
        out_shape=[
            shape((3, 8, 128, 128), f32), shape((2, 72, 128), f32), shape((2, 56, 128), f32),
            shape((128, 128), f32), shape((48, 128), jnp.int32), shape((32, 128), f32),
        ],
        scratch_shapes=[
            pltpu.VMEM((128, 128), f32), pltpu.VMEM((128, 128), f32), pltpu.VMEM((128, 128), f32),
            pltpu.VMEM((128, 128), f32), pltpu.VMEM((2, 48, 128), f32),
        ],
        compiler_params=params,
        name="first",
    )(device, block_owner, velocity, thickness, coriolis, elem_mass, along_x, expand, expand_t, tiles)
    squares = count // 16
    same_place = [[16 * s + i for s in range(squares)] for i in range(16)]
    same_square = [[16 * s + i for i in range(16)] for s in range(squares)]
    tops = lax.all_to_all(
        top[:squares], axes, 0, 0, axis_index_groups=same_place, tiled=True
    )
    ahead = lax.ppermute(side[1], axes, [(b, (b - 16) % count) for b in range(count)])
    behind = lax.ppermute(side[0], axes, [(b, (b + 16) % count) for b in range(count)])
    send = pl.pallas_call(
        pack_kernel,
        in_specs=[whole((48, 128), pltpu.SMEM)] + [pl.BlockSpec(memory_space=pltpu.VMEM)] * 5,
        out_specs=pl.BlockSpec(memory_space=pltpu.VMEM),
        out_shape=shape((32, 56, 128), f32),
        compiler_params=pltpu.CompilerParams(vmem_limit_bytes=32 * 1024 * 1024),
        name="pack",
    )(table, side, upright, ahead, behind, tops)
    received = lax.all_to_all(
        send.reshape(16, 112, 128), axes, 0, 0, axis_index_groups=same_square, tiled=True
    ).reshape(32, 56, 128)
    new_velocity, new_thickness = pl.pallas_call(
        last_kernel,
        grid=(8,),
        in_specs=[
            whole((48, 128), pltpu.SMEM), whole((2, 72, 128)), whole((2, 56, 128)),
            whole((32, 56, 128)), whole((27, 8, 128)), whole((128, 128)), pair, single, triple,
        ],
        out_specs=[pair, single],
        out_shape=[shape((2, 8, 128, 128), f32), shape((8, 128, 128), f32)],
        scratch_shapes=[
            pltpu.VMEM((4, 24, 128), f32), pltpu.VMEM((128, 128), f32), pltpu.VMEM((128, 128), f32),
        ],
        compiler_params=params,
        name="last",
    )(table, side, upright, received, tiles, local_mass, velocity, thickness, partial)
    return new_velocity[:, :, None], new_thickness[:, None]


def solution(mesh):
    return jax.shard_map(
        per_device,
        mesh=mesh,
        in_specs=(
            P(None, None, axes, None, None),
            P(None, axes, None, None),
            P(axes, None, None),
            P(axes, None, None),
            P(),
        ),
        out_specs=(
            P(None, None, axes, None, None),
            P(None, axes, None, None),
        ),
        check_vma=False,
    )
```

```python
import functools
import math

import jax
import jax.numpy as jnp
import numpy as np
from jax import lax
from jax.experimental import pallas as pl
from jax.experimental.pallas import tpu as pltpu
from jax.sharding import PartitionSpec as P

courant = 0.1
hyper_coef = 0.002
TOP_ROWS = 256
MIB = 1024 * 1024
EDGE_VMEM = 60 * MIB
PACK_VMEM = 60 * MIB
BLOCK_VMEM = 60 * MIB
LAST_VMEM = 60 * MIB
axes = ("elem", "sub")
f32 = jnp.float32
HIGH = lax.Precision.HIGHEST
RIGHT, LEFT, UPPER, LOWER = range(4)
steps8 = ((0, 1), (0, -1), (1, 0), (-1, 0), (1, 1), (1, -1), (-1, 1), (-1, -1))


def gll_tables():
    points = [-1.0, -1.0 / math.sqrt(5.0), 1.0 / math.sqrt(5.0), 1.0]
    weights = np.array([1.0 / 6.0, 5.0 / 6.0, 5.0 / 6.0, 1.0 / 6.0])
    spread = [
        math.prod([points[target] - points[others] for others in range(4) if others != target])
        for target in range(4)
    ]
    derivative = np.zeros((4, 4))
    for target in range(4):
        for source in range(4):
            if target == source:
                derivative[target, source] = sum(
                    1.0 / (points[target] - points[others]) for others in range(4) if others != target
                )
            else:
                derivative[target, source] = spread[target] / (
                    spread[source] * (points[target] - points[source])
                )
    return weights, 2.0 * derivative


WEIGHTS, FIRST = gll_tables()
SECOND = FIRST @ FIRST
CENTRE = float(SECOND[0, 0])


def offset_rows(table):
    rows = np.zeros((7, 4))
    for shift in range(-3, 4):
        for target in range(4):
            if 0 <= target + shift < 4:
                rows[shift + 3, target] = table[target, target + shift]
    return rows


def constant_tables():
    along_x = np.stack([np.kron(np.eye(32), FIRST.T), np.kron(np.eye(32), SECOND.T)])
    expand = np.kron(np.eye(32), WEIGHTS[:, None])
    tiles = np.zeros((27, 8, 128))
    for base, table in ((0, FIRST), (7, SECOND)):
        tiles[base : base + 7] = np.tile(offset_rows(table), (1, 2))[:, :, None]
    tiles[14:21] = np.tile(offset_rows(SECOND), (1, 32))[:, None, :]
    arm_low = np.array([0.0, SECOND[0, 1], SECOND[0, 2], SECOND[0, 3]])
    arm_high = np.array([SECOND[3, 0], SECOND[3, 1], SECOND[3, 2], 0.0])
    tiles[21] = np.tile(arm_low, 32)[None]
    tiles[22] = np.tile(arm_high, 32)[None]
    high = np.array([-hyper_coef * WEIGHTS[a] / WEIGHTS[3] * SECOND[a, 3] for a in range(4)])
    low = np.array([-hyper_coef * WEIGHTS[a] / WEIGHTS[0] * SECOND[a, 0] for a in range(4)])
    tiles[23] = np.concatenate([[0.0, 0.0, 0.0, high[0]], high])[:, None]
    tiles[24] = np.concatenate([low, [low[3], 0.0, 0.0, 0.0]])[:, None]
    across = np.zeros(128)
    across[:5] = [*low, low[3]]
    across[123:] = [high[0], *high]
    tiles[25] = across[None]
    ends = np.zeros(128)
    ends[0] = ends[127] = 1.0
    tiles[26] = ends[None]
    return (
        jnp.asarray(along_x, f32),
        jnp.asarray(expand, f32),
        jnp.asarray(expand.T, f32),
        jnp.asarray(tiles, f32),
    )


def lane_index(rows):
    return lax.broadcasted_iota(jnp.int32, (rows, 128), 1)


def turn(values, steps, axis=1):
    steps = steps % values.shape[axis]
    return values if steps == 0 else pltpu.roll(values, steps, axis)


def share_lanes(values):
    lane = lane_index(values.shape[0])
    first = (lane % 4 == 0) & (lane > 0)
    last = (lane % 4 == 3) & (lane < 127)
    return values + jnp.where(first, turn(values, 1), jnp.where(last, turn(values, 127), 0.0))


def share_rows(values):
    row = lax.broadcasted_iota(jnp.int32, values.shape, 0)
    first = (row % 4 == 0) & (row > 0)
    last = (row % 4 == 3) & (row < 127)
    return values + jnp.where(
        first, turn(values, 1, 0), jnp.where(last, turn(values, 127, 0), 0.0)
    )


def share_block(values):
    return share_rows(share_lanes(values))


def along_rows(values, tiles_ref, base):
    grouped = values.reshape(16, 8, 128)
    total = grouped * tiles_ref[base + 3][None]
    for shift in (-3, -2, -1, 1, 2, 3):
        total = total + pltpu.roll(grouped, (-shift) % 8, 1) * tiles_ref[base + 3 + shift][None]
    return total.reshape(128, 128)


def second_lanes(values, tiles_ref):
    total = values * tiles_ref[17, 0:1]
    for shift in (-3, -2, -1, 1, 2, 3):
        total = total + turn(values, -shift) * tiles_ref[17 + shift, 0:1]
    return total


def pack_end(lines, at_high):
    lane = lane_index(8)
    start = 124 if at_high else 0
    packed = jnp.zeros((8, 128), f32)
    for part in range(3):
        moved = turn(lines[8 * part : 8 * part + 8], 4 * part - start)
        packed = jnp.where(lane // 4 == part, moved, packed)
    return packed


def pack_mass(line, at_high):
    lane = lane_index(8)
    start = 124 if at_high else 0
    wide = jnp.broadcast_to(line, (8, 128))
    packed = jnp.zeros((8, 128), f32)
    for part in range(3):
        packed = jnp.where(lane // 4 == 6 + part, turn(wide, 24 + 4 * part - start), packed)
    return packed


def fold_line(line):
    lane = lane_index(8)
    row = lax.broadcasted_iota(jnp.int32, (8, 128), 0)
    wide = jnp.broadcast_to(line, (8, 128))
    folded = jnp.zeros((8, 128), f32)
    for part in range(4):
        folded = jnp.where((row == part) & (lane // 32 == 2), turn(wide, 64 - 32 * part), folded)
    return folded


def unfold_line(tile):
    lane = lane_index(1)
    line = jnp.zeros((1, 128), f32)
    for part in range(4):
        line = jnp.where(lane // 32 == part, turn(tile[part : part + 1], 32 * part - 64), line)
    return line


def find_tables(device, owner_ref, table_ref, cols_b):
    square = device // 16
    squares = cols_b // 4
    place = jnp.zeros((48, 128), f32)
    index = lax.broadcasted_iota(jnp.int32, (48, 1), 0)
    wanted = ((square + index // 16 + squares - 1) % squares) * 16 + index % 16
    lane = lane_index(1)
    own = jnp.zeros((1, 128), f32)
    for row in range(4):
        line = owner_ref[row : row + 1, :]
        code = (128 * row + lane).astype(f32)
        place = place + jnp.where(line == wanted, code, 0.0)
        own = own + jnp.where(line == device, code, 0.0)
    place = jnp.sum(place, axis=1, keepdims=True).astype(jnp.int32)
    own = jnp.sum(own, axis=1, keepdims=True).astype(jnp.int32)
    own_row, own_col = own // 128, own % 128
    rows, cols = place // 128, place % 128
    member = device % 16
    here_rows, here_cols = rows[16:32], cols[16:32]
    down, over = here_rows - own_row, here_cols - own_col
    inside = jnp.full((16, 1), 8, jnp.int32)
    for number, (step_y, step_x) in enumerate(steps8):
        inside = jnp.where((down == step_y) & (over == step_x), number, inside)
    table_ref[0:16, :] = jnp.broadcast_to(inside, (16, 128))
    crossing = jnp.full((16, 1), 6, jnp.int32)
    sixteen = lax.broadcasted_iota(jnp.int32, (16, 1), 0)
    for side, start, step_x in ((0, 32, 1), (1, 0, -1)):
        picked = sixteen == member
        their = jnp.sum(
            jnp.where(picked, place[start : start + 16], 0).astype(f32), axis=0, keepdims=True
        ).astype(jnp.int32)
        their_row, their_col = their // 128, their % 128
        beside = their_col == (here_cols + step_x + cols_b) % cols_b
        for number, step_y in enumerate((0, 1, -1)):
            crossing = jnp.where(
                beside & (here_rows - their_row == step_y), 3 * side + number, crossing
            )
    table_ref[16:32, :] = jnp.broadcast_to(crossing, (16, 128))
    way = lax.broadcasted_iota(jnp.int32, (8, 1), 0)
    step_y = jnp.zeros((8, 1), jnp.int32)
    step_x = jnp.zeros((8, 1), jnp.int32)
    for number, (along_y, along_x) in enumerate(steps8):
        step_y = jnp.where(way == number, along_y, step_y)
        step_x = jnp.where(way == number, along_x, step_x)
    near_row = own_row + step_y
    near_col = (own_col + step_x + cols_b) % cols_b
    found = jnp.zeros((8, 128), f32)
    for row in range(4):
        line = owner_ref[row : row + 1, :].astype(f32)
        found = found + jnp.where((near_row == row) & (near_col == lane), line, 0.0)
    found = jnp.sum(found, axis=1, keepdims=True).astype(jnp.int32)
    there = (near_row >= 0) & (near_row < 4)
    slot = 2 * (found % 16) + jnp.where(found // 16 == square, 0, 1)
    table_ref[32:40, :] = jnp.broadcast_to(slot, (8, 128))
    table_ref[40:48, :] = jnp.broadcast_to(there.astype(jnp.int32), (8, 128))


def share_band(values):
    across = share_lanes(values).reshape(16, 8, 128)
    row = lax.broadcasted_iota(jnp.int32, (1, 8, 128), 1)
    above = pltpu.roll(across, 1, 1)
    below = pltpu.roll(across, 7, 1)
    shared = across + jnp.where(row == 4, above, jnp.where(row == 3, below, 0.0))
    return shared.reshape(128, 128)


def changes(east, north, height, coriolis, mass, inverse, share, along_x_ref, tiles_ref):
    energy = 0.5 * (east * east + north * north) + height
    flux_x, flux_y = height * east, height * north
    first_x = jnp.dot(
        jnp.concatenate([north, energy, flux_x], 0), along_x_ref[0],
        precision=HIGH, preferred_element_type=f32,
    )
    second_x = jnp.dot(
        jnp.concatenate([east, north, height], 0), along_x_ref[1],
        precision=HIGH, preferred_element_type=f32,
    )
    absolute = first_x[:128] - along_rows(east, tiles_ref, 0) + coriolis
    tendencies = (
        absolute * north - first_x[128:256],
        -absolute * east - along_rows(energy, tiles_ref, 0),
        -(first_x[256:] + along_rows(flux_y, tiles_ref, 0)),
    )
    locals_, smoothed = [], []
    for part, values in enumerate((east, north, height)):
        lap = second_x[128 * part : 128 * part + 128] + along_rows(values, tiles_ref, 7)
        local = share(lap * mass)
        locals_.append(local)
        smoothed.append(local * inverse)
    second_x = jnp.dot(
        jnp.concatenate(smoothed, 0), along_x_ref[1], precision=HIGH, preferred_element_type=f32
    )
    changed = []
    for part in range(3):
        lap = second_x[128 * part : 128 * part + 128] + along_rows(smoothed[part], tiles_ref, 7)
        changed.append(share((tendencies[part] - hyper_coef * lap) * mass))
    return locals_, changed


def edge_kernel(
    cols_b, device_ref, owner_ref, velocity_ref, height_ref, coriolis_ref, elem_mass_ref,
    along_x_ref, expand_ref, expand_t_ref, tiles_ref,
    side_ref, upright_ref, mass_ref, table_ref, top_ref,
    smooth, change,
):
    lane = lane_index(128)
    top = jnp.zeros((128, 128), f32)
    for level in range(8):
        east, north = velocity_ref[0, level], velocity_ref[1, level]
        top = jnp.maximum(
            top, jnp.sqrt(east * east + north * north) + jnp.sqrt(height_ref[level])
        )
    top_ref[...] = jnp.broadcast_to(jnp.max(top), top_ref.shape)
    rows = jnp.dot(expand_ref[...], elem_mass_ref[0], precision=HIGH, preferred_element_type=f32)
    mass = jnp.dot(rows, expand_t_ref[...], precision=HIGH, preferred_element_type=f32)
    mass_ref[...] = mass
    find_tables(device_ref[0], owner_ref, table_ref, cols_b)
    mass_t = jnp.transpose(mass)
    coriolis = coriolis_ref[0]

    def upright_band(ref_value):
        return jnp.concatenate([ref_value[120:128], ref_value[0:8]], 0)

    def upright_plane(read):
        return jnp.concatenate(
            [piece for level in range(8) for piece in (read(level, 120), read(level, 0))], 0
        )

    def sideways_plane(read):
        packed = jnp.zeros((128, 128), f32)
        for level in range(8):
            packed = jnp.where(lane // 16 == level, turn(read(level), 8 + 16 * level), packed)
        return jnp.transpose(packed)

    def repeat(band):
        return jnp.concatenate([band] * 8, 0)

    row = lax.broadcasted_iota(jnp.int32, (128, 128), 0) % 16
    inner = (row != 7) & (row != 8) & (lane > 0) & (lane < 127)
    for way in range(2):
        if way == 0:
            planes = [
                upright_plane(lambda level, at, c=c: velocity_ref[c, level, at : at + 8, :])
                for c in range(2)
            ] + [upright_plane(lambda level, at: height_ref[level, at : at + 8, :])]
            turning = repeat(upright_band(coriolis))
            band_mass = repeat(upright_band(mass))
        else:
            planes = [
                sideways_plane(lambda level, c=c: velocity_ref[c, level]) for c in (1, 0)
            ] + [sideways_plane(lambda level: height_ref[level])]
            turning = -sideways_plane(lambda level: coriolis)
            band_mass = repeat(upright_band(mass_t))
        inverse = jnp.where(inner, 1.0 / share_band(band_mass), 0.0)
        locals_, changed = changes(
            *planes, turning, band_mass, inverse, share_band, along_x_ref, tiles_ref
        )
        for part in range(3):
            target = part if way == 0 or part == 2 else 1 - part
            smooth[way, target] = locals_[part]
            change[way, target] = changed[part]

    for way, ref in ((0, upright_ref), (1, side_ref)):
        for end in range(2):
            for part in range(3):
                place = pl.ds(7 + end, 8, stride=16)
                ref[end, 8 * part : 8 * part + 8, :] = smooth.at[way, part][place, :]
                ref[end, 24 + 8 * part : 32 + 8 * part, :] = change.at[way, part][place, :]
    mass_lines = (mass_t[127:128], mass_t[0:1], mass[127:128], mass[0:1])
    lines = (side_ref[0], side_ref[1], upright_ref[0], upright_ref[1])
    ends = {}
    for side in range(4):
        local_mass = share_lanes(mass_lines[side])
        for high in (False, True):
            ends[side, high] = pack_end(lines[side][0:24], high) + pack_mass(local_mass, high)
    extras = (
        ends[UPPER, True] + turn(ends[LOWER, True], 12),
        ends[UPPER, False] + turn(ends[LOWER, False], 12),
        ends[LEFT, True] + turn(ends[RIGHT, True], 12),
        ends[LEFT, False] + turn(ends[RIGHT, False], 12),
    )
    for side in range(4):
        tile = extras[side] + fold_line(mass_lines[side])
        if side < 2:
            side_ref[side, 48:56, :] = tile
        else:
            upright_ref[side - 2, 48:56, :] = tile
    for across, sideways in ((RIGHT, True), (LEFT, False)):
        for number, (along, upward) in enumerate(((UPPER, True), (LOWER, False))):
            tile = ends[along, sideways] + turn(ends[across, upward], 12)
            tile = tile + turn(pack_end(lines[along][24:48], sideways), 48)
            side_ref[across, 56 + 8 * number : 64 + 8 * number, :] = tile


def block_kernel(
    velocity_ref, height_ref, coriolis_ref, mass_in_ref, along_x_ref, tiles_ref, after_ref,
    partial_ref, mass_ref, inner_inverse,
):
    lane = lane_index(128)

    @pl.when(pl.program_id(0) == 0)
    def _():
        local_mass = share_block(mass_in_ref[...])
        mass_ref[...] = local_mass
        row = lax.broadcasted_iota(jnp.int32, (128, 128), 0)
        inner = (row > 0) & (row < 127) & (lane > 0) & (lane < 127)
        inner_inverse[...] = jnp.where(inner, 1.0 / local_mass, 0.0)

    _, changed = changes(
        velocity_ref[0, 0], velocity_ref[1, 0], height_ref[0], coriolis_ref[0], mass_in_ref[...],
        inner_inverse[...], share_block, along_x_ref, tiles_ref,
    )
    for part in range(3):
        partial_ref[part, 0] = changed[part]


def pack_kernel(table_ref, side_ref, upright_ref, ahead_ref, behind_ref, tops_ref, send_ref):
    lane = lane_index(8)
    top = jnp.max(tops_ref[...])
    for place in range(16):
        message = table_ref[place, 0]

        @pl.when(message < 2)
        def _():
            send_ref[2 * place] = side_ref[jnp.minimum(message, 1), 0:56, :]

        @pl.when((message >= 2) & (message < 4))
        def _():
            send_ref[2 * place] = upright_ref[jnp.clip(message - 2, 0, 1)]

        for corner, (side, row) in enumerate(((0, 56), (1, 56), (0, 64), (1, 64))):

            @pl.when(message == 4 + corner)
            def _(side=side, row=row):
                send_ref[2 * place, 48:56, :] = side_ref[side, row : row + 8, :]

        send_ref[2 * place, 48:56, :] = jnp.where(lane >= 96, top, send_ref[2 * place, 48:56, :])
        crossing = table_ref[16 + place, 0]
        for base, ref in ((0, ahead_ref), (3, behind_ref)):

            @pl.when(crossing == base)
            def _(ref=ref):
                send_ref[2 * place + 1] = ref[0:56, :]

            @pl.when(crossing == base + 1)
            def _(ref=ref):
                send_ref[2 * place + 1, 48:56, :] = ref[56:64, :]

            @pl.when(crossing == base + 2)
            def _(ref=ref):
                send_ref[2 * place + 1, 48:56, :] = ref[64:72, :]


def edge_terms(table_ref, side_ref, upright_ref, received_ref, tiles_ref):
    lane = lane_index(1)

    def message(way, start, stop):
        values = received_ref[table_ref[32 + way, 0], start:stop, :]
        return jnp.where(table_ref[40 + way, 0] > 0, values, 0.0)

    own = (
        side_ref[0, 0:24, :], side_ref[1, 0:24, :], upright_ref[0, 0:24, :], upright_ref[1, 0:24, :],
    )
    own_mass = (
        unfold_line(side_ref[0, 48:56, :]), unfold_line(side_ref[1, 48:56, :]),
        unfold_line(upright_ref[0, 48:56, :]), unfold_line(upright_ref[1, 48:56, :]),
    )
    near = [message(side, 0, 24) for side in range(4)]
    change = [message(side, 24, 48) for side in range(4)]
    extra = [message(side, 48, 56) for side in range(4)]
    mass = [unfold_line(extra[side]) for side in range(4)]
    shared_mass = [share_lanes(mass[side]) for side in range(4)]
    total = [own[side] + near[side] for side in range(4)]
    total_mass = [share_lanes(own_mass[side]) + shared_mass[side] for side in range(4)]
    corners = []
    for along in (UPPER, LOWER):
        for across in (RIGHT, LEFT):
            corner = 4 + 2 * (along - UPPER) + across
            at_x = 127 if across == RIGHT else 0
            at_y = 127 if along == UPPER else 0
            tile = message(corner, 48, 56)
            end_x = 0 if across == RIGHT else 3

            def spread_out(packed, start, at_x=at_x):
                return jnp.concatenate(
                    [turn(packed, at_x - start - 4 * part) for part in range(3)], 0
                )

            far = spread_out(tile, end_x)
            far_mass = turn(tile, at_x - 24 - end_x)[0:1]
            corners.append((along, across, at_x, at_y, tile, far_mass, spread_out))
            on_x, on_y = lane == at_x, lane == at_y
            total[along] = total[along] + jnp.where(
                on_x, turn(near[across], at_x - at_y) + far, 0.0
            )
            total_mass[along] = total_mass[along] + jnp.where(
                on_x, turn(mass[across], at_x - at_y) + far_mass, 0.0
            )
            total[across] = total[across] + jnp.where(
                on_y, turn(near[along] + far, at_y - at_x), 0.0
            )
            total_mass[across] = total_mass[across] + jnp.where(
                on_y, turn(mass[along] + far_mass, at_y - at_x), 0.0
            )
    smooth = [total[side] / total_mass[side] for side in range(4)]
    curve = [second_lanes(smooth[side], tiles_ref) for side in range(4)]
    added = [
        change[side]
        - hyper_coef
        * (shared_mass[side] * CENTRE * smooth[side] + share_lanes(mass[side] * curve[side]))
        for side in range(4)
    ]

    def arm(beside, diagonal, coefs):
        both = beside + diagonal
        weight = turn(both, -24)
        value = jnp.where(weight > 0.0, both / jnp.where(weight > 0.0, weight, 1.0), 0.0) * coefs
        value = value + turn(value, -1)
        return value + turn(value, -2)

    for along, across, at_x, at_y, tile, far_mass, spread_out in corners:
        beside = extra[across] if along == UPPER else turn(extra[across], -12)
        arm_x = spread_out(arm(beside, tile, tiles_ref[21 if across == RIGHT else 22]), 0)
        beside = extra[along] if across == LEFT else turn(extra[along], -12)
        arm_y = spread_out(
            arm(beside, turn(tile, -12), tiles_ref[21 if along == UPPER else 22]), 0
        )
        middle = CENTRE * smooth[along]
        arm_x, arm_y = arm_x + middle, arm_y + middle
        own_x = curve[along]
        own_y = turn(curve[across], at_x - at_y)
        mass_x = turn(mass[across], at_x - at_y)
        end_x = 0 if across == RIGHT else 3
        value = (
            turn(change[across], at_x - at_y) + change[along] + spread_out(tile, 48 + end_x)
        ) - hyper_coef * (
            mass_x * (arm_x + own_y) + mass[along] * (own_x + arm_y) + far_mass * (arm_x + arm_y)
        )
        added[along] = jnp.where(lane == at_x, value, added[along])
    ends = (lane == 0) | (lane == 127)
    plain, edge = [], []
    for side in range(4):
        line = smooth[side] if side >= UPPER else jnp.where(ends, 0.0, smooth[side])
        outside = added[side] if side >= UPPER else jnp.where(ends, 0.0, added[side])
        bend = curve[side] if side >= UPPER else second_lanes(line, tiles_ref)
        plain.append(share_lanes(own_mass[side] * line))
        edge.append(outside - hyper_coef * share_lanes(own_mass[side] * bend))
    return plain, edge, total_mass


def last_kernel(
    table_ref, side_ref, upright_ref, received_ref, tiles_ref, mass_ref,
    velocity_ref, height_ref, partial_ref, new_velocity_ref, new_height_ref,
    rows, columns, inverse,
):
    level = pl.program_id(0)
    lane = lane_index(128)

    @pl.when(level == 0)
    def _():
        plain, edge, total_mass = edge_terms(
            table_ref, side_ref, upright_ref, received_ref, tiles_ref
        )
        rows[0] = plain[UPPER]
        rows[1] = plain[LOWER]
        rows[2] = edge[UPPER]
        rows[3] = edge[LOWER]
        stacked = jnp.concatenate(
            [plain[LEFT], plain[RIGHT], edge[LEFT], edge[RIGHT]]
            + [jnp.broadcast_to(total_mass[side], (16, 128)) for side in (LEFT, RIGHT)],
            0,
        )
        columns[...] = jnp.transpose(stacked)
        sides = columns[...]
        mass = mass_ref[...]
        mass = jnp.where(lane == 0, sides[:, 96:97], mass)
        mass = jnp.where(lane == 127, sides[:, 112:113], mass)
        row = lax.broadcasted_iota(jnp.int32, (128, 128), 0)
        mass = jnp.where(row == 127, total_mass[UPPER], mass)
        mass = jnp.where(row == 0, total_mass[LOWER], mass)
        top = jnp.zeros((8, 128), f32)
        for place in range(16):
            top = jnp.maximum(top, received_ref[2 * place, 48:56, :])
        top = jnp.max(jnp.where(lane_index(8) >= 96, top, 0.0))
        inverse[...] = (courant / top) / mass

    moved = pltpu.roll(columns[...], (128 - level) % 128, 1)
    factor = inverse[...]
    left = lane < 64
    across = tiles_ref[25, 0:1]
    ends = tiles_ref[26, 0:1]
    for part in range(3):
        start = 8 * part
        plain = jnp.where(left, moved[:, start : start + 1], moved[:, start + 24 : start + 25])
        edge = jnp.where(left, moved[:, start + 48 : start + 49], moved[:, start + 72 : start + 73])
        value = partial_ref[part, 0] + across * plain + ends * edge
        place = pl.ds(start + level, 1)
        upper = tiles_ref[23] * rows[0, place, :]
        lower = tiles_ref[24] * rows[1, place, :]
        row = lax.broadcasted_iota(jnp.int32, (8, 128), 0)
        upper = upper + jnp.where(row == 7, rows[2, place, :], 0.0)
        lower = lower + jnp.where(row == 0, rows[3, place, :], 0.0)
        value = jnp.concatenate([value[:8] + lower, value[8:120], value[120:] + upper], 0)
        if part < 2:
            new_velocity_ref[part, 0] = velocity_ref[part, 0] + factor * value
        else:
            new_height_ref[0] = height_ref[0] + factor * value


def whole(shape, space=None):
    if space is None:
        return pl.BlockSpec(shape, lambda level: (0,) * len(shape))
    return pl.BlockSpec(memory_space=space)


def per_device(velocity, thickness, coriolis, elem_mass, block_owner):
    cols_b = block_owner.shape[1]
    count = 4 * cols_b
    velocity = velocity[:, :, 0]
    thickness = thickness[:, 0]
    along_x, expand, expand_t, tiles = constant_tables()
    device = (lax.axis_index("elem") * lax.axis_size("sub") + lax.axis_index("sub")).reshape(1)
    if cols_b < 128:
        block_owner = jnp.pad(block_owner, ((0, 0), (0, 128 - cols_b)), constant_values=-1)
    pair = pl.BlockSpec((2, 1, 128, 128), lambda level: (0, level, 0, 0))
    single = pl.BlockSpec((1, 128, 128), lambda level: (level, 0, 0))
    triple = pl.BlockSpec((3, 1, 128, 128), lambda level: (0, level, 0, 0))
    shape = jax.ShapeDtypeStruct
    params = pltpu.CompilerParams(
        dimension_semantics=("arbitrary",), vmem_limit_bytes=BLOCK_VMEM
    )
    vmem = pltpu.VMEM
    side, upright, mass, table, top = pl.pallas_call(
        functools.partial(edge_kernel, cols_b),
        in_specs=[pl.BlockSpec(memory_space=pltpu.SMEM)] + [pl.BlockSpec(memory_space=vmem)] * 9,
        out_specs=[pl.BlockSpec(memory_space=vmem)] * 5,
        out_shape=[
            shape((2, 72, 128), f32), shape((2, 56, 128), f32),
            shape((128, 128), f32), shape((48, 128), jnp.int32), shape((TOP_ROWS, 128), f32),
        ],
        scratch_shapes=[
            pltpu.VMEM((2, 3, 128, 128), f32), pltpu.VMEM((2, 3, 128, 128), f32),
        ],
        compiler_params=pltpu.CompilerParams(vmem_limit_bytes=EDGE_VMEM),
        name="edge",
    )(device, block_owner, velocity, thickness, coriolis, elem_mass, along_x, expand, expand_t, tiles)
    squares = count // 16
    same_place = [[16 * s + i for s in range(squares)] for i in range(16)]
    same_square = [[16 * s + i for i in range(16)] for s in range(squares)]
    tops = lax.all_to_all(
        top[: 8 * squares], axes, 0, 0, axis_index_groups=same_place, tiled=True
    )
    ahead = lax.ppermute(side[1], axes, [(b, (b - 16) % count) for b in range(count)])
    behind = lax.ppermute(side[0], axes, [(b, (b + 16) % count) for b in range(count)])
    send = pl.pallas_call(
        pack_kernel,
        in_specs=[whole((48, 128), pltpu.SMEM)] + [pl.BlockSpec(memory_space=pltpu.VMEM)] * 5,
        out_specs=pl.BlockSpec(memory_space=pltpu.VMEM),
        out_shape=shape((32, 56, 128), f32),
        compiler_params=pltpu.CompilerParams(vmem_limit_bytes=PACK_VMEM),
        name="pack",
    )(table, side, upright, ahead, behind, tops)
    received = lax.all_to_all(
        send.reshape(16, 112, 128), axes, 0, 0, axis_index_groups=same_square, tiled=True
    ).reshape(32, 56, 128)
    partial, local_mass = pl.pallas_call(
        block_kernel,
        grid=(8,),
        in_specs=[
            pair, single, whole((1, 128, 128)), whole((128, 128)), whole((2, 128, 128)),
            whole((27, 8, 128)), whole((1, 8, 128)),
        ],
        out_specs=[triple, whole((128, 128))],
        out_shape=[shape((3, 8, 128, 128), f32), shape((128, 128), f32)],
        scratch_shapes=[pltpu.VMEM((128, 128), f32)],
        compiler_params=params,
        cost_estimate=pl.CostEstimate(
            flops=2_000_000_000, bytes_accessed=3_200_000, transcendentals=0
        ),
        name="block",
    )(velocity, thickness, coriolis, mass, along_x, tiles, send)
    new_velocity, new_thickness = pl.pallas_call(
        last_kernel,
        grid=(8,),
        in_specs=[
            whole((48, 128), pltpu.SMEM), whole((2, 72, 128)), whole((2, 56, 128)),
            whole((32, 56, 128)), whole((27, 8, 128)), whole((128, 128)), pair, single, triple,
        ],
        out_specs=[pair, single],
        out_shape=[shape((2, 8, 128, 128), f32), shape((8, 128, 128), f32)],
        scratch_shapes=[
            pltpu.VMEM((4, 24, 128), f32), pltpu.VMEM((128, 128), f32), pltpu.VMEM((128, 128), f32),
        ],
        compiler_params=pltpu.CompilerParams(
            dimension_semantics=("arbitrary",), vmem_limit_bytes=LAST_VMEM
        ),
        name="last",
    )(table, side, upright, received, tiles, local_mass, velocity, thickness, partial)
    return new_velocity[:, :, None], new_thickness[:, None]


def solution(mesh):
    return jax.shard_map(
        per_device,
        mesh=mesh,
        in_specs=(
            P(None, None, axes, None, None),
            P(None, axes, None, None),
            P(axes, None, None),
            P(axes, None, None),
            P(),
        ),
        out_specs=(
            P(None, None, axes, None, None),
            P(None, axes, None, None),
        ),
        check_vma=False,
    )
```

```python
import functools
import math

import jax
import jax.numpy as jnp
import numpy as np
from jax import lax
from jax.experimental import pallas as pl
from jax.experimental.pallas import tpu as pltpu
from jax.sharding import PartitionSpec as P

courant = 0.1
hyper_coef = 0.002
TOP_ROWS = 256
MIB = 1024 * 1024
EDGE_VMEM = 60 * MIB
PACK_VMEM = 53 * MIB
BLOCK_VMEM = 60 * MIB
LAST_VMEM = 52 * MIB
GROUPS = 4
LEVELS_EACH = 8 // GROUPS
axes = ("elem", "sub")
f32 = jnp.float32
HIGH = lax.Precision.HIGHEST
RIGHT, LEFT, UPPER, LOWER = range(4)
steps8 = ((0, 1), (0, -1), (1, 0), (-1, 0), (1, 1), (1, -1), (-1, 1), (-1, -1))


def gll_tables():
    points = [-1.0, -1.0 / math.sqrt(5.0), 1.0 / math.sqrt(5.0), 1.0]
    weights = np.array([1.0 / 6.0, 5.0 / 6.0, 5.0 / 6.0, 1.0 / 6.0])
    spread = [
        math.prod([points[target] - points[others] for others in range(4) if others != target])
        for target in range(4)
    ]
    derivative = np.zeros((4, 4))
    for target in range(4):
        for source in range(4):
            if target == source:
                derivative[target, source] = sum(
                    1.0 / (points[target] - points[others]) for others in range(4) if others != target
                )
            else:
                derivative[target, source] = spread[target] / (
                    spread[source] * (points[target] - points[source])
                )
    return weights, 2.0 * derivative


WEIGHTS, FIRST = gll_tables()
SECOND = FIRST @ FIRST
CENTRE = float(SECOND[0, 0])


def offset_rows(table):
    rows = np.zeros((7, 4))
    for shift in range(-3, 4):
        for target in range(4):
            if 0 <= target + shift < 4:
                rows[shift + 3, target] = table[target, target + shift]
    return rows


def constant_tables():
    along_x = np.stack([np.kron(np.eye(32), FIRST.T), np.kron(np.eye(32), SECOND.T)])
    expand = np.kron(np.eye(32), WEIGHTS[:, None])
    tiles = np.zeros((27, 8, 128))
    for base, table in ((0, FIRST), (7, SECOND)):
        tiles[base : base + 7] = np.tile(offset_rows(table), (1, 2))[:, :, None]
    tiles[14:21] = np.tile(offset_rows(SECOND), (1, 32))[:, None, :]
    arm_low = np.array([0.0, SECOND[0, 1], SECOND[0, 2], SECOND[0, 3]])
    arm_high = np.array([SECOND[3, 0], SECOND[3, 1], SECOND[3, 2], 0.0])
    tiles[21] = np.tile(arm_low, 32)[None]
    tiles[22] = np.tile(arm_high, 32)[None]
    high = np.array([-hyper_coef * WEIGHTS[a] / WEIGHTS[3] * SECOND[a, 3] for a in range(4)])
    low = np.array([-hyper_coef * WEIGHTS[a] / WEIGHTS[0] * SECOND[a, 0] for a in range(4)])
    tiles[23] = np.concatenate([[0.0, 0.0, 0.0, high[0]], high])[:, None]
    tiles[24] = np.concatenate([low, [low[3], 0.0, 0.0, 0.0]])[:, None]
    across = np.zeros(128)
    across[:5] = [*low, low[3]]
    across[123:] = [high[0], *high]
    tiles[25] = across[None]
    ends = np.zeros(128)
    ends[0] = ends[127] = 1.0
    tiles[26] = ends[None]
    return (
        jnp.asarray(along_x, f32),
        jnp.asarray(expand, f32),
        jnp.asarray(expand.T, f32),
        jnp.asarray(tiles, f32),
    )


def lane_index(rows):
    return lax.broadcasted_iota(jnp.int32, (rows, 128), 1)


def turn(values, steps, axis=1):
    steps = steps % values.shape[axis]
    return values if steps == 0 else pltpu.roll(values, steps, axis)


def share_lanes(values):
    lane = lane_index(values.shape[0])
    first = (lane % 4 == 0) & (lane > 0)
    last = (lane % 4 == 3) & (lane < 127)
    return values + jnp.where(first, turn(values, 1), jnp.where(last, turn(values, 127), 0.0))


def share_rows(values):
    row = lax.broadcasted_iota(jnp.int32, values.shape, 0)
    first = (row % 4 == 0) & (row > 0)
    last = (row % 4 == 3) & (row < 127)
    return values + jnp.where(
        first, turn(values, 1, 0), jnp.where(last, turn(values, 127, 0), 0.0)
    )


def share_block(values):
    return share_rows(share_lanes(values))


def along_rows(values, tiles_ref, base):
    grouped = values.reshape(16, 8, 128)
    total = grouped * tiles_ref[base + 3][None]
    for shift in (-3, -2, -1, 1, 2, 3):
        total = total + pltpu.roll(grouped, (-shift) % 8, 1) * tiles_ref[base + 3 + shift][None]
    return total.reshape(128, 128)


def second_lanes(values, tiles_ref):
    total = values * tiles_ref[17, 0:1]
    for shift in (-3, -2, -1, 1, 2, 3):
        total = total + turn(values, -shift) * tiles_ref[17 + shift, 0:1]
    return total


def pack_end(lines, at_high):
    lane = lane_index(8)
    start = 124 if at_high else 0
    packed = jnp.zeros((8, 128), f32)
    for part in range(3):
        moved = turn(lines[8 * part : 8 * part + 8], 4 * part - start)
        packed = jnp.where(lane // 4 == part, moved, packed)
    return packed


def pack_mass(line, at_high):
    lane = lane_index(8)
    start = 124 if at_high else 0
    wide = jnp.broadcast_to(line, (8, 128))
    packed = jnp.zeros((8, 128), f32)
    for part in range(3):
        packed = jnp.where(lane // 4 == 6 + part, turn(wide, 24 + 4 * part - start), packed)
    return packed


def fold_line(line):
    lane = lane_index(8)
    row = lax.broadcasted_iota(jnp.int32, (8, 128), 0)
    wide = jnp.broadcast_to(line, (8, 128))
    folded = jnp.zeros((8, 128), f32)
    for part in range(4):
        folded = jnp.where((row == part) & (lane // 32 == 2), turn(wide, 64 - 32 * part), folded)
    return folded


def unfold_line(tile):
    lane = lane_index(1)
    line = jnp.zeros((1, 128), f32)
    for part in range(4):
        line = jnp.where(lane // 32 == part, turn(tile[part : part + 1], 32 * part - 64), line)
    return line


def find_tables(device, owner_ref, table_ref, cols_b):
    square = device // 16
    squares = cols_b // 4
    place = jnp.zeros((48, 128), f32)
    index = lax.broadcasted_iota(jnp.int32, (48, 1), 0)
    wanted = ((square + index // 16 + squares - 1) % squares) * 16 + index % 16
    lane = lane_index(1)
    own = jnp.zeros((1, 128), f32)
    for row in range(4):
        line = owner_ref[row : row + 1, :]
        code = (128 * row + lane).astype(f32)
        place = place + jnp.where(line == wanted, code, 0.0)
        own = own + jnp.where(line == device, code, 0.0)
    place = jnp.sum(place, axis=1, keepdims=True).astype(jnp.int32)
    own = jnp.sum(own, axis=1, keepdims=True).astype(jnp.int32)
    own_row, own_col = own // 128, own % 128
    rows, cols = place // 128, place % 128
    member = device % 16
    here_rows, here_cols = rows[16:32], cols[16:32]
    down, over = here_rows - own_row, here_cols - own_col
    inside = jnp.full((16, 1), 8, jnp.int32)
    for number, (step_y, step_x) in enumerate(steps8):
        inside = jnp.where((down == step_y) & (over == step_x), number, inside)
    crossing = jnp.full((16, 1), 6, jnp.int32)
    sixteen = lax.broadcasted_iota(jnp.int32, (16, 1), 0)
    for side, start, step_x in ((0, 32, 1), (1, 0, -1)):
        picked = sixteen == member
        their = jnp.sum(
            jnp.where(picked, place[start : start + 16], 0).astype(f32), axis=0, keepdims=True
        ).astype(jnp.int32)
        their_row, their_col = their // 128, their % 128
        beside = their_col == (here_cols + step_x + cols_b) % cols_b
        for number, step_y in enumerate((0, 1, -1)):
            crossing = jnp.where(
                beside & (here_rows - their_row == step_y), 3 * side + number, crossing
            )
    way = lax.broadcasted_iota(jnp.int32, (8, 1), 0)
    step_y = jnp.zeros((8, 1), jnp.int32)
    step_x = jnp.zeros((8, 1), jnp.int32)
    for number, (along_y, along_x) in enumerate(steps8):
        step_y = jnp.where(way == number, along_y, step_y)
        step_x = jnp.where(way == number, along_x, step_x)
    near_row = own_row + step_y
    near_col = (own_col + step_x + cols_b) % cols_b
    found = jnp.zeros((8, 128), f32)
    for row in range(4):
        line = owner_ref[row : row + 1, :].astype(f32)
        found = found + jnp.where((near_row == row) & (near_col == lane), line, 0.0)
    found = jnp.sum(found, axis=1, keepdims=True).astype(jnp.int32)
    there = (near_row >= 0) & (near_row < 4)
    slot = 2 * (found % 16) + jnp.where(found // 16 == square, 0, 1)
    column = jnp.concatenate([inside, crossing, slot, there.astype(jnp.int32)], 0).astype(f32)
    picked = lax.broadcasted_iota(jnp.int32, (48, 128), 0) == lane_index(48)
    table_ref[...] = jnp.sum(jnp.where(picked, column, 0.0), axis=0, keepdims=True).astype(
        jnp.int32
    )


def share_band(values):
    across = share_lanes(values).reshape(16, 8, 128)
    row = lax.broadcasted_iota(jnp.int32, (1, 8, 128), 1)
    above = pltpu.roll(across, 1, 1)
    below = pltpu.roll(across, 7, 1)
    shared = across + jnp.where(row == 4, above, jnp.where(row == 3, below, 0.0))
    return shared.reshape(128, 128)


def changes(east, north, height, coriolis, mass, inverse, share, along_x_ref, tiles_ref):
    energy = 0.5 * (east * east + north * north) + height
    flux_x, flux_y = height * east, height * north
    first_x = jnp.dot(
        jnp.concatenate([north, energy, flux_x], 0), along_x_ref[0],
        precision=HIGH, preferred_element_type=f32,
    )
    second_x = jnp.dot(
        jnp.concatenate([east, north, height], 0), along_x_ref[1],
        precision=HIGH, preferred_element_type=f32,
    )
    absolute = first_x[:128] - along_rows(east, tiles_ref, 0) + coriolis
    tendencies = (
        absolute * north - first_x[128:256],
        -absolute * east - along_rows(energy, tiles_ref, 0),
        -(first_x[256:] + along_rows(flux_y, tiles_ref, 0)),
    )
    locals_, smoothed = [], []
    for part, values in enumerate((east, north, height)):
        lap = second_x[128 * part : 128 * part + 128] + along_rows(values, tiles_ref, 7)
        local = share(lap * mass)
        locals_.append(local)
        smoothed.append(local * inverse)
    second_x = jnp.dot(
        jnp.concatenate(smoothed, 0), along_x_ref[1], precision=HIGH, preferred_element_type=f32
    )
    changed = []
    for part in range(3):
        lap = second_x[128 * part : 128 * part + 128] + along_rows(smoothed[part], tiles_ref, 7)
        changed.append(share((tendencies[part] - hyper_coef * lap) * mass))
    return locals_, changed


def edge_kernel(
    cols_b, device_ref, owner_far, velocity_far, height_far, coriolis_far, elem_mass_far,
    along_x_far, expand_far, expand_t_far, tiles_far,
    right_ref, left_ref, message_ref, mass_ref, table_ref, top_ref,
    smooth, change, owner_ref, velocity_ref, height_ref, coriolis_ref, elem_mass_ref,
    along_x_ref, expand_ref, expand_t_ref, tiles_ref, arrived,
):
    far = (
        expand_far, elem_mass_far, expand_t_far, owner_far, height_far, velocity_far,
        coriolis_far, tiles_far, along_x_far,
    )
    near = (
        expand_ref, elem_mass_ref, expand_t_ref, owner_ref, height_ref, velocity_ref,
        coriolis_ref, tiles_ref, along_x_ref,
    )
    copies = [
        pltpu.make_async_copy(far[k], near[k], arrived.at[k]) for k in range(len(far))
    ]
    for copy in copies:
        copy.start()
    for copy in copies:
        copy.wait()
    lane = lane_index(128)
    top = jnp.zeros((128, 128), f32)
    for level in range(8):
        east, north = velocity_ref[0, level], velocity_ref[1, level]
        top = jnp.maximum(
            top, jnp.sqrt(east * east + north * north) + jnp.sqrt(height_ref[level])
        )
    top_ref[...] = jnp.broadcast_to(jnp.max(top), top_ref.shape)
    rows = jnp.dot(expand_ref[...], elem_mass_ref[0], precision=HIGH, preferred_element_type=f32)
    mass = jnp.dot(rows, expand_t_ref[...], precision=HIGH, preferred_element_type=f32)
    mass_ref[...] = mass
    find_tables(device_ref[0], owner_ref, table_ref, cols_b)
    mass_t = jnp.transpose(mass)
    coriolis = coriolis_ref[0]

    def upright_band(ref_value):
        return jnp.concatenate([ref_value[120:128], ref_value[0:8]], 0)

    def upright_plane(read):
        return jnp.concatenate(
            [piece for level in range(8) for piece in (read(level, 120), read(level, 0))], 0
        )

    def sideways_plane(read):
        packed = jnp.zeros((128, 128), f32)
        for level in range(8):
            packed = jnp.where(lane // 16 == level, turn(read(level), 8 + 16 * level), packed)
        return jnp.transpose(packed)

    def repeat(band):
        return jnp.concatenate([band] * 8, 0)

    row = lax.broadcasted_iota(jnp.int32, (128, 128), 0) % 16
    inner = (row != 7) & (row != 8) & (lane > 0) & (lane < 127)
    for way in range(2):
        if way == 0:
            planes = [
                upright_plane(lambda level, at, c=c: velocity_ref[c, level, at : at + 8, :])
                for c in range(2)
            ] + [upright_plane(lambda level, at: height_ref[level, at : at + 8, :])]
            turning = repeat(upright_band(coriolis))
            band_mass = repeat(upright_band(mass))
        else:
            planes = [
                sideways_plane(lambda level, c=c: velocity_ref[c, level]) for c in (1, 0)
            ] + [sideways_plane(lambda level: height_ref[level])]
            turning = -sideways_plane(lambda level: coriolis)
            band_mass = repeat(upright_band(mass_t))
        inverse = jnp.where(inner, 1.0 / share_band(band_mass), 0.0)
        locals_, changed = changes(
            *planes, turning, band_mass, inverse, share_band, along_x_ref, tiles_ref
        )
        for part in range(3):
            target = part if way == 0 or part == 2 else 1 - part
            smooth[way, target] = locals_[part]
            change[way, target] = changed[part]

    for way in range(2):
        for end in range(2):
            side = 2 * (1 - way) + end
            for part in range(3):
                place = pl.ds(7 + end, 8, stride=16)
                message_ref[side, 8 * part : 8 * part + 8, :] = smooth.at[way, part][place, :]
                message_ref[side, 24 + 8 * part : 32 + 8 * part, :] = change.at[way, part][place, :]
    right_ref[0:48, :] = message_ref[RIGHT, 0:48, :]
    left_ref[0:48, :] = message_ref[LEFT, 0:48, :]
    mass_lines = (mass_t[127:128], mass_t[0:1], mass[127:128], mass[0:1])
    lines = [message_ref[side, 0:48, :] for side in range(4)]
    ends = {}
    for side in range(4):
        local_mass = share_lanes(mass_lines[side])
        for high in (False, True):
            ends[side, high] = pack_end(lines[side][0:24], high) + pack_mass(local_mass, high)
    extras = (
        ends[UPPER, True] + turn(ends[LOWER, True], 12),
        ends[UPPER, False] + turn(ends[LOWER, False], 12),
        ends[LEFT, True] + turn(ends[RIGHT, True], 12),
        ends[LEFT, False] + turn(ends[RIGHT, False], 12),
    )
    for side in range(4):
        tile = extras[side] + fold_line(mass_lines[side])
        message_ref[side, 48:56, :] = tile
        if side == RIGHT:
            right_ref[48:56, :] = tile
        elif side == LEFT:
            left_ref[48:56, :] = tile
    for number, (along, upward) in enumerate(((UPPER, True), (LOWER, False))):
        for across, sideways, ref in ((RIGHT, True, right_ref), (LEFT, False, left_ref)):
            tile = ends[along, sideways] + turn(ends[across, upward], 12)
            tile = tile + turn(pack_end(lines[along][24:48], sideways), 48)
            message_ref[4 + 2 * number + across, 48:56, :] = tile
            ref[56 + 8 * number : 64 + 8 * number, :] = tile


def block_kernel(
    velocity_ref, height_ref, coriolis_ref, mass_in_ref, along_x_ref, tiles_ref, after_ref,
    partial_ref, inner_inverse,
):
    lane = lane_index(128)
    step = pl.program_id(0)

    @pl.when(step == 0)
    def _():
        local_mass = share_block(mass_in_ref[...])
        row = lax.broadcasted_iota(jnp.int32, (128, 128), 0)
        inner = (row > 0) & (row < 127) & (lane > 0) & (lane < 127)
        inner_inverse[...] = jnp.where(inner, 1.0 / local_mass, 0.0)

    @pl.when(step < 8)
    def _():
        _, changed = changes(
            velocity_ref[0, 0], velocity_ref[1, 0], height_ref[0], coriolis_ref[0],
            mass_in_ref[...], inner_inverse[...], share_block, along_x_ref, tiles_ref,
        )
        for part in range(3):
            partial_ref[part] = changed[part]

    @pl.when(step == 8)
    def _():
        partial_ref[0] = share_block(mass_in_ref[...])


def pack_kernel(table_ref, message_ref, ahead_ref, behind_ref, tops_ref, send_ref):
    lane = lane_index(8)
    top = jnp.max(tops_ref[...], axis=(0, 1), keepdims=True)[0]
    for place in range(16):
        message = table_ref[0, place]
        crossing = table_ref[0, 16 + place]

        @pl.when(message < 4)
        def _(place=place, message=message):
            send_ref[2 * place, 0:48, :] = message_ref[message, 0:48, :]

        tile = message_ref[jnp.minimum(message, 7), 48:56, :]
        send_ref[2 * place, 48:56, :] = jnp.where(lane >= 96, top, tile)
        for base, ref in ((0, ahead_ref), (3, behind_ref)):

            @pl.when((crossing >= base) & (crossing < base + 3))
            def _(place=place, base=base, ref=ref, crossing=crossing):
                start = pl.multiple_of(8 * (crossing - base), 8)
                send_ref[2 * place + 1] = ref[pl.ds(start, 56), :]


def edge_terms(table_ref, message_ref, received_ref, tiles_ref):
    lane = lane_index(1)

    def message(way, start, stop):
        values = received_ref[table_ref[0, 32 + way], start:stop, :]
        return jnp.where(table_ref[0, 40 + way] > 0, values, 0.0)

    own = [message_ref[side, 0:24, :] for side in range(4)]
    own_mass = [unfold_line(message_ref[side, 48:56, :]) for side in range(4)]
    near = [message(side, 0, 24) for side in range(4)]
    change = [message(side, 24, 48) for side in range(4)]
    extra = [message(side, 48, 56) for side in range(4)]
    mass = [unfold_line(extra[side]) for side in range(4)]
    shared_mass = [share_lanes(mass[side]) for side in range(4)]
    total = [own[side] + near[side] for side in range(4)]
    total_mass = [share_lanes(own_mass[side]) + shared_mass[side] for side in range(4)]
    corners = []
    for along in (UPPER, LOWER):
        for across in (RIGHT, LEFT):
            corner = 4 + 2 * (along - UPPER) + across
            at_x = 127 if across == RIGHT else 0
            at_y = 127 if along == UPPER else 0
            tile = message(corner, 48, 56)
            end_x = 0 if across == RIGHT else 3

            def spread_out(packed, start, at_x=at_x):
                return jnp.concatenate(
                    [turn(packed, at_x - start - 4 * part) for part in range(3)], 0
                )

            far = spread_out(tile, end_x)
            far_mass = turn(tile, at_x - 24 - end_x)[0:1]
            corners.append((along, across, at_x, at_y, tile, far_mass, spread_out))
            on_x, on_y = lane == at_x, lane == at_y
            total[along] = total[along] + jnp.where(
                on_x, turn(near[across], at_x - at_y) + far, 0.0
            )
            total_mass[along] = total_mass[along] + jnp.where(
                on_x, turn(mass[across], at_x - at_y) + far_mass, 0.0
            )
            total[across] = total[across] + jnp.where(
                on_y, turn(near[along] + far, at_y - at_x), 0.0
            )
            total_mass[across] = total_mass[across] + jnp.where(
                on_y, turn(mass[along] + far_mass, at_y - at_x), 0.0
            )
    smooth = [total[side] / total_mass[side] for side in range(4)]
    curve = [second_lanes(smooth[side], tiles_ref) for side in range(4)]
    added = [
        change[side]
        - hyper_coef
        * (shared_mass[side] * CENTRE * smooth[side] + share_lanes(mass[side] * curve[side]))
        for side in range(4)
    ]

    def arm(beside, diagonal, coefs):
        both = beside + diagonal
        weight = turn(both, -24)
        value = jnp.where(weight > 0.0, both / jnp.where(weight > 0.0, weight, 1.0), 0.0) * coefs
        value = value + turn(value, -1)
        return value + turn(value, -2)

    for along, across, at_x, at_y, tile, far_mass, spread_out in corners:
        beside = extra[across] if along == UPPER else turn(extra[across], -12)
        arm_x = spread_out(arm(beside, tile, tiles_ref[21 if across == RIGHT else 22]), 0)
        beside = extra[along] if across == LEFT else turn(extra[along], -12)
        arm_y = spread_out(
            arm(beside, turn(tile, -12), tiles_ref[21 if along == UPPER else 22]), 0
        )
        middle = CENTRE * smooth[along]
        arm_x, arm_y = arm_x + middle, arm_y + middle
        own_x = curve[along]
        own_y = turn(curve[across], at_x - at_y)
        mass_x = turn(mass[across], at_x - at_y)
        end_x = 0 if across == RIGHT else 3
        value = (
            turn(change[across], at_x - at_y) + change[along] + spread_out(tile, 48 + end_x)
        ) - hyper_coef * (
            mass_x * (arm_x + own_y) + mass[along] * (own_x + arm_y) + far_mass * (arm_x + arm_y)
        )
        added[along] = jnp.where(lane == at_x, value, added[along])
    ends = (lane == 0) | (lane == 127)
    plain, edge = [], []
    for side in range(4):
        line = smooth[side] if side >= UPPER else jnp.where(ends, 0.0, smooth[side])
        outside = added[side] if side >= UPPER else jnp.where(ends, 0.0, added[side])
        bend = curve[side] if side >= UPPER else second_lanes(line, tiles_ref)
        plain.append(share_lanes(own_mass[side] * line))
        edge.append(outside - hyper_coef * share_lanes(own_mass[side] * bend))
    return plain, edge, total_mass


def last_kernel(
    table_ref, message_ref, received_ref, tiles_ref,
    velocity_far, height_far, partial_far, new_velocity_far, new_height_far,
    rows, velocity_ref, height_ref, partial_ref, arrived, left_off,
):
    lane = lane_index(128)
    mass_in = pltpu.make_async_copy(partial_far.at[24], partial_ref.at[24], arrived.at[3, 0])
    mass_in.start()
    incoming = []
    for group in range(GROUPS):
        part = pl.ds(LEVELS_EACH * group, LEVELS_EACH)
        incoming.append(
            (
                pltpu.make_async_copy(
                    partial_far.at[pl.ds(3 * LEVELS_EACH * group, 3 * LEVELS_EACH)],
                    partial_ref.at[pl.ds(3 * LEVELS_EACH * group, 3 * LEVELS_EACH)],
                    arrived.at[0, group],
                ),
                pltpu.make_async_copy(
                    velocity_far.at[:, part], velocity_ref.at[:, part], arrived.at[1, group]
                ),
                pltpu.make_async_copy(
                    height_far.at[part], height_ref.at[part], arrived.at[2, group]
                ),
            )
        )
        for copy in incoming[-1]:
            copy.start()

    plain, edge, total_mass = edge_terms(table_ref, message_ref, received_ref, tiles_ref)
    rows[0] = plain[UPPER]
    rows[1] = plain[LOWER]
    rows[2] = edge[UPPER]
    rows[3] = edge[LOWER]
    stacked = jnp.concatenate(
        [plain[LEFT], plain[RIGHT], edge[LEFT], edge[RIGHT]]
        + [jnp.broadcast_to(total_mass[side], (16, 128)) for side in (LEFT, RIGHT)],
        0,
    )
    columns = jnp.transpose(stacked)
    mass_in.wait()
    mass = partial_ref[24]
    mass = jnp.where(lane == 0, columns[:, 96:97], mass)
    mass = jnp.where(lane == 127, columns[:, 112:113], mass)
    row = lax.broadcasted_iota(jnp.int32, (128, 128), 0)
    mass = jnp.where(row == 127, total_mass[UPPER], mass)
    mass = jnp.where(row == 0, total_mass[LOWER], mass)
    top = jnp.zeros((8, 128), f32)
    for place in range(16):
        top = jnp.maximum(top, received_ref[2 * place, 48:56, :])
    top = jnp.max(
        jnp.where(lane_index(8) >= 96, top, 0.0), axis=(0, 1), keepdims=True
    )
    factor = (courant / top) / mass
    left = lane < 64
    across = tiles_ref[25, 0:1]
    ends = tiles_ref[26, 0:1]
    row = lax.broadcasted_iota(jnp.int32, (8, 128), 0)
    outgoing = []
    for group in range(GROUPS):
        for copy in incoming[group]:
            copy.wait()
        for level in range(LEVELS_EACH * group, LEVELS_EACH * (group + 1)):
            for part in range(3):
                at = 8 * part + level
                plain = jnp.where(left, columns[:, at : at + 1], columns[:, at + 24 : at + 25])
                edge = jnp.where(
                    left, columns[:, at + 48 : at + 49], columns[:, at + 72 : at + 73]
                )
                value = partial_ref[3 * level + part] + across * plain + ends * edge
                upper = tiles_ref[23] * rows[0, at : at + 1, :]
                lower = tiles_ref[24] * rows[1, at : at + 1, :]
                upper = upper + jnp.where(row == 7, rows[2, at : at + 1, :], 0.0)
                lower = lower + jnp.where(row == 0, rows[3, at : at + 1, :], 0.0)
                value = jnp.concatenate([value[:8] + lower, value[8:120], value[120:] + upper], 0)
                if part < 2:
                    velocity_ref[part, level] = velocity_ref[part, level] + factor * value
                else:
                    height_ref[level] = height_ref[level] + factor * value
        part = pl.ds(LEVELS_EACH * group, LEVELS_EACH)
        for copy in (
            pltpu.make_async_copy(
                velocity_ref.at[:, part], new_velocity_far.at[:, part], left_off.at[0, group]
            ),
            pltpu.make_async_copy(
                height_ref.at[part], new_height_far.at[part], left_off.at[1, group]
            ),
        ):
            copy.start()
            outgoing.append(copy)
    for copy in outgoing:
        copy.wait()


def whole(shape, space=None):
    if space is None:
        return pl.BlockSpec(shape, lambda level: (0,) * len(shape))
    return pl.BlockSpec(memory_space=space)


def per_device(velocity, thickness, coriolis, elem_mass, block_owner):
    cols_b = block_owner.shape[1]
    count = 4 * cols_b
    velocity = velocity[:, :, 0]
    thickness = thickness[:, 0]
    along_x, expand, expand_t, tiles = constant_tables()
    device = (lax.axis_index("elem") * lax.axis_size("sub") + lax.axis_index("sub")).reshape(1)
    if cols_b < 128:
        block_owner = jnp.pad(block_owner, ((0, 0), (0, 128 - cols_b)), constant_values=-1)
    shape = jax.ShapeDtypeStruct
    params = pltpu.CompilerParams(
        dimension_semantics=("arbitrary",), vmem_limit_bytes=BLOCK_VMEM
    )
    vmem = pltpu.VMEM
    far = pl.BlockSpec(memory_space=pltpu.HBM)
    held = pl.BlockSpec(memory_space=vmem)
    small = pl.BlockSpec(memory_space=pltpu.SMEM)
    arrays = (
        block_owner, velocity, thickness, coriolis, elem_mass, along_x, expand, expand_t, tiles,
    )
    right, left, message, mass, table, top = pl.pallas_call(
        functools.partial(edge_kernel, cols_b),
        in_specs=[small] + [far] * 9,
        out_specs=[held] * 6,
        out_shape=[
            shape((72, 128), f32), shape((72, 128), f32), shape((8, 56, 128), f32),
            shape((128, 128), f32), shape((1, 128), jnp.int32), shape((TOP_ROWS, 128), f32),
        ],
        scratch_shapes=[
            pltpu.VMEM((2, 3, 128, 128), f32), pltpu.VMEM((2, 3, 128, 128), f32),
        ]
        + [pltpu.VMEM(array.shape, array.dtype) for array in arrays]
        + [pltpu.SemaphoreType.DMA((9,))],
        compiler_params=pltpu.CompilerParams(vmem_limit_bytes=EDGE_VMEM),
        name="edge",
    )(device, *arrays)
    squares = count // 16
    same_place = [[16 * s + i for s in range(squares)] for i in range(16)]
    same_square = [[16 * s + i for i in range(16)] for s in range(squares)]
    tops = lax.all_to_all(
        top[: 8 * squares], axes, 0, 0, axis_index_groups=same_place, tiled=True
    )
    ahead = lax.ppermute(left, axes, [(b, (b - 16) % count) for b in range(count)])
    behind = lax.ppermute(right, axes, [(b, (b + 16) % count) for b in range(count)])
    send = pl.pallas_call(
        pack_kernel,
        in_specs=[small] + [held] * 4,
        out_specs=held,
        out_shape=shape((32, 56, 128), f32),
        compiler_params=pltpu.CompilerParams(vmem_limit_bytes=PACK_VMEM),
        name="pack",
    )(table, message, ahead, behind, tops)
    received = lax.all_to_all(
        send.reshape(16, 112, 128), axes, 0, 0, axis_index_groups=same_square, tiled=True
    ).reshape(32, 56, 128)
    pair = pl.BlockSpec((2, 1, 128, 128), lambda step: (0, jnp.minimum(step, 7), 0, 0))
    single = pl.BlockSpec((1, 128, 128), lambda step: (jnp.minimum(step, 7), 0, 0))
    partial = pl.pallas_call(
        block_kernel,
        grid=(9,),
        in_specs=[
            pair, single, whole((1, 128, 128)), whole((128, 128)), whole((2, 128, 128)),
            whole((27, 8, 128)), whole((1, 8, 128)),
        ],
        out_specs=pl.BlockSpec((3, 128, 128), lambda step: (step, 0, 0)),
        out_shape=shape((27, 128, 128), f32),
        scratch_shapes=[pltpu.VMEM((128, 128), f32)],
        compiler_params=params,
        cost_estimate=pl.CostEstimate(
            flops=2_000_000_000, bytes_accessed=3_200_000, transcendentals=0
        ),
        name="block",
    )(velocity, thickness, coriolis, mass, along_x, tiles, send)
    new_velocity, new_thickness = pl.pallas_call(
        last_kernel,
        in_specs=[small] + [held] * 3 + [far] * 3,
        out_specs=[far] * 2,
        out_shape=[shape((2, 8, 128, 128), f32), shape((8, 128, 128), f32)],
        scratch_shapes=[
            pltpu.VMEM((4, 24, 128), f32), pltpu.VMEM((2, 8, 128, 128), f32),
            pltpu.VMEM((8, 128, 128), f32), pltpu.VMEM((25, 128, 128), f32),
            pltpu.SemaphoreType.DMA((4, GROUPS)), pltpu.SemaphoreType.DMA((2, GROUPS)),
        ],
        compiler_params=pltpu.CompilerParams(vmem_limit_bytes=LAST_VMEM),
        name="last",
    )(table, message, received, tiles, velocity, thickness, partial)
    return new_velocity[:, :, None], new_thickness[:, None]


def solution(mesh):
    return jax.shard_map(
        per_device,
        mesh=mesh,
        in_specs=(
            P(None, None, axes, None, None),
            P(None, axes, None, None),
            P(axes, None, None),
            P(axes, None, None),
            P(),
        ),
        out_specs=(
            P(None, None, axes, None, None),
            P(None, axes, None, None),
        ),
        check_vma=False,
    )
```

```python
import functools
import math

import jax
import jax.numpy as jnp
import numpy as np
from jax import lax
from jax.experimental import pallas as pl
from jax.experimental.pallas import tpu as pltpu
from jax.sharding import PartitionSpec as P

courant = 0.1
hyper_coef = 0.002
TOP_ROWS = 256
MIB = 1024 * 1024
EDGE_VMEM = 60 * MIB
PACK_VMEM = 53 * MIB
FILL_VMEM = 53 * MIB
BLOCK_VMEM = 60 * MIB
LAST_VMEM = 52 * MIB
GROUPS = 2
LEVELS_EACH = 8 // GROUPS
axes = ("elem", "sub")
f32 = jnp.float32
HIGH = lax.Precision.HIGHEST
RIGHT, LEFT, UPPER, LOWER = range(4)
STARTS = (0, 72, 144, 200, 8, 80, 16, 88)
steps8 = ((0, 1), (0, -1), (1, 0), (-1, 0), (1, 1), (1, -1), (-1, 1), (-1, -1))


def gll_tables():
    points = [-1.0, -1.0 / math.sqrt(5.0), 1.0 / math.sqrt(5.0), 1.0]
    weights = np.array([1.0 / 6.0, 5.0 / 6.0, 5.0 / 6.0, 1.0 / 6.0])
    spread = [
        math.prod([points[target] - points[others] for others in range(4) if others != target])
        for target in range(4)
    ]
    derivative = np.zeros((4, 4))
    for target in range(4):
        for source in range(4):
            if target == source:
                derivative[target, source] = sum(
                    1.0 / (points[target] - points[others]) for others in range(4) if others != target
                )
            else:
                derivative[target, source] = spread[target] / (
                    spread[source] * (points[target] - points[source])
                )
    return weights, 2.0 * derivative


WEIGHTS, FIRST = gll_tables()
SECOND = FIRST @ FIRST
CENTRE = float(SECOND[0, 0])


def offset_rows(table):
    rows = np.zeros((7, 4))
    for shift in range(-3, 4):
        for target in range(4):
            if 0 <= target + shift < 4:
                rows[shift + 3, target] = table[target, target + shift]
    return rows


def constant_tables():
    along_x = np.stack([np.kron(np.eye(32), FIRST.T), np.kron(np.eye(32), SECOND.T)])
    expand = np.kron(np.eye(32), WEIGHTS[:, None])
    tiles = np.zeros((25, 8, 128))
    expand_tiles = np.zeros((128, 128))
    expand_tiles[:, :32] = expand
    for base, table in ((0, FIRST), (7, SECOND)):
        tiles[base : base + 7] = np.tile(offset_rows(table), (1, 2))[:, :, None]
    tiles[14:21] = np.tile(offset_rows(SECOND), (1, 32))[:, None, :]
    arm_low = np.array([0.0, SECOND[0, 1], SECOND[0, 2], SECOND[0, 3]])
    arm_high = np.array([SECOND[3, 0], SECOND[3, 1], SECOND[3, 2], 0.0])
    tiles[21] = np.tile(arm_low, 32)[None]
    tiles[22] = np.tile(arm_high, 32)[None]
    high = np.array([-hyper_coef * WEIGHTS[a] / WEIGHTS[3] * SECOND[a, 3] for a in range(4)])
    low = np.array([-hyper_coef * WEIGHTS[a] / WEIGHTS[0] * SECOND[a, 0] for a in range(4)])
    tiles[23] = np.concatenate([[0.0, 0.0, 0.0, high[0]], high])[:, None]
    tiles[24] = np.concatenate([low, [low[3], 0.0, 0.0, 0.0]])[:, None]
    across = np.zeros(128)
    across[:5] = [*low, low[3]]
    across[123:] = [high[0], *high]
    widen = np.zeros((128, 256))
    for plane in range(24):
        start = 128 * (plane // 12) + 10 * (plane % 12)
        for lane in range(10):
            widen[24 * (lane < 5) + plane, start + lane] = across[(123 + lane) % 128]
        widen[72 + plane, start + 4] = 1.0
        widen[48 + plane, start + 5] = 1.0
    return (
        split_matrix(widen),
        split_matrix(along_x),
        jnp.asarray(
            np.concatenate([tiles, expand_tiles.reshape(16, 8, 128), expand.T.reshape(4, 8, 128)]), f32
        ),
    )


def lane_index(rows):
    return lax.broadcasted_iota(jnp.int32, (rows, 128), 1)


def turn(values, steps, axis=1):
    steps = steps % values.shape[axis]
    return values if steps == 0 else pltpu.roll(values, steps, axis)


def share_lanes(values):
    lane = lane_index(values.shape[0])
    first = (lane % 4 == 0) & (lane > 0)
    last = (lane % 4 == 3) & (lane < 127)
    return values + jnp.where(first, turn(values, 1), jnp.where(last, turn(values, 127), 0.0))


def share_rows(values):
    row = lax.broadcasted_iota(jnp.int32, values.shape, 0)
    first = (row % 4 == 0) & (row > 0)
    last = (row % 4 == 3) & (row < 127)
    return values + jnp.where(
        first, turn(values, 1, 0), jnp.where(last, turn(values, 127, 0), 0.0)
    )


def share_block(values):
    return share_rows(share_lanes(values))


def split_matrix(table):
    high = jnp.asarray(table, f32).astype(jnp.bfloat16)
    low = (jnp.asarray(table, f32) - high.astype(f32)).astype(jnp.bfloat16)
    return jnp.concatenate([high, high, low], -2)


def product(values, matrix):
    high = values.astype(jnp.bfloat16)
    low = (values - high.astype(f32)).astype(jnp.bfloat16)
    return jnp.dot(
        jnp.concatenate([high, low, high], 1), matrix, preferred_element_type=f32
    )


def along_rows(values, tiles_ref, base):
    grouped = values.reshape(16, 8, 128)
    total = grouped * tiles_ref[base + 3][None]
    for shift in (-3, -2, -1, 1, 2, 3):
        total = total + pltpu.roll(grouped, (-shift) % 8, 1) * tiles_ref[base + 3 + shift][None]
    return total.reshape(128, 128)


def second_lanes(values, tiles_ref):
    total = values * tiles_ref[17, 0:1]
    for shift in (-3, -2, -1, 1, 2, 3):
        total = total + turn(values, -shift) * tiles_ref[17 + shift, 0:1]
    return total


def pack_end(lines, at_high):
    lane = lane_index(8)
    start = 124 if at_high else 0
    packed = jnp.zeros((8, 128), f32)
    for part in range(3):
        moved = turn(lines[8 * part : 8 * part + 8], 4 * part - start)
        packed = jnp.where(lane // 4 == part, moved, packed)
    return packed


def pack_mass(line, at_high):
    lane = lane_index(8)
    start = 124 if at_high else 0
    wide = jnp.broadcast_to(line, (8, 128))
    packed = jnp.zeros((8, 128), f32)
    for part in range(3):
        packed = jnp.where(lane // 4 == 6 + part, turn(wide, 24 + 4 * part - start), packed)
    return packed


def fold_line(line):
    lane = lane_index(8)
    row = lax.broadcasted_iota(jnp.int32, (8, 128), 0)
    wide = jnp.broadcast_to(line, (8, 128))
    folded = jnp.zeros((8, 128), f32)
    for part in range(4):
        folded = jnp.where((row == part) & (lane // 32 == 2), turn(wide, 64 - 32 * part), folded)
    return folded


def unfold_line(tile):
    lane = lane_index(1)
    line = jnp.zeros((1, 128), f32)
    for part in range(4):
        line = jnp.where(lane // 32 == part, turn(tile[part : part + 1], 32 * part - 64), line)
    return line


def mass_of_nodes(elem_mass, tiles_ref):
    wide = tiles_ref[25:41].reshape(128, 128)[:, :32]
    rows = jnp.dot(wide, elem_mass, precision=HIGH, preferred_element_type=f32)
    return jnp.dot(
        rows, tiles_ref[41:45].reshape(32, 128), precision=HIGH, preferred_element_type=f32
    )


def find_tables(device, owner_ref, table_ref, cols_b):
    square = device // 16
    squares = cols_b // 4
    place = jnp.zeros((48, 128), f32)
    index = lax.broadcasted_iota(jnp.int32, (48, 1), 0)
    wanted = ((square + index // 16 + squares - 1) % squares) * 16 + index % 16
    lane = lane_index(1)
    own = jnp.zeros((1, 128), f32)
    for row in range(4):
        line = owner_ref[row : row + 1, :]
        code = (128 * row + lane).astype(f32)
        place = place + jnp.where(line == wanted, code, 0.0)
        own = own + jnp.where(line == device, code, 0.0)
    place = jnp.sum(place, axis=1, keepdims=True).astype(jnp.int32)
    own = jnp.sum(own, axis=1, keepdims=True).astype(jnp.int32)
    own_row, own_col = own // 128, own % 128
    rows, cols = place // 128, place % 128
    member = device % 16
    here_rows, here_cols = rows[16:32], cols[16:32]
    down, over = here_rows - own_row, here_cols - own_col
    inside = jnp.full((16, 1), -1, jnp.int32)
    for start, (step_y, step_x) in zip(STARTS, steps8):
        inside = jnp.where((down == step_y) & (over == step_x), start, inside)
    crossing = jnp.full((16, 1), 6, jnp.int32)
    sixteen = lax.broadcasted_iota(jnp.int32, (16, 1), 0)
    for side, start, step_x in ((0, 32, 1), (1, 0, -1)):
        picked = sixteen == member
        their = jnp.sum(
            jnp.where(picked, place[start : start + 16], 0).astype(f32), axis=0, keepdims=True
        ).astype(jnp.int32)
        their_row, their_col = their // 128, their % 128
        beside = their_col == (here_cols + step_x + cols_b) % cols_b
        for number, step_y in enumerate((0, 1, -1)):
            crossing = jnp.where(
                beside & (here_rows - their_row == step_y), 3 * side + number, crossing
            )
    way = lax.broadcasted_iota(jnp.int32, (8, 1), 0)
    step_y = jnp.zeros((8, 1), jnp.int32)
    step_x = jnp.zeros((8, 1), jnp.int32)
    for number, (along_y, along_x) in enumerate(steps8):
        step_y = jnp.where(way == number, along_y, step_y)
        step_x = jnp.where(way == number, along_x, step_x)
    near_row = own_row + step_y
    near_col = (own_col + step_x + cols_b) % cols_b
    found = jnp.zeros((8, 128), f32)
    for row in range(4):
        line = owner_ref[row : row + 1, :].astype(f32)
        found = found + jnp.where((near_row == row) & (near_col == lane), line, 0.0)
    found = jnp.sum(found, axis=1, keepdims=True).astype(jnp.int32)
    there = (near_row >= 0) & (near_row < 4)
    slot = 2 * (found % 16) + jnp.where(found // 16 == square, 0, 1)
    column = jnp.concatenate([inside, crossing, slot, there.astype(jnp.int32)], 0).astype(f32)
    picked = lax.broadcasted_iota(jnp.int32, (48, 128), 0) == lane_index(48)
    table_ref[...] = jnp.sum(jnp.where(picked, column, 0.0), axis=0, keepdims=True).astype(
        jnp.int32
    )


def share_band(values):
    across = share_lanes(values).reshape(16, 8, 128)
    row = lax.broadcasted_iota(jnp.int32, (1, 8, 128), 1)
    above = pltpu.roll(across, 1, 1)
    below = pltpu.roll(across, 7, 1)
    shared = across + jnp.where(row == 4, above, jnp.where(row == 3, below, 0.0))
    return shared.reshape(128, 128)


def changes(east, north, height, coriolis, mass, inverse, share, along_x_ref, tiles_ref):
    energy = 0.5 * (east * east + north * north) + height
    flux_x, flux_y = height * east, height * north
    first_x = product(jnp.concatenate([north, energy, flux_x], 0), along_x_ref[0])
    second_x = product(jnp.concatenate([east, north, height], 0), along_x_ref[1])
    absolute = first_x[:128] - along_rows(east, tiles_ref, 0) + coriolis
    tendencies = (
        absolute * north - first_x[128:256],
        -absolute * east - along_rows(energy, tiles_ref, 0),
        -(first_x[256:] + along_rows(flux_y, tiles_ref, 0)),
    )
    locals_, smoothed = [], []
    for part, values in enumerate((east, north, height)):
        lap = second_x[128 * part : 128 * part + 128] + along_rows(values, tiles_ref, 7)
        local = share(lap * mass)
        locals_.append(local)
        smoothed.append(local * inverse)
    second_x = product(jnp.concatenate(smoothed, 0), along_x_ref[1])
    changed = []
    for part in range(3):
        lap = second_x[128 * part : 128 * part + 128] + along_rows(smoothed[part], tiles_ref, 7)
        changed.append(share((tendencies[part] - hyper_coef * lap) * mass))
    return locals_, changed


def edge_kernel(
    velocity_far, height_far, coriolis_far, elem_mass_far, along_x_far, tiles_far,
    right_ref, left_ref, lines_ref, top_ref,
    smooth, change, velocity_ref, height_ref, coriolis_ref, elem_mass_ref,
    along_x_ref, tiles_ref, arrived,
):
    far = (elem_mass_far, tiles_far, height_far, velocity_far, coriolis_far, along_x_far)
    near = (elem_mass_ref, tiles_ref, height_ref, velocity_ref, coriolis_ref, along_x_ref)
    copies = [
        pltpu.make_async_copy(far[k], near[k], arrived.at[k]) for k in range(len(far))
    ]
    for copy in copies:
        copy.start()
    lane = lane_index(128)
    copies[0].wait()
    copies[1].wait()
    mass = mass_of_nodes(elem_mass_ref[0], tiles_ref)
    mass_t = jnp.transpose(mass)
    for copy in copies[2:]:
        copy.wait()
    coriolis = coriolis_ref[0]

    def upright_band(ref_value):
        return jnp.concatenate([ref_value[120:128], ref_value[0:8]], 0)

    def upright_plane(read):
        return jnp.concatenate(
            [piece for level in range(8) for piece in (read(level, 120), read(level, 0))], 0
        )

    def sideways_plane(read):
        packed = jnp.zeros((128, 128), f32)
        for level in range(8):
            packed = jnp.where(lane // 16 == level, turn(read(level), 8 + 16 * level), packed)
        return jnp.transpose(packed)

    def repeat(band):
        return jnp.concatenate([band] * 8, 0)

    row = lax.broadcasted_iota(jnp.int32, (128, 128), 0) % 16
    inner = (row != 7) & (row != 8) & (lane > 0) & (lane < 127)
    for way in range(2):
        if way == 0:
            planes = [
                upright_plane(lambda level, at, c=c: velocity_ref[c, level, at : at + 8, :])
                for c in range(2)
            ] + [upright_plane(lambda level, at: height_ref[level, at : at + 8, :])]
            turning = repeat(upright_band(coriolis))
            band_mass = repeat(upright_band(mass))
        else:
            top = jnp.zeros((128, 128), f32)
            for level in range(8):
                east, north = velocity_ref[0, level], velocity_ref[1, level]
                top = jnp.maximum(
                    top, jnp.sqrt(east * east + north * north) + jnp.sqrt(height_ref[level])
                )
            top_ref[...] = jnp.broadcast_to(jnp.max(top), top_ref.shape)
            planes = [
                sideways_plane(lambda level, c=c: velocity_ref[c, level]) for c in (1, 0)
            ] + [sideways_plane(lambda level: height_ref[level])]
            turning = -sideways_plane(lambda level: coriolis)
            band_mass = repeat(upright_band(mass_t))
        inverse = jnp.where(inner, 1.0 / share_band(band_mass), 0.0)
        locals_, changed = changes(
            *planes, turning, band_mass, inverse, share_band, along_x_ref, tiles_ref
        )
        for part in range(3):
            target = part if way == 0 or part == 2 else 1 - part
            smooth[way, target] = locals_[part]
            change[way, target] = changed[part]

    sizes = (72, 72, 56, 56)
    targets = [lines_ref.at[pl.ds(STARTS[side], sizes[side])] for side in range(4)]
    for way in range(2):
        for end in range(2):
            target = targets[2 * (1 - way) + end]
            for part in range(3):
                place = pl.ds(7 + end, 8, stride=16)
                target[8 * part : 8 * part + 8, :] = smooth.at[way, part][place, :]
                target[24 + 8 * part : 32 + 8 * part, :] = change.at[way, part][place, :]
    mass_lines = (mass_t[127:128], mass_t[0:1], mass[127:128], mass[0:1])
    lines = [targets[side][0:48, :] for side in range(4)]
    ends = {}
    for side in range(4):
        local_mass = share_lanes(mass_lines[side])
        for high in (False, True):
            ends[side, high] = pack_end(lines[side][0:24], high) + pack_mass(local_mass, high)
    extras = (
        ends[UPPER, True] + turn(ends[LOWER, True], 12),
        ends[UPPER, False] + turn(ends[LOWER, False], 12),
        ends[LEFT, True] + turn(ends[RIGHT, True], 12),
        ends[LEFT, False] + turn(ends[RIGHT, False], 12),
    )
    for side in range(4):
        targets[side][48:56, :] = extras[side] + fold_line(mass_lines[side])
    for number, (along, upward) in enumerate(((UPPER, True), (LOWER, False))):
        for across, sideways in ((RIGHT, True), (LEFT, False)):
            tile = ends[along, sideways] + turn(ends[across, upward], 12)
            tile = tile + turn(pack_end(lines[along][24:48], sideways), 48)
            targets[across][56 + 8 * number : 64 + 8 * number, :] = tile
    right_ref[...] = targets[RIGHT][...]
    left_ref[...] = targets[LEFT][...]


def fill_kernel(
    cols_b, device_ref, owner_ref, lines_ref, send_ref, table_ref,
    near_ref, sem,
):
    find_tables(device_ref[0], owner_ref, table_ref, cols_b)
    copy = pltpu.make_async_copy(table_ref, near_ref, sem)
    copy.start()
    copy.wait()
    for place in range(16):
        start = near_ref[0, place]

        @pl.when(start >= 0)
        def _(place=place, start=start):
            send_ref[place, 0] = lines_ref[pl.ds(pl.multiple_of(start, 8), 56), :]


def block_kernel(
    velocity_ref, height_ref, coriolis_ref, elem_mass_ref, along_x_ref, tiles_ref, after_ref,
    partial_ref, node_mass, inner_inverse,
):
    lane = lane_index(128)
    step = pl.program_id(0)

    @pl.when(step == 0)
    def _():
        node_mass[...] = mass_of_nodes(elem_mass_ref[0], tiles_ref)
        local_mass = share_block(node_mass[...])
        row = lax.broadcasted_iota(jnp.int32, (128, 128), 0)
        inner = (row > 0) & (row < 127) & (lane > 0) & (lane < 127)
        inner_inverse[...] = jnp.where(inner, 1.0 / local_mass, 0.0)

    @pl.when(step < 8)
    def _():
        _, changed = changes(
            velocity_ref[0, 0], velocity_ref[1, 0], height_ref[0], coriolis_ref[0],
            node_mass[...], inner_inverse[...], share_block, along_x_ref, tiles_ref,
        )
        for part in range(3):
            partial_ref[part] = changed[part]

    @pl.when(step == 8)
    def _():
        partial_ref[0] = share_block(node_mass[...])


def pack_kernel(table_ref, ahead_ref, behind_ref, tops_ref, send_in, send_far, crossing_ref, sem):
    lane = lane_index(8)
    top = jnp.max(tops_ref[...], axis=(0, 1), keepdims=True)[0]
    for place in range(16):
        crossing = table_ref[0, 16 + place]
        for base, ref in ((0, ahead_ref), (3, behind_ref)):

            @pl.when((crossing >= base) & (crossing < base + 3))
            def _(place=place, base=base, ref=ref, crossing=crossing):
                start = pl.multiple_of(8 * (crossing - base), 8)
                crossing_ref[place] = ref[pl.ds(start, 56), :]

        crossing_ref[place, 48:56, :] = jnp.where(lane >= 96, top, crossing_ref[place, 48:56, :])
    copy = pltpu.make_async_copy(crossing_ref, send_far.at[:, 1], sem)
    copy.start()
    copy.wait()


def edge_terms(table_ref, lines, received_ref, tiles_ref):
    lane = lane_index(1)

    def message(way, start, stop):
        values = received_ref[table_ref[0, 32 + way], start:stop, :]
        return jnp.where(table_ref[0, 40 + way] > 0, values, 0.0)

    own = [line[0:24, :] for line in lines]
    own_mass = [unfold_line(line[48:56, :]) for line in lines]
    near = [message(side, 0, 24) for side in range(4)]
    change = [message(side, 24, 48) for side in range(4)]
    extra = [message(side, 48, 56) for side in range(4)]
    mass = [unfold_line(extra[side]) for side in range(4)]
    shared_mass = [share_lanes(mass[side]) for side in range(4)]
    total = [own[side] + near[side] for side in range(4)]
    total_mass = [share_lanes(own_mass[side]) + shared_mass[side] for side in range(4)]
    corners = []
    for along in (UPPER, LOWER):
        for across in (RIGHT, LEFT):
            corner = 4 + 2 * (along - UPPER) + across
            at_x = 127 if across == RIGHT else 0
            at_y = 127 if along == UPPER else 0
            tile = message(corner, 48, 56)
            end_x = 0 if across == RIGHT else 3

            def spread_out(packed, start, at_x=at_x):
                return jnp.concatenate(
                    [turn(packed, at_x - start - 4 * part) for part in range(3)], 0
                )

            far = spread_out(tile, end_x)
            far_mass = turn(tile, at_x - 24 - end_x)[0:1]
            corners.append((along, across, at_x, at_y, tile, far_mass, spread_out))
            on_x, on_y = lane == at_x, lane == at_y
            total[along] = total[along] + jnp.where(
                on_x, turn(near[across], at_x - at_y) + far, 0.0
            )
            total_mass[along] = total_mass[along] + jnp.where(
                on_x, turn(mass[across], at_x - at_y) + far_mass, 0.0
            )
            total[across] = total[across] + jnp.where(
                on_y, turn(near[along] + far, at_y - at_x), 0.0
            )
            total_mass[across] = total_mass[across] + jnp.where(
                on_y, turn(mass[along] + far_mass, at_y - at_x), 0.0
            )
    smooth = [total[side] / total_mass[side] for side in range(4)]
    curve = [second_lanes(smooth[side], tiles_ref) for side in range(4)]
    added = [
        change[side]
        - hyper_coef
        * (shared_mass[side] * CENTRE * smooth[side] + share_lanes(mass[side] * curve[side]))
        for side in range(4)
    ]

    def arm(beside, diagonal, coefs):
        both = beside + diagonal
        weight = turn(both, -24)
        value = jnp.where(weight > 0.0, both / jnp.where(weight > 0.0, weight, 1.0), 0.0) * coefs
        value = value + turn(value, -1)
        return value + turn(value, -2)

    for along, across, at_x, at_y, tile, far_mass, spread_out in corners:
        beside = extra[across] if along == UPPER else turn(extra[across], -12)
        arm_x = spread_out(arm(beside, tile, tiles_ref[21 if across == RIGHT else 22]), 0)
        beside = extra[along] if across == LEFT else turn(extra[along], -12)
        arm_y = spread_out(
            arm(beside, turn(tile, -12), tiles_ref[21 if along == UPPER else 22]), 0
        )
        middle = CENTRE * smooth[along]
        arm_x, arm_y = arm_x + middle, arm_y + middle
        own_x = curve[along]
        own_y = turn(curve[across], at_x - at_y)
        mass_x = turn(mass[across], at_x - at_y)
        end_x = 0 if across == RIGHT else 3
        value = (
            turn(change[across], at_x - at_y) + change[along] + spread_out(tile, 48 + end_x)
        ) - hyper_coef * (
            mass_x * (arm_x + own_y) + mass[along] * (own_x + arm_y) + far_mass * (arm_x + arm_y)
        )
        added[along] = jnp.where(lane == at_x, value, added[along])
    ends = (lane == 0) | (lane == 127)
    plain, edge = [], []
    for side in range(4):
        line = smooth[side] if side >= UPPER else jnp.where(ends, 0.0, smooth[side])
        outside = added[side] if side >= UPPER else jnp.where(ends, 0.0, added[side])
        bend = curve[side] if side >= UPPER else second_lanes(line, tiles_ref)
        plain.append(share_lanes(own_mass[side] * line))
        edge.append(outside - hyper_coef * share_lanes(own_mass[side] * bend))
    return plain, edge, total_mass


def last_kernel(
    table_ref, lines_ref, received_ref, tiles_ref, widen_ref,
    velocity_far, height_far, partial_far, new_velocity_far, new_height_far,
    rows, velocity_ref, height_ref, partial_ref, arrived, left_off,
):
    lane = lane_index(128)
    mass_in = pltpu.make_async_copy(partial_far.at[24], partial_ref.at[24], arrived.at[3, 0])
    mass_in.start()
    incoming = []
    for group in range(GROUPS):
        part = pl.ds(LEVELS_EACH * group, LEVELS_EACH)
        incoming.append(
            (
                pltpu.make_async_copy(
                    partial_far.at[pl.ds(3 * LEVELS_EACH * group, 3 * LEVELS_EACH)],
                    partial_ref.at[pl.ds(3 * LEVELS_EACH * group, 3 * LEVELS_EACH)],
                    arrived.at[0, group],
                ),
                pltpu.make_async_copy(
                    velocity_far.at[:, part], velocity_ref.at[:, part], arrived.at[1, group]
                ),
                pltpu.make_async_copy(
                    height_far.at[part], height_ref.at[part], arrived.at[2, group]
                ),
            )
        )
        for copy in incoming[-1]:
            copy.start()

    lines = [lines_ref.at[pl.ds(STARTS[side], 56)] for side in range(4)]
    plain, edge, total_mass = edge_terms(table_ref, lines, received_ref, tiles_ref)
    rows[0] = plain[UPPER]
    rows[1] = plain[LOWER]
    rows[2] = edge[UPPER]
    rows[3] = edge[LOWER]
    stacked = jnp.concatenate(
        [plain[LEFT], plain[RIGHT], edge[LEFT], edge[RIGHT]]
        + [jnp.broadcast_to(total_mass[side], (16, 128)) for side in (LEFT, RIGHT)],
        0,
    )
    columns = jnp.transpose(stacked)
    mass_in.wait()
    mass = partial_ref[24]
    mass = jnp.where(lane == 0, columns[:, 96:97], mass)
    mass = jnp.where(lane == 127, columns[:, 112:113], mass)
    row = lax.broadcasted_iota(jnp.int32, (128, 128), 0)
    mass = jnp.where(row == 127, total_mass[UPPER], mass)
    mass = jnp.where(row == 0, total_mass[LOWER], mass)
    top = jnp.zeros((8, 128), f32)
    for place in range(16):
        top = jnp.maximum(top, received_ref[2 * place + 1, 48:56, :])
    top = jnp.max(
        jnp.where(lane_index(8) >= 96, top, 0.0), axis=(0, 1), keepdims=True
    )
    factor = (courant / top) / mass
    near_edge = (lane < 5) | (lane > 122)
    widened = product(columns, widen_ref[...])
    row = lax.broadcasted_iota(jnp.int32, (8, 128), 0)
    outgoing = []
    for group in range(GROUPS):
        for copy in incoming[group]:
            copy.wait()
        for level in range(LEVELS_EACH * group, LEVELS_EACH * (group + 1)):
            for part in range(3):
                at = 8 * part + level
                half = 128 * (at // 12)
                beside = turn(widened[:, half : half + 128], 123 - 10 * (at % 12))
                value = partial_ref[3 * level + part] + jnp.where(near_edge, beside, 0.0)
                upper = tiles_ref[23] * rows[0, at : at + 1, :]
                lower = tiles_ref[24] * rows[1, at : at + 1, :]
                upper = upper + jnp.where(row == 7, rows[2, at : at + 1, :], 0.0)
                lower = lower + jnp.where(row == 0, rows[3, at : at + 1, :], 0.0)
                value = jnp.concatenate([value[:8] + lower, value[8:120], value[120:] + upper], 0)
                if part < 2:
                    velocity_ref[part, level] = velocity_ref[part, level] + factor * value
                else:
                    height_ref[level] = height_ref[level] + factor * value
        part = pl.ds(LEVELS_EACH * group, LEVELS_EACH)
        for copy in (
            pltpu.make_async_copy(
                velocity_ref.at[:, part], new_velocity_far.at[:, part], left_off.at[0, group]
            ),
            pltpu.make_async_copy(
                height_ref.at[part], new_height_far.at[part], left_off.at[1, group]
            ),
        ):
            copy.start()
            outgoing.append(copy)
    for copy in outgoing:
        copy.wait()


def whole(shape, space=None):
    if space is None:
        return pl.BlockSpec(shape, lambda level: (0,) * len(shape))
    return pl.BlockSpec(memory_space=space)


def per_device(velocity, thickness, coriolis, elem_mass, block_owner):
    cols_b = block_owner.shape[1]
    count = 4 * cols_b
    velocity = velocity[:, :, 0]
    thickness = thickness[:, 0]
    widen, along_x, tiles = constant_tables()
    device = (lax.axis_index("elem") * lax.axis_size("sub") + lax.axis_index("sub")).reshape(1)
    if cols_b < 128:
        block_owner = jnp.pad(block_owner, ((0, 0), (0, 128 - cols_b)), constant_values=-1)
    shape = jax.ShapeDtypeStruct
    params = pltpu.CompilerParams(
        dimension_semantics=("arbitrary",), vmem_limit_bytes=BLOCK_VMEM
    )
    vmem = pltpu.VMEM
    far = pl.BlockSpec(memory_space=pltpu.HBM)
    held = pl.BlockSpec(memory_space=vmem)
    small = pl.BlockSpec(memory_space=pltpu.SMEM)
    arrays = (velocity, thickness, coriolis, elem_mass, along_x, tiles)
    right, left, lines, top = pl.pallas_call(
        edge_kernel,
        in_specs=[far] * 6,
        out_specs=[held] * 4,
        out_shape=[
            shape((72, 128), f32), shape((72, 128), f32), shape((256, 128), f32),
            shape((TOP_ROWS, 128), f32),
        ],
        scratch_shapes=[
            pltpu.VMEM((2, 3, 128, 128), f32), pltpu.VMEM((2, 3, 128, 128), f32),
        ]
        + [pltpu.VMEM(array.shape, array.dtype) for array in arrays]
        + [pltpu.SemaphoreType.DMA((6,))],
        compiler_params=pltpu.CompilerParams(vmem_limit_bytes=EDGE_VMEM),
        name="edge",
    )(*arrays)
    squares = count // 16
    same_place = [[16 * s + i for s in range(squares)] for i in range(16)]
    same_square = [[16 * s + i for i in range(16)] for s in range(squares)]
    tops = lax.all_to_all(
        top[: 8 * squares], axes, 0, 0, axis_index_groups=same_place, tiled=True
    )
    ahead = lax.ppermute(left, axes, [(b, (b - 16) % count) for b in range(count)])
    behind = lax.ppermute(right, axes, [(b, (b + 16) % count) for b in range(count)])
    send, table = pl.pallas_call(
        functools.partial(fill_kernel, cols_b),
        in_specs=[small] + [held] * 2,
        out_specs=[held] * 2,
        out_shape=[shape((16, 2, 56, 128), f32), shape((1, 128), jnp.int32)],
        scratch_shapes=[pltpu.SMEM((1, 128), jnp.int32), pltpu.SemaphoreType.DMA(())],
        compiler_params=pltpu.CompilerParams(vmem_limit_bytes=FILL_VMEM),
        cost_estimate=pl.CostEstimate(flops=0, bytes_accessed=2_000_000, transcendentals=0),
        name="fill",
    )(device, block_owner, lines)
    send = pl.pallas_call(
        pack_kernel,
        in_specs=[small] + [held] * 3 + [far],
        out_specs=far,
        out_shape=shape((16, 2, 56, 128), f32),
        input_output_aliases={4: 0},
        scratch_shapes=[pltpu.VMEM((16, 56, 128), f32), pltpu.SemaphoreType.DMA(())],
        compiler_params=pltpu.CompilerParams(vmem_limit_bytes=PACK_VMEM),
        name="pack",
    )(table, ahead, behind, tops, send)
    received = lax.all_to_all(
        send.reshape(16, 112, 128), axes, 0, 0, axis_index_groups=same_square, tiled=True
    ).reshape(32, 56, 128)
    pair = pl.BlockSpec((2, 1, 128, 128), lambda step: (0, jnp.minimum(step, 7), 0, 0))
    single = pl.BlockSpec((1, 128, 128), lambda step: (jnp.minimum(step, 7), 0, 0))
    partial = pl.pallas_call(
        block_kernel,
        grid=(9,),
        in_specs=[
            pair, single, whole((1, 128, 128)), whole((1, 32, 32)), whole((2, 384, 128)),
            whole((45, 8, 128)), whole((1, 8, 128)),
        ],
        out_specs=pl.BlockSpec((3, 128, 128), lambda step: (step, 0, 0)),
        out_shape=shape((27, 128, 128), f32),
        scratch_shapes=[pltpu.VMEM((128, 128), f32), pltpu.VMEM((128, 128), f32)],
        compiler_params=params,
        cost_estimate=pl.CostEstimate(
            flops=2_000_000_000, bytes_accessed=3_200_000, transcendentals=0
        ),
        name="block",
    )(velocity, thickness, coriolis, elem_mass, along_x, tiles, send.reshape(32, 56, 128))
    new_velocity, new_thickness = pl.pallas_call(
        last_kernel,
        in_specs=[small] + [held] * 4 + [far] * 3,
        out_specs=[far] * 2,
        out_shape=[shape((2, 8, 128, 128), f32), shape((8, 128, 128), f32)],
        scratch_shapes=[
            pltpu.VMEM((4, 24, 128), f32), pltpu.VMEM((2, 8, 128, 128), f32),
            pltpu.VMEM((8, 128, 128), f32), pltpu.VMEM((25, 128, 128), f32),
            pltpu.SemaphoreType.DMA((4, GROUPS)), pltpu.SemaphoreType.DMA((2, GROUPS)),
        ],
        compiler_params=pltpu.CompilerParams(vmem_limit_bytes=LAST_VMEM),
        name="last",
    )(table, lines, received, tiles, widen, velocity, thickness, partial)
    return new_velocity[:, :, None], new_thickness[:, None]


def solution(mesh):
    return jax.shard_map(
        per_device,
        mesh=mesh,
        in_specs=(
            P(None, None, axes, None, None),
            P(None, axes, None, None),
            P(axes, None, None),
            P(axes, None, None),
            P(),
        ),
        out_specs=(
            P(None, None, axes, None, None),
            P(None, axes, None, None),
        ),
        check_vma=False,
    )
```

```python
import functools
import math

import jax
import jax.numpy as jnp
import numpy as np
from jax import lax
from jax.experimental import pallas as pl
from jax.experimental.pallas import tpu as pltpu
from jax.sharding import PartitionSpec as P

courant = 0.1
hyper_coef = 0.002
TOP_ROWS = 8
MIB = 1024 * 1024
EDGE_VMEM = 60 * MIB
PACK_VMEM = 52 * MIB
BLOCK_VMEM = 60 * MIB
LAST_VMEM = 51 * MIB
GROUPS = 2
LEVELS_EACH = 8 // GROUPS
axes = ("elem", "sub")
f32 = jnp.float32
HIGH = lax.Precision.HIGHEST
RIGHT, LEFT, UPPER, LOWER = range(4)
STARTS = (0, 72, 144, 200, 8, 80, 16, 88)
steps8 = ((0, 1), (0, -1), (1, 0), (-1, 0), (1, 1), (1, -1), (-1, 1), (-1, -1))


def gll_tables():
    points = [-1.0, -1.0 / math.sqrt(5.0), 1.0 / math.sqrt(5.0), 1.0]
    weights = np.array([1.0 / 6.0, 5.0 / 6.0, 5.0 / 6.0, 1.0 / 6.0])
    spread = [
        math.prod([points[target] - points[others] for others in range(4) if others != target])
        for target in range(4)
    ]
    derivative = np.zeros((4, 4))
    for target in range(4):
        for source in range(4):
            if target == source:
                derivative[target, source] = sum(
                    1.0 / (points[target] - points[others]) for others in range(4) if others != target
                )
            else:
                derivative[target, source] = spread[target] / (
                    spread[source] * (points[target] - points[source])
                )
    return weights, 2.0 * derivative


WEIGHTS, FIRST = gll_tables()
SECOND = FIRST @ FIRST
CENTRE = float(SECOND[0, 0])


def offset_rows(table):
    rows = np.zeros((7, 4))
    for shift in range(-3, 4):
        for target in range(4):
            if 0 <= target + shift < 4:
                rows[shift + 3, target] = table[target, target + shift]
    return rows


def constant_tables():
    along_x = np.stack([np.kron(np.eye(32), FIRST.T), np.kron(np.eye(32), SECOND.T)])
    expand = np.kron(np.eye(32), WEIGHTS[:, None])
    tiles = np.zeros((25, 8, 128))
    expand_tiles = np.zeros((128, 128))
    expand_tiles[:, :32] = expand
    for base, table in ((0, FIRST), (7, SECOND)):
        tiles[base : base + 7] = np.tile(offset_rows(table), (1, 2))[:, :, None]
    tiles[14:21] = np.tile(offset_rows(SECOND), (1, 32))[:, None, :]
    arm_low = np.array([0.0, SECOND[0, 1], SECOND[0, 2], SECOND[0, 3]])
    arm_high = np.array([SECOND[3, 0], SECOND[3, 1], SECOND[3, 2], 0.0])
    tiles[21] = np.tile(arm_low, 32)[None]
    tiles[22] = np.tile(arm_high, 32)[None]
    high = np.array([-hyper_coef * WEIGHTS[a] / WEIGHTS[3] * SECOND[a, 3] for a in range(4)])
    low = np.array([-hyper_coef * WEIGHTS[a] / WEIGHTS[0] * SECOND[a, 0] for a in range(4)])
    tiles[23] = np.concatenate([[0.0, 0.0, 0.0, high[0]], high])[:, None]
    tiles[24] = np.concatenate([low, [low[3], 0.0, 0.0, 0.0]])[:, None]
    across = np.zeros(128)
    across[:5] = [*low, low[3]]
    across[123:] = [high[0], *high]
    widen = np.zeros((128, 256))
    for plane in range(24):
        start = 128 * (plane // 12) + 10 * (plane % 12)
        for lane in range(10):
            widen[24 * (lane < 5) + plane, start + lane] = across[(123 + lane) % 128]
        widen[72 + plane, start + 4] = 1.0
        widen[48 + plane, start + 5] = 1.0
    return (
        split_matrix(widen),
        split_matrix(along_x),
        jnp.asarray(
            np.concatenate([tiles, expand_tiles.reshape(16, 8, 128), expand.T.reshape(4, 8, 128)]), f32
        ),
    )


def lane_index(rows):
    return lax.broadcasted_iota(jnp.int32, (rows, 128), 1)


def turn(values, steps, axis=1):
    steps = steps % values.shape[axis]
    return values if steps == 0 else pltpu.roll(values, steps, axis)


def share_lanes(values):
    lane = lane_index(values.shape[0])
    first = (lane % 4 == 0) & (lane > 0)
    last = (lane % 4 == 3) & (lane < 127)
    return values + jnp.where(first, turn(values, 1), jnp.where(last, turn(values, 127), 0.0))


def share_rows(values):
    row = lax.broadcasted_iota(jnp.int32, values.shape, 0)
    first = (row % 4 == 0) & (row > 0)
    last = (row % 4 == 3) & (row < 127)
    return values + jnp.where(
        first, turn(values, 1, 0), jnp.where(last, turn(values, 127, 0), 0.0)
    )


def share_block(values):
    return share_rows(share_lanes(values))


def split_matrix(table):
    high = jnp.asarray(table, f32).astype(jnp.bfloat16)
    low = (jnp.asarray(table, f32) - high.astype(f32)).astype(jnp.bfloat16)
    return jnp.concatenate([high, high, low], -2)


def product(values, matrix):
    high = values.astype(jnp.bfloat16)
    low = (values - high.astype(f32)).astype(jnp.bfloat16)
    return jnp.dot(
        jnp.concatenate([high, low, high], 1), matrix, preferred_element_type=f32
    )


def along_rows(values, tiles_ref, base):
    grouped = values.reshape(16, 8, 128)
    total = grouped * tiles_ref[base + 3][None]
    for shift in (-3, -2, -1, 1, 2, 3):
        total = total + pltpu.roll(grouped, (-shift) % 8, 1) * tiles_ref[base + 3 + shift][None]
    return total.reshape(128, 128)


def second_lanes(values, tiles_ref):
    total = values * tiles_ref[17, 0:1]
    for shift in (-3, -2, -1, 1, 2, 3):
        total = total + turn(values, -shift) * tiles_ref[17 + shift, 0:1]
    return total


def pack_end(lines, at_high):
    lane = lane_index(8)
    start = 124 if at_high else 0
    packed = jnp.zeros((8, 128), f32)
    for part in range(3):
        moved = turn(lines[8 * part : 8 * part + 8], 4 * part - start)
        packed = jnp.where(lane // 4 == part, moved, packed)
    return packed


def pack_mass(line, at_high):
    lane = lane_index(8)
    start = 124 if at_high else 0
    wide = jnp.broadcast_to(line, (8, 128))
    packed = jnp.zeros((8, 128), f32)
    for part in range(3):
        packed = jnp.where(lane // 4 == 6 + part, turn(wide, 24 + 4 * part - start), packed)
    return packed


def fold_line(line):
    lane = lane_index(8)
    row = lax.broadcasted_iota(jnp.int32, (8, 128), 0)
    wide = jnp.broadcast_to(line, (8, 128))
    folded = jnp.zeros((8, 128), f32)
    for part in range(4):
        folded = jnp.where((row == part) & (lane // 32 == 2), turn(wide, 64 - 32 * part), folded)
    return folded


def unfold_line(tile):
    lane = lane_index(1)
    line = jnp.zeros((1, 128), f32)
    for part in range(4):
        line = jnp.where(lane // 32 == part, turn(tile[part : part + 1], 32 * part - 64), line)
    return line


def mass_of_nodes(elem_mass, tiles_ref):
    wide = tiles_ref[25:41].reshape(128, 128)[:, :32]
    rows = jnp.dot(wide, elem_mass, precision=HIGH, preferred_element_type=f32)
    return jnp.dot(
        rows, tiles_ref[41:45].reshape(32, 128), precision=HIGH, preferred_element_type=f32
    )


def find_tables(device, owner_ref, table_ref, cols_b):
    square = device // 16
    squares = cols_b // 4
    place = jnp.zeros((48, 128), f32)
    index = lax.broadcasted_iota(jnp.int32, (48, 1), 0)
    wanted = ((square + index // 16 + squares - 1) % squares) * 16 + index % 16
    lane = lane_index(1)
    own = jnp.zeros((1, 128), f32)
    for row in range(4):
        line = owner_ref[row : row + 1, :]
        code = (128 * row + lane).astype(f32)
        place = place + jnp.where(line == wanted, code, 0.0)
        own = own + jnp.where(line == device, code, 0.0)
    place = jnp.sum(place, axis=1, keepdims=True).astype(jnp.int32)
    own = jnp.sum(own, axis=1, keepdims=True).astype(jnp.int32)
    own_row, own_col = own // 128, own % 128
    rows, cols = place // 128, place % 128
    member = device % 16
    here_rows, here_cols = rows[16:32], cols[16:32]
    down, over = here_rows - own_row, here_cols - own_col
    inside = jnp.full((16, 1), -1, jnp.int32)
    for start, (step_y, step_x) in zip(STARTS, steps8):
        inside = jnp.where((down == step_y) & (over == step_x), start, inside)
    crossing = jnp.full((16, 1), -1, jnp.int32)
    sixteen = lax.broadcasted_iota(jnp.int32, (16, 1), 0)
    sources = []
    for side, begin, step_x in ((RIGHT, 32, 1), (LEFT, 0, -1)):
        there_rows, there_cols = rows[begin : begin + 16], cols[begin : begin + 16]
        beside = there_cols == (own_col + step_x + cols_b) % cols_b
        picked = sixteen == member
        their = jnp.sum(
            jnp.where(picked, place[begin : begin + 16], 0).astype(f32), axis=0, keepdims=True
        ).astype(jnp.int32)
        their_row, their_col = their // 128, their % 128
        facing = here_cols == (their_col - step_x + cols_b) % cols_b
        for number, step_y in enumerate((0, 1, -1)):
            start = STARTS[side] if step_y == 0 else STARTS[side] + 8 * number
            crossing = jnp.where(beside & (there_rows - own_row == step_y), start, crossing)
            found = facing & (their_row - here_rows == step_y)
            sources.append(
                jnp.sum(jnp.where(found, sixteen, 0).astype(f32), axis=0, keepdims=True).astype(
                    jnp.int32
                )
            )
    way = lax.broadcasted_iota(jnp.int32, (8, 1), 0)
    step_y = jnp.zeros((8, 1), jnp.int32)
    step_x = jnp.zeros((8, 1), jnp.int32)
    for number, (along_y, along_x) in enumerate(steps8):
        step_y = jnp.where(way == number, along_y, step_y)
        step_x = jnp.where(way == number, along_x, step_x)
    near_row = own_row + step_y
    near_col = (own_col + step_x + cols_b) % cols_b
    found = jnp.zeros((8, 128), f32)
    for row in range(4):
        line = owner_ref[row : row + 1, :].astype(f32)
        found = found + jnp.where((near_row == row) & (near_col == lane), line, 0.0)
    found = jnp.sum(found, axis=1, keepdims=True).astype(jnp.int32)
    there = (near_row >= 0) & (near_row < 4)
    slot = 2 * (found % 16)
    kind = jnp.where(there, jnp.where(found // 16 == square, 1, 2), 0)
    ahead_of = jnp.where(way == 0, sources[0], 0)
    for number in range(1, 6):
        ahead_of = jnp.where(way == number, sources[number], ahead_of)
    column = jnp.concatenate([inside, crossing, slot, kind, ahead_of], 0).astype(f32)
    picked = lax.broadcasted_iota(jnp.int32, (56, 128), 0) == lane_index(56)
    table_ref[...] = jnp.sum(jnp.where(picked, column, 0.0), axis=0, keepdims=True).astype(
        jnp.int32
    )


def share_band(values):
    across = share_lanes(values).reshape(16, 8, 128)
    row = lax.broadcasted_iota(jnp.int32, (1, 8, 128), 1)
    above = pltpu.roll(across, 1, 1)
    below = pltpu.roll(across, 7, 1)
    shared = across + jnp.where(row == 4, above, jnp.where(row == 3, below, 0.0))
    return shared.reshape(128, 128)


def changes(east, north, height, coriolis, mass, inverse, share, along_x_ref, tiles_ref):
    energy = 0.5 * (east * east + north * north) + height
    flux_x, flux_y = height * east, height * north
    first_x = product(jnp.concatenate([north, energy, flux_x], 0), along_x_ref[0])
    second_x = product(jnp.concatenate([east, north, height], 0), along_x_ref[1])
    absolute = first_x[:128] - along_rows(east, tiles_ref, 0) + coriolis
    tendencies = (
        absolute * north - first_x[128:256],
        -absolute * east - along_rows(energy, tiles_ref, 0),
        -(first_x[256:] + along_rows(flux_y, tiles_ref, 0)),
    )
    locals_, smoothed = [], []
    for part, values in enumerate((east, north, height)):
        lap = second_x[128 * part : 128 * part + 128] + along_rows(values, tiles_ref, 7)
        local = share(lap * mass)
        locals_.append(local)
        smoothed.append(local * inverse)
    second_x = product(jnp.concatenate(smoothed, 0), along_x_ref[1])
    changed = []
    for part in range(3):
        lap = second_x[128 * part : 128 * part + 128] + along_rows(smoothed[part], tiles_ref, 7)
        changed.append(share((tendencies[part] - hyper_coef * lap) * mass))
    return locals_, changed


def edge_kernel(
    cols_b, device_ref, owner_far,
    velocity_far, height_far, coriolis_far, elem_mass_far, along_x_far, tiles_far,
    lines_ref, send_ref, table_ref,
    smooth, change, owner_ref, near_ref, velocity_ref, height_ref, coriolis_ref, elem_mass_ref,
    along_x_ref, tiles_ref, arrived,
):
    far = (
        owner_far, elem_mass_far, tiles_far, height_far, velocity_far, coriolis_far, along_x_far,
    )
    near = (
        owner_ref, elem_mass_ref, tiles_ref, height_ref, velocity_ref, coriolis_ref, along_x_ref,
    )
    copies = [
        pltpu.make_async_copy(far[k], near[k], arrived.at[k]) for k in range(len(far))
    ]
    for copy in copies:
        copy.start()
    lane = lane_index(128)
    copies[0].wait()
    find_tables(device_ref[0], owner_ref, table_ref, cols_b)
    table_copy = pltpu.make_async_copy(table_ref, near_ref, arrived.at[7])
    table_copy.start()
    copies[1].wait()
    copies[2].wait()
    mass = mass_of_nodes(elem_mass_ref[0], tiles_ref)
    mass_t = jnp.transpose(mass)
    for copy in copies[3:]:
        copy.wait()
    coriolis = coriolis_ref[0]

    def upright_band(ref_value):
        return jnp.concatenate([ref_value[120:128], ref_value[0:8]], 0)

    def upright_plane(read):
        return jnp.concatenate(
            [piece for level in range(8) for piece in (read(level, 120), read(level, 0))], 0
        )

    def sideways_plane(read):
        packed = jnp.zeros((128, 128), f32)
        for level in range(8):
            packed = jnp.where(lane // 16 == level, turn(read(level), 8 + 16 * level), packed)
        return jnp.transpose(packed)

    def repeat(band):
        return jnp.concatenate([band] * 8, 0)

    row = lax.broadcasted_iota(jnp.int32, (128, 128), 0) % 16
    inner = (row != 7) & (row != 8) & (lane > 0) & (lane < 127)
    for way in range(2):
        if way == 0:
            planes = [
                upright_plane(lambda level, at, c=c: velocity_ref[c, level, at : at + 8, :])
                for c in range(2)
            ] + [upright_plane(lambda level, at: height_ref[level, at : at + 8, :])]
            turning = repeat(upright_band(coriolis))
            band_mass = repeat(upright_band(mass))
        else:
            top = jnp.zeros((128, 128), f32)
            for level in range(8):
                east, north = velocity_ref[0, level], velocity_ref[1, level]
                top = jnp.maximum(
                    top, jnp.sqrt(east * east + north * north) + jnp.sqrt(height_ref[level])
                )
            top = jnp.max(top, axis=(0, 1), keepdims=True)
            planes = [
                sideways_plane(lambda level, c=c: velocity_ref[c, level]) for c in (1, 0)
            ] + [sideways_plane(lambda level: height_ref[level])]
            turning = -sideways_plane(lambda level: coriolis)
            band_mass = repeat(upright_band(mass_t))
        inverse = jnp.where(inner, 1.0 / share_band(band_mass), 0.0)
        locals_, changed = changes(
            *planes, turning, band_mass, inverse, share_band, along_x_ref, tiles_ref
        )
        for part in range(3):
            target = part if way == 0 or part == 2 else 1 - part
            smooth[way, target] = locals_[part]
            change[way, target] = changed[part]

    sizes = (72, 72, 56, 56)
    targets = [lines_ref.at[pl.ds(STARTS[side], sizes[side])] for side in range(4)]
    for way in range(2):
        for end in range(2):
            target = targets[2 * (1 - way) + end]
            for part in range(3):
                place = pl.ds(7 + end, 8, stride=16)
                target[8 * part : 8 * part + 8, :] = smooth.at[way, part][place, :]
                target[24 + 8 * part : 32 + 8 * part, :] = change.at[way, part][place, :]
    mass_lines = (mass_t[127:128], mass_t[0:1], mass[127:128], mass[0:1])
    lines = [targets[side][0:48, :] for side in range(4)]
    ends = {}
    for side in range(4):
        local_mass = share_lanes(mass_lines[side])
        for high in (False, True):
            ends[side, high] = pack_end(lines[side][0:24], high) + pack_mass(local_mass, high)
    extras = (
        ends[UPPER, True] + turn(ends[LOWER, True], 12),
        ends[UPPER, False] + turn(ends[LOWER, False], 12),
        ends[LEFT, True] + turn(ends[RIGHT, True], 12),
        ends[LEFT, False] + turn(ends[RIGHT, False], 12),
    )
    for side in range(4):
        targets[side][48:56, :] = extras[side] + fold_line(mass_lines[side])
    for number, (along, upward) in enumerate(((UPPER, True), (LOWER, False))):
        for across, sideways in ((RIGHT, True), (LEFT, False)):
            tile = ends[along, sideways] + turn(ends[across, upward], 12)
            tile = tile + turn(pack_end(lines[along][24:48], sideways), 48)
            targets[across][56 + 8 * number : 64 + 8 * number, :] = tile
    table_copy.wait()
    after = lane_index(8) >= 96
    for place in range(16):
        for part in range(2):
            start = near_ref[0, 16 * part + place]

            @pl.when(start >= 0)
            def _(place=place, part=part, start=start):
                send_ref[place, part] = lines_ref[pl.ds(pl.multiple_of(start, 8), 56), :]

        send_ref[place, 0, 48:56, :] = jnp.where(after, top, send_ref[place, 0, 48:56, :])


def block_kernel(
    velocity_ref, height_ref, coriolis_ref, elem_mass_ref, along_x_ref, tiles_ref, after_ref,
    partial_ref, node_mass, inner_inverse,
):
    lane = lane_index(128)
    step = pl.program_id(0)

    @pl.when(step == 0)
    def _():
        node_mass[...] = mass_of_nodes(elem_mass_ref[0], tiles_ref)
        local_mass = share_block(node_mass[...])
        row = lax.broadcasted_iota(jnp.int32, (128, 128), 0)
        inner = (row > 0) & (row < 127) & (lane > 0) & (lane < 127)
        inner_inverse[...] = jnp.where(inner, 1.0 / local_mass, 0.0)

    @pl.when(step < 8)
    def _():
        _, changed = changes(
            velocity_ref[0, 0], velocity_ref[1, 0], height_ref[0], coriolis_ref[0],
            node_mass[...], inner_inverse[...], share_block, along_x_ref, tiles_ref,
        )
        for part in range(3):
            partial_ref[part] = changed[part]

    @pl.when(step == 8)
    def _():
        partial_ref[0] = share_block(node_mass[...])


def pack_kernel(table_ref, received_ref, after_ref, ahead_ref, behind_ref, top_ref):
    top = jnp.zeros((8, 128), f32)
    for place in range(16):
        top = jnp.maximum(top, received_ref[2 * place, 48:56, :])
    top = jnp.max(jnp.where(lane_index(8) >= 96, top, 0.0), axis=(0, 1), keepdims=True)
    top_ref[...] = jnp.broadcast_to(top, top_ref.shape)
    for base, ref in ((48, ahead_ref), (51, behind_ref)):
        ref[0:56, :] = received_ref[2 * table_ref[0, base] + 1]
        ref[56:64, :] = received_ref[2 * table_ref[0, base + 1] + 1, 48:56, :]
        ref[64:72, :] = received_ref[2 * table_ref[0, base + 2] + 1, 48:56, :]


def edge_terms(table_ref, lines, received_ref, ahead_ref, behind_ref, tiles_ref):
    lane = lane_index(1)

    def message(way, start, stop):
        kind = table_ref[0, 40 + way]
        values = received_ref[table_ref[0, 32 + way], start:stop, :]
        step_y, step_x = steps8[way]
        if step_x != 0:
            crossed = ahead_ref if step_x > 0 else behind_ref
            shift = (0, 16, 8)[step_y]
            values = jnp.where(kind == 2, crossed[start + shift : stop + shift, :], values)
        return jnp.where(kind > 0, values, 0.0)

    own = [line[0:24, :] for line in lines]
    own_mass = [unfold_line(line[48:56, :]) for line in lines]
    near = [message(side, 0, 24) for side in range(4)]
    change = [message(side, 24, 48) for side in range(4)]
    extra = [message(side, 48, 56) for side in range(4)]
    mass = [unfold_line(extra[side]) for side in range(4)]
    shared_mass = [share_lanes(mass[side]) for side in range(4)]
    total = [own[side] + near[side] for side in range(4)]
    total_mass = [share_lanes(own_mass[side]) + shared_mass[side] for side in range(4)]
    corners = []
    for along in (UPPER, LOWER):
        for across in (RIGHT, LEFT):
            corner = 4 + 2 * (along - UPPER) + across
            at_x = 127 if across == RIGHT else 0
            at_y = 127 if along == UPPER else 0
            tile = message(corner, 48, 56)
            end_x = 0 if across == RIGHT else 3

            def spread_out(packed, start, at_x=at_x):
                return jnp.concatenate(
                    [turn(packed, at_x - start - 4 * part) for part in range(3)], 0
                )

            far = spread_out(tile, end_x)
            far_mass = turn(tile, at_x - 24 - end_x)[0:1]
            corners.append((along, across, at_x, at_y, tile, far_mass, spread_out))
            on_x, on_y = lane == at_x, lane == at_y
            total[along] = total[along] + jnp.where(
                on_x, turn(near[across], at_x - at_y) + far, 0.0
            )
            total_mass[along] = total_mass[along] + jnp.where(
                on_x, turn(mass[across], at_x - at_y) + far_mass, 0.0
            )
            total[across] = total[across] + jnp.where(
                on_y, turn(near[along] + far, at_y - at_x), 0.0
            )
            total_mass[across] = total_mass[across] + jnp.where(
                on_y, turn(mass[along] + far_mass, at_y - at_x), 0.0
            )
    smooth = [total[side] / total_mass[side] for side in range(4)]
    curve = [second_lanes(smooth[side], tiles_ref) for side in range(4)]
    added = [
        change[side]
        - hyper_coef
        * (shared_mass[side] * CENTRE * smooth[side] + share_lanes(mass[side] * curve[side]))
        for side in range(4)
    ]

    def arm(beside, diagonal, coefs):
        both = beside + diagonal
        weight = turn(both, -24)
        value = jnp.where(weight > 0.0, both / jnp.where(weight > 0.0, weight, 1.0), 0.0) * coefs
        value = value + turn(value, -1)
        return value + turn(value, -2)

    for along, across, at_x, at_y, tile, far_mass, spread_out in corners:
        beside = extra[across] if along == UPPER else turn(extra[across], -12)
        arm_x = spread_out(arm(beside, tile, tiles_ref[21 if across == RIGHT else 22]), 0)
        beside = extra[along] if across == LEFT else turn(extra[along], -12)
        arm_y = spread_out(
            arm(beside, turn(tile, -12), tiles_ref[21 if along == UPPER else 22]), 0
        )
        middle = CENTRE * smooth[along]
        arm_x, arm_y = arm_x + middle, arm_y + middle
        own_x = curve[along]
        own_y = turn(curve[across], at_x - at_y)
        mass_x = turn(mass[across], at_x - at_y)
        end_x = 0 if across == RIGHT else 3
        value = (
            turn(change[across], at_x - at_y) + change[along] + spread_out(tile, 48 + end_x)
        ) - hyper_coef * (
            mass_x * (arm_x + own_y) + mass[along] * (own_x + arm_y) + far_mass * (arm_x + arm_y)
        )
        added[along] = jnp.where(lane == at_x, value, added[along])
    ends = (lane == 0) | (lane == 127)
    plain, edge = [], []
    for side in range(4):
        line = smooth[side] if side >= UPPER else jnp.where(ends, 0.0, smooth[side])
        outside = added[side] if side >= UPPER else jnp.where(ends, 0.0, added[side])
        bend = curve[side] if side >= UPPER else second_lanes(line, tiles_ref)
        plain.append(share_lanes(own_mass[side] * line))
        edge.append(outside - hyper_coef * share_lanes(own_mass[side] * bend))
    return plain, edge, total_mass


def last_kernel(
    table_ref, lines_ref, received_ref, ahead_ref, behind_ref, tops_ref, tiles_ref, widen_ref,
    velocity_far, height_far, partial_far, new_velocity_far, new_height_far,
    rows, velocity_ref, height_ref, partial_ref, arrived, left_off,
):
    lane = lane_index(128)
    mass_in = pltpu.make_async_copy(partial_far.at[24], partial_ref.at[24], arrived.at[3, 0])
    mass_in.start()
    incoming = []
    for group in range(GROUPS):
        part = pl.ds(LEVELS_EACH * group, LEVELS_EACH)
        incoming.append(
            (
                pltpu.make_async_copy(
                    partial_far.at[pl.ds(3 * LEVELS_EACH * group, 3 * LEVELS_EACH)],
                    partial_ref.at[pl.ds(3 * LEVELS_EACH * group, 3 * LEVELS_EACH)],
                    arrived.at[0, group],
                ),
                pltpu.make_async_copy(
                    velocity_far.at[:, part], velocity_ref.at[:, part], arrived.at[1, group]
                ),
                pltpu.make_async_copy(
                    height_far.at[part], height_ref.at[part], arrived.at[2, group]
                ),
            )
        )
        for copy in incoming[-1]:
            copy.start()

    lines = [lines_ref.at[pl.ds(STARTS[side], 56)] for side in range(4)]
    plain, edge, total_mass = edge_terms(
        table_ref, lines, received_ref, ahead_ref, behind_ref, tiles_ref
    )
    rows[0] = plain[UPPER]
    rows[1] = plain[LOWER]
    rows[2] = edge[UPPER]
    rows[3] = edge[LOWER]
    stacked = jnp.concatenate(
        [plain[LEFT], plain[RIGHT], edge[LEFT], edge[RIGHT]]
        + [jnp.broadcast_to(total_mass[side], (16, 128)) for side in (LEFT, RIGHT)],
        0,
    )
    columns = jnp.transpose(stacked)
    mass_in.wait()
    mass = partial_ref[24]
    mass = jnp.where(lane == 0, columns[:, 96:97], mass)
    mass = jnp.where(lane == 127, columns[:, 112:113], mass)
    row = lax.broadcasted_iota(jnp.int32, (128, 128), 0)
    mass = jnp.where(row == 127, total_mass[UPPER], mass)
    mass = jnp.where(row == 0, total_mass[LOWER], mass)
    top = jnp.max(tops_ref[...], axis=(0, 1), keepdims=True)
    factor = (courant / top) / mass
    near_edge = (lane < 5) | (lane > 122)
    widened = product(columns, widen_ref[...])
    row = lax.broadcasted_iota(jnp.int32, (8, 128), 0)
    outgoing = []
    for group in range(GROUPS):
        for copy in incoming[group]:
            copy.wait()
        for level in range(LEVELS_EACH * group, LEVELS_EACH * (group + 1)):
            for part in range(3):
                at = 8 * part + level
                half = 128 * (at // 12)
                beside = turn(widened[:, half : half + 128], 123 - 10 * (at % 12))
                value = partial_ref[3 * level + part] + jnp.where(near_edge, beside, 0.0)
                upper = tiles_ref[23] * rows[0, at : at + 1, :]
                lower = tiles_ref[24] * rows[1, at : at + 1, :]
                upper = upper + jnp.where(row == 7, rows[2, at : at + 1, :], 0.0)
                lower = lower + jnp.where(row == 0, rows[3, at : at + 1, :], 0.0)
                value = jnp.concatenate([value[:8] + lower, value[8:120], value[120:] + upper], 0)
                if part < 2:
                    velocity_ref[part, level] = velocity_ref[part, level] + factor * value
                else:
                    height_ref[level] = height_ref[level] + factor * value
        part = pl.ds(LEVELS_EACH * group, LEVELS_EACH)
        for copy in (
            pltpu.make_async_copy(
                velocity_ref.at[:, part], new_velocity_far.at[:, part], left_off.at[0, group]
            ),
            pltpu.make_async_copy(
                height_ref.at[part], new_height_far.at[part], left_off.at[1, group]
            ),
        ):
            copy.start()
            outgoing.append(copy)
    for copy in outgoing:
        copy.wait()


def whole(shape, space=None):
    if space is None:
        return pl.BlockSpec(shape, lambda level: (0,) * len(shape))
    return pl.BlockSpec(memory_space=space)


def per_device(velocity, thickness, coriolis, elem_mass, block_owner):
    cols_b = block_owner.shape[1]
    count = 4 * cols_b
    velocity = velocity[:, :, 0]
    thickness = thickness[:, 0]
    widen, along_x, tiles = constant_tables()
    device = (lax.axis_index("elem") * lax.axis_size("sub") + lax.axis_index("sub")).reshape(1)
    if cols_b < 128:
        block_owner = jnp.pad(block_owner, ((0, 0), (0, 128 - cols_b)), constant_values=-1)
    shape = jax.ShapeDtypeStruct
    params = pltpu.CompilerParams(
        dimension_semantics=("arbitrary",), vmem_limit_bytes=BLOCK_VMEM
    )
    vmem = pltpu.VMEM
    far = pl.BlockSpec(memory_space=pltpu.HBM)
    held = pl.BlockSpec(memory_space=vmem)
    small = pl.BlockSpec(memory_space=pltpu.SMEM)
    arrays = (block_owner, velocity, thickness, coriolis, elem_mass, along_x, tiles)
    lines, send, table = pl.pallas_call(
        functools.partial(edge_kernel, cols_b),
        in_specs=[small] + [far] * 7,
        out_specs=[held] * 3,
        out_shape=[
            shape((256, 128), f32), shape((16, 2, 56, 128), f32), shape((1, 128), jnp.int32),
        ],
        scratch_shapes=[
            pltpu.VMEM((2, 3, 128, 128), f32), pltpu.VMEM((2, 3, 128, 128), f32),
            pltpu.VMEM(block_owner.shape, jnp.int32), pltpu.SMEM((1, 128), jnp.int32),
        ]
        + [pltpu.VMEM(array.shape, array.dtype) for array in arrays[1:]]
        + [pltpu.SemaphoreType.DMA((8,))],
        compiler_params=pltpu.CompilerParams(vmem_limit_bytes=EDGE_VMEM),
        name="edge",
    )(device, *arrays)
    squares = count // 16
    same_place = [[16 * s + i for s in range(squares)] for i in range(16)]
    same_square = [[16 * s + i for i in range(16)] for s in range(squares)]
    received = lax.all_to_all(
        send.reshape(16, 112, 128), axes, 0, 0, axis_index_groups=same_square, tiled=True
    ).reshape(32, 56, 128)
    pair = pl.BlockSpec((2, 1, 128, 128), lambda step: (0, jnp.minimum(step, 7), 0, 0))
    single = pl.BlockSpec((1, 128, 128), lambda step: (jnp.minimum(step, 7), 0, 0))
    partial = pl.pallas_call(
        block_kernel,
        grid=(9,),
        in_specs=[
            pair, single, whole((1, 128, 128)), whole((1, 32, 32)), whole((2, 384, 128)),
            whole((45, 8, 128)), whole((1, 8, 128)),
        ],
        out_specs=pl.BlockSpec((3, 128, 128), lambda step: (step, 0, 0)),
        out_shape=shape((27, 128, 128), f32),
        scratch_shapes=[pltpu.VMEM((128, 128), f32), pltpu.VMEM((128, 128), f32)],
        compiler_params=params,
        cost_estimate=pl.CostEstimate(
            flops=2_000_000_000, bytes_accessed=3_200_000, transcendentals=0
        ),
        name="block",
    )(velocity, thickness, coriolis, elem_mass, along_x, tiles, send.reshape(32, 56, 128))
    to_ahead, to_behind, top = pl.pallas_call(
        pack_kernel,
        grid=(1,),
        in_specs=[
            whole((1, 128), pltpu.SMEM), whole((32, 56, 128)),
            pl.BlockSpec((1, 8, 128), lambda step: (0, 0, 0)),
        ],
        out_specs=[
            whole((72, 128)), whole((72, 128)), whole((squares * TOP_ROWS, 128)),
        ],
        out_shape=[
            shape((72, 128), f32), shape((72, 128), f32), shape((squares * TOP_ROWS, 128), f32),
        ],
        compiler_params=pltpu.CompilerParams(vmem_limit_bytes=PACK_VMEM),
        name="pack",
    )(table, received, partial)
    tops = lax.all_to_all(top, axes, 0, 0, axis_index_groups=same_place, tiled=True)
    ahead = lax.ppermute(to_behind, axes, [(b, (b - 16) % count) for b in range(count)])
    behind = lax.ppermute(to_ahead, axes, [(b, (b + 16) % count) for b in range(count)])
    new_velocity, new_thickness = pl.pallas_call(
        last_kernel,
        in_specs=[small] + [held] * 7 + [far] * 3,
        out_specs=[far] * 2,
        out_shape=[shape((2, 8, 128, 128), f32), shape((8, 128, 128), f32)],
        scratch_shapes=[
            pltpu.VMEM((4, 24, 128), f32), pltpu.VMEM((2, 8, 128, 128), f32),
            pltpu.VMEM((8, 128, 128), f32), pltpu.VMEM((25, 128, 128), f32),
            pltpu.SemaphoreType.DMA((4, GROUPS)), pltpu.SemaphoreType.DMA((2, GROUPS)),
        ],
        compiler_params=pltpu.CompilerParams(vmem_limit_bytes=LAST_VMEM),
        name="last",
    )(table, lines, received, ahead, behind, tops, tiles, widen, velocity, thickness, partial)
    return new_velocity[:, :, None], new_thickness[:, None]


def solution(mesh):
    return jax.shard_map(
        per_device,
        mesh=mesh,
        in_specs=(
            P(None, None, axes, None, None),
            P(None, axes, None, None),
            P(axes, None, None),
            P(axes, None, None),
            P(),
        ),
        out_specs=(
            P(None, None, axes, None, None),
            P(None, axes, None, None),
        ),
        check_vma=False,
    )
```

```python
import functools
import math

import jax
import jax.numpy as jnp
import numpy as np
from jax import lax
from jax.experimental import pallas as pl
from jax.experimental.pallas import tpu as pltpu
from jax.sharding import PartitionSpec as P

courant = 0.1
hyper_coef = 0.002
TOP_ROWS = 8
MIB = 1024 * 1024
EDGE_VMEM = 60 * MIB
PACK_VMEM = 52 * MIB
BLOCK_VMEM = 60 * MIB
LAST_VMEM = 51 * MIB
GROUPS = 2
LEVELS_EACH = 8 // GROUPS
axes = ("elem", "sub")
f32 = jnp.float32
HIGH = lax.Precision.HIGHEST
RIGHT, LEFT, UPPER, LOWER = range(4)
STARTS = (0, 72, 144, 200, 8, 80, 16, 88)
steps8 = ((0, 1), (0, -1), (1, 0), (-1, 0), (1, 1), (1, -1), (-1, 1), (-1, -1))


def gll_tables():
    points = [-1.0, -1.0 / math.sqrt(5.0), 1.0 / math.sqrt(5.0), 1.0]
    weights = np.array([1.0 / 6.0, 5.0 / 6.0, 5.0 / 6.0, 1.0 / 6.0])
    spread = [
        math.prod([points[target] - points[others] for others in range(4) if others != target])
        for target in range(4)
    ]
    derivative = np.zeros((4, 4))
    for target in range(4):
        for source in range(4):
            if target == source:
                derivative[target, source] = sum(
                    1.0 / (points[target] - points[others]) for others in range(4) if others != target
                )
            else:
                derivative[target, source] = spread[target] / (
                    spread[source] * (points[target] - points[source])
                )
    return weights, 2.0 * derivative


WEIGHTS, FIRST = gll_tables()
SECOND = FIRST @ FIRST
CENTRE = float(SECOND[0, 0])


def offset_rows(table):
    rows = np.zeros((7, 4))
    for shift in range(-3, 4):
        for target in range(4):
            if 0 <= target + shift < 4:
                rows[shift + 3, target] = table[target, target + shift]
    return rows


def constant_tables():
    along_x = np.stack([np.kron(np.eye(32), FIRST.T), np.kron(np.eye(32), SECOND.T)])
    expand = np.kron(np.eye(32), WEIGHTS[:, None])
    tiles = np.zeros((25, 8, 128))
    expand_tiles = np.zeros((128, 128))
    expand_tiles[:, :32] = expand
    for base, table in ((0, FIRST), (7, SECOND)):
        tiles[base : base + 7] = np.tile(offset_rows(table), (1, 2))[:, :, None]
    tiles[14:21] = np.tile(offset_rows(SECOND), (1, 32))[:, None, :]
    arm_low = np.array([0.0, SECOND[0, 1], SECOND[0, 2], SECOND[0, 3]])
    arm_high = np.array([SECOND[3, 0], SECOND[3, 1], SECOND[3, 2], 0.0])
    tiles[21] = np.tile(arm_low, 32)[None]
    tiles[22] = np.tile(arm_high, 32)[None]
    high = np.array([-hyper_coef * WEIGHTS[a] / WEIGHTS[3] * SECOND[a, 3] for a in range(4)])
    low = np.array([-hyper_coef * WEIGHTS[a] / WEIGHTS[0] * SECOND[a, 0] for a in range(4)])
    tiles[23] = np.concatenate([[0.0, 0.0, 0.0, high[0]], high])[:, None]
    tiles[24] = np.concatenate([low, [low[3], 0.0, 0.0, 0.0]])[:, None]
    across = np.zeros(128)
    across[:5] = [*low, low[3]]
    across[123:] = [high[0], *high]
    widen = np.zeros((128, 256))
    for plane in range(24):
        start = 128 * (plane // 12) + 10 * (plane % 12)
        for lane in range(10):
            widen[24 * (lane < 5) + plane, start + lane] = across[(123 + lane) % 128]
        widen[72 + plane, start + 4] = 1.0
        widen[48 + plane, start + 5] = 1.0
    return (
        split_matrix(widen),
        split_matrix(along_x),
        jnp.asarray(
            np.concatenate([tiles, expand_tiles.reshape(16, 8, 128), expand.T.reshape(4, 8, 128)]), f32
        ),
    )


def lane_index(rows):
    return lax.broadcasted_iota(jnp.int32, (rows, 128), 1)


def turn(values, steps, axis=1):
    steps = steps % values.shape[axis]
    return values if steps == 0 else pltpu.roll(values, steps, axis)


def share_lanes(values):
    lane = lane_index(values.shape[0])
    first = (lane % 4 == 0) & (lane > 0)
    last = (lane % 4 == 3) & (lane < 127)
    return values + jnp.where(first, turn(values, 1), jnp.where(last, turn(values, 127), 0.0))


def share_rows(values):
    row = lax.broadcasted_iota(jnp.int32, values.shape, 0)
    first = (row % 4 == 0) & (row > 0)
    last = (row % 4 == 3) & (row < 127)
    return values + jnp.where(
        first, turn(values, 1, 0), jnp.where(last, turn(values, 127, 0), 0.0)
    )


def share_block(values):
    return share_rows(share_lanes(values))


def split_matrix(table):
    high = jnp.asarray(table, f32).astype(jnp.bfloat16)
    low = (jnp.asarray(table, f32) - high.astype(f32)).astype(jnp.bfloat16)
    return jnp.concatenate([high, high, low], -2)


def product(values, matrix):
    high = values.astype(jnp.bfloat16)
    low = (values - high.astype(f32)).astype(jnp.bfloat16)
    return jnp.dot(
        jnp.concatenate([high, low, high], 1), matrix, preferred_element_type=f32
    )


def along_rows(values, tiles_ref, base):
    grouped = values.reshape(16, 8, 128)
    total = grouped * tiles_ref[base + 3][None]
    for shift in (-3, -2, -1, 1, 2, 3):
        total = total + pltpu.roll(grouped, (-shift) % 8, 1) * tiles_ref[base + 3 + shift][None]
    return total.reshape(128, 128)


def second_lanes(values, tiles_ref):
    total = values * tiles_ref[17, 0:1]
    for shift in (-3, -2, -1, 1, 2, 3):
        total = total + turn(values, -shift) * tiles_ref[17 + shift, 0:1]
    return total


def pack_end(lines, at_high):
    lane = lane_index(8)
    start = 124 if at_high else 0
    packed = jnp.zeros((8, 128), f32)
    for part in range(3):
        moved = turn(lines[8 * part : 8 * part + 8], 4 * part - start)
        packed = jnp.where(lane // 4 == part, moved, packed)
    return packed


def pack_mass(line, at_high):
    lane = lane_index(8)
    start = 124 if at_high else 0
    wide = jnp.broadcast_to(line, (8, 128))
    packed = jnp.zeros((8, 128), f32)
    for part in range(3):
        packed = jnp.where(lane // 4 == 6 + part, turn(wide, 24 + 4 * part - start), packed)
    return packed


def fold_line(line):
    lane = lane_index(8)
    row = lax.broadcasted_iota(jnp.int32, (8, 128), 0)
    wide = jnp.broadcast_to(line, (8, 128))
    folded = jnp.zeros((8, 128), f32)
    for part in range(8):
        folded = jnp.where((row == part) & (lane // 16 == 3), turn(wide, 48 - 16 * part), folded)
    return folded


def unfold_line(tile):
    lane = lane_index(8)
    row = lax.broadcasted_iota(jnp.int32, (8, 128), 0)
    moved = pltpu.roll(turn(tile, -48), 0, 1, stride=16, stride_axis=0)
    return jnp.sum(jnp.where(lane // 16 == row, moved, 0.0), axis=0, keepdims=True)


def top_lanes():
    lane = lane_index(8)
    row = lax.broadcasted_iota(jnp.int32, (8, 128), 0)
    return (row == 7) & (lane >= 24) & (lane < 48)


def mass_of_nodes(elem_mass, tiles_ref):
    wide = tiles_ref[25:41].reshape(128, 128)[:, :32]
    rows = jnp.dot(wide, elem_mass, precision=HIGH, preferred_element_type=f32)
    return jnp.dot(
        rows, tiles_ref[41:45].reshape(32, 128), precision=HIGH, preferred_element_type=f32
    )


def find_tables(device, owner_ref, table_ref, cols_b):
    square = device // 16
    squares = cols_b // 4
    place = jnp.zeros((48, 128), f32)
    index = lax.broadcasted_iota(jnp.int32, (48, 1), 0)
    wanted = ((square + index // 16 + squares - 1) % squares) * 16 + index % 16
    lane = lane_index(1)
    own = jnp.zeros((1, 128), f32)
    for row in range(4):
        line = owner_ref[row : row + 1, :]
        code = (128 * row + lane).astype(f32)
        place = place + jnp.where(line == wanted, code, 0.0)
        own = own + jnp.where(line == device, code, 0.0)
    place = jnp.sum(place, axis=1, keepdims=True).astype(jnp.int32)
    own = jnp.sum(own, axis=1, keepdims=True).astype(jnp.int32)
    own_row, own_col = own // 128, own % 128
    rows, cols = place // 128, place % 128
    member = device % 16
    here_rows, here_cols = rows[16:32], cols[16:32]
    down, over = here_rows - own_row, here_cols - own_col
    inside = jnp.full((16, 1), -1, jnp.int32)
    for start, (step_y, step_x) in zip(STARTS, steps8):
        inside = jnp.where((down == step_y) & (over == step_x), start, inside)
    crossing = jnp.full((16, 1), -1, jnp.int32)
    sixteen = lax.broadcasted_iota(jnp.int32, (16, 1), 0)
    sources = []
    for side, begin, step_x in ((RIGHT, 32, 1), (LEFT, 0, -1)):
        there_rows, there_cols = rows[begin : begin + 16], cols[begin : begin + 16]
        beside = there_cols == (own_col + step_x + cols_b) % cols_b
        picked = sixteen == member
        their = jnp.sum(
            jnp.where(picked, place[begin : begin + 16], 0).astype(f32), axis=0, keepdims=True
        ).astype(jnp.int32)
        their_row, their_col = their // 128, their % 128
        facing = here_cols == (their_col - step_x + cols_b) % cols_b
        for number, step_y in enumerate((0, 1, -1)):
            start = STARTS[side] if step_y == 0 else STARTS[side] + 8 * number
            crossing = jnp.where(beside & (there_rows - own_row == step_y), start, crossing)
            found = facing & (their_row - here_rows == step_y)
            sources.append(
                jnp.sum(jnp.where(found, sixteen, 0).astype(f32), axis=0, keepdims=True).astype(
                    jnp.int32
                )
            )
    way = lax.broadcasted_iota(jnp.int32, (8, 1), 0)
    step_y = jnp.zeros((8, 1), jnp.int32)
    step_x = jnp.zeros((8, 1), jnp.int32)
    for number, (along_y, along_x) in enumerate(steps8):
        step_y = jnp.where(way == number, along_y, step_y)
        step_x = jnp.where(way == number, along_x, step_x)
    near_row = own_row + step_y
    near_col = (own_col + step_x + cols_b) % cols_b
    found = jnp.zeros((8, 128), f32)
    for row in range(4):
        line = owner_ref[row : row + 1, :].astype(f32)
        found = found + jnp.where((near_row == row) & (near_col == lane), line, 0.0)
    found = jnp.sum(found, axis=1, keepdims=True).astype(jnp.int32)
    there = (near_row >= 0) & (near_row < 4)
    slot = found % 16
    kind = jnp.where(there, jnp.where(found // 16 == square, 1, 2), 0)
    ahead_of = jnp.where(way == 0, sources[0], 0)
    for number in range(1, 6):
        ahead_of = jnp.where(way == number, sources[number], ahead_of)
    column = jnp.concatenate([inside, crossing, slot, kind, ahead_of], 0).astype(f32)
    picked = lax.broadcasted_iota(jnp.int32, (56, 128), 0) == lane_index(56)
    table_ref[...] = jnp.sum(jnp.where(picked, column, 0.0), axis=0, keepdims=True).astype(
        jnp.int32
    )


def share_band(values):
    across = share_lanes(values).reshape(16, 8, 128)
    row = lax.broadcasted_iota(jnp.int32, (1, 8, 128), 1)
    above = pltpu.roll(across, 1, 1)
    below = pltpu.roll(across, 7, 1)
    shared = across + jnp.where(row == 4, above, jnp.where(row == 3, below, 0.0))
    return shared.reshape(128, 128)


def changes(east, north, height, coriolis, mass, inverse, share, along_x_ref, tiles_ref):
    energy = 0.5 * (east * east + north * north) + height
    flux_x, flux_y = height * east, height * north
    first_x = product(jnp.concatenate([north, energy, flux_x], 0), along_x_ref[0])
    second_x = product(jnp.concatenate([east, north, height], 0), along_x_ref[1])
    absolute = first_x[:128] - along_rows(east, tiles_ref, 0) + coriolis
    tendencies = (
        absolute * north - first_x[128:256],
        -absolute * east - along_rows(energy, tiles_ref, 0),
        -(first_x[256:] + along_rows(flux_y, tiles_ref, 0)),
    )
    locals_, smoothed = [], []
    for part, values in enumerate((east, north, height)):
        lap = second_x[128 * part : 128 * part + 128] + along_rows(values, tiles_ref, 7)
        local = share(lap * mass)
        locals_.append(local)
        smoothed.append(local * inverse)
    second_x = product(jnp.concatenate(smoothed, 0), along_x_ref[1])
    changed = []
    for part in range(3):
        lap = second_x[128 * part : 128 * part + 128] + along_rows(smoothed[part], tiles_ref, 7)
        changed.append(share((tendencies[part] - hyper_coef * lap) * mass))
    return locals_, changed


def edge_kernel(
    cols_b, device_ref, owner_far,
    velocity_far, height_far, coriolis_far, elem_mass_far, along_x_far, tiles_far,
    lines_ref, send_ref, table_ref,
    smooth, change, owner_ref, near_ref, velocity_ref, height_ref, coriolis_ref, elem_mass_ref,
    along_x_ref, tiles_ref, arrived,
):
    far = (
        owner_far, elem_mass_far, tiles_far, height_far, velocity_far, coriolis_far, along_x_far,
    )
    near = (
        owner_ref, elem_mass_ref, tiles_ref, height_ref, velocity_ref, coriolis_ref, along_x_ref,
    )
    copies = [
        pltpu.make_async_copy(far[k], near[k], arrived.at[k]) for k in range(len(far))
    ]
    for copy in copies:
        copy.start()
    lane = lane_index(128)
    copies[0].wait()
    find_tables(device_ref[0], owner_ref, table_ref, cols_b)
    table_copy = pltpu.make_async_copy(table_ref, near_ref, arrived.at[7])
    table_copy.start()
    copies[1].wait()
    copies[2].wait()
    mass = mass_of_nodes(elem_mass_ref[0], tiles_ref)
    mass_t = jnp.transpose(mass)
    for copy in copies[3:]:
        copy.wait()
    coriolis = coriolis_ref[0]

    def upright_band(ref_value):
        return jnp.concatenate([ref_value[120:128], ref_value[0:8]], 0)

    def upright_plane(read):
        return jnp.concatenate(
            [piece for level in range(8) for piece in (read(level, 120), read(level, 0))], 0
        )

    def sideways_plane(read):
        packed = jnp.zeros((128, 128), f32)
        for level in range(8):
            packed = jnp.where(lane // 16 == level, turn(read(level), 8 + 16 * level), packed)
        return jnp.transpose(packed)

    def repeat(band):
        return jnp.concatenate([band] * 8, 0)

    row = lax.broadcasted_iota(jnp.int32, (128, 128), 0) % 16
    inner = (row != 7) & (row != 8) & (lane > 0) & (lane < 127)
    for way in range(2):
        if way == 0:
            planes = [
                upright_plane(lambda level, at, c=c: velocity_ref[c, level, at : at + 8, :])
                for c in range(2)
            ] + [upright_plane(lambda level, at: height_ref[level, at : at + 8, :])]
            turning = repeat(upright_band(coriolis))
            band_mass = repeat(upright_band(mass))
        else:
            top = jnp.zeros((128, 128), f32)
            for level in range(8):
                east, north = velocity_ref[0, level], velocity_ref[1, level]
                top = jnp.maximum(
                    top, jnp.sqrt(east * east + north * north) + jnp.sqrt(height_ref[level])
                )
            top = jnp.max(top, axis=(0, 1), keepdims=True)
            planes = [
                sideways_plane(lambda level, c=c: velocity_ref[c, level]) for c in (1, 0)
            ] + [sideways_plane(lambda level: height_ref[level])]
            turning = -sideways_plane(lambda level: coriolis)
            band_mass = repeat(upright_band(mass_t))
        inverse = jnp.where(inner, 1.0 / share_band(band_mass), 0.0)
        locals_, changed = changes(
            *planes, turning, band_mass, inverse, share_band, along_x_ref, tiles_ref
        )
        for part in range(3):
            target = part if way == 0 or part == 2 else 1 - part
            smooth[way, target] = locals_[part]
            change[way, target] = changed[part]

    sizes = (72, 72, 56, 56)
    targets = [lines_ref.at[pl.ds(STARTS[side], sizes[side])] for side in range(4)]
    for way in range(2):
        for end in range(2):
            target = targets[2 * (1 - way) + end]
            for part in range(3):
                place = pl.ds(7 + end, 8, stride=16)
                target[8 * part : 8 * part + 8, :] = smooth.at[way, part][place, :]
                target[24 + 8 * part : 32 + 8 * part, :] = change.at[way, part][place, :]
    mass_lines = (mass_t[127:128], mass_t[0:1], mass[127:128], mass[0:1])
    lines = [targets[side][0:48, :] for side in range(4)]
    ends = {}
    for side in range(4):
        local_mass = share_lanes(mass_lines[side])
        for high in (False, True):
            ends[side, high] = pack_end(lines[side][0:24], high) + pack_mass(local_mass, high)
    extras = (
        ends[UPPER, True] + turn(ends[LOWER, True], 12),
        ends[UPPER, False] + turn(ends[LOWER, False], 12),
        ends[LEFT, True] + turn(ends[RIGHT, True], 12),
        ends[LEFT, False] + turn(ends[RIGHT, False], 12),
    )
    for side in range(4):
        targets[side][48:56, :] = extras[side] + fold_line(mass_lines[side])
    for number, (along, upward) in enumerate(((UPPER, True), (LOWER, False))):
        for across, sideways in ((RIGHT, True), (LEFT, False)):
            tile = ends[along, sideways] + turn(ends[across, upward], 12)
            tile = tile + turn(pack_end(lines[along][24:48], sideways), 48)
            targets[across][56 + 8 * number : 64 + 8 * number, :] = tile
    table_copy.wait()
    starts = [
        [pl.multiple_of(jnp.maximum(near_ref[0, 16 * part + place], 0), 8) for part in range(2)]
        for place in range(16)
    ]
    for place in range(16):
        for part in range(2):
            rows = pl.ds(starts[place][part], 48)
            send_ref[place, 48 * part : 48 * part + 48, :] = lines_ref[rows, :]
    for place in range(16):
        tiles = [lines_ref[pl.ds(starts[place][part] + 48, 8), :] for part in range(2)]
        tile = jnp.where(lane_index(8) < 64, tiles[0], turn(tiles[1], 64))
        send_ref[place, 96:104, :] = jnp.where(top_lanes(), top, tile)


def block_kernel(
    velocity_ref, height_ref, coriolis_ref, elem_mass_ref, along_x_ref, tiles_ref, after_ref,
    partial_ref, node_mass, inner_inverse,
):
    lane = lane_index(128)
    step = pl.program_id(0)

    @pl.when(step == 0)
    def _():
        node_mass[...] = mass_of_nodes(elem_mass_ref[0], tiles_ref)
        local_mass = share_block(node_mass[...])
        row = lax.broadcasted_iota(jnp.int32, (128, 128), 0)
        inner = (row > 0) & (row < 127) & (lane > 0) & (lane < 127)
        inner_inverse[...] = jnp.where(inner, 1.0 / local_mass, 0.0)

    @pl.when(step < 8)
    def _():
        _, changed = changes(
            velocity_ref[0, 0], velocity_ref[1, 0], height_ref[0], coriolis_ref[0],
            node_mass[...], inner_inverse[...], share_block, along_x_ref, tiles_ref,
        )
        for part in range(3):
            partial_ref[part] = changed[part]

    @pl.when(step == 8)
    def _():
        partial_ref[0] = share_block(node_mass[...])


def pack_kernel(table_ref, received_ref, after_ref, ahead_ref, behind_ref, top_ref):
    top = jnp.zeros((8, 128), f32)
    for place in range(16):
        top = jnp.maximum(top, received_ref[place, 96:104, :])
    top = jnp.max(jnp.where(top_lanes(), top, 0.0), axis=(0, 1), keepdims=True)
    top_ref[...] = jnp.broadcast_to(top, top_ref.shape)
    for base, ref in ((48, ahead_ref), (51, behind_ref)):
        ref[0:48, :] = received_ref[table_ref[0, base], 48:96, :]
        for number in range(3):
            tile = received_ref[table_ref[0, base + number], 96:104, :]
            ref[48 + 8 * number : 56 + 8 * number, :] = turn(tile, 64)


def edge_terms(table_ref, lines, received_ref, ahead_ref, behind_ref, tiles_ref):
    lane = lane_index(1)

    def message(way, start, stop):
        kind = table_ref[0, 40 + way]
        skip = 48 if start == 48 else 0
        values = received_ref[table_ref[0, 32 + way], start + skip : stop + skip, :]
        step_y, step_x = steps8[way]
        if step_x != 0:
            crossed = ahead_ref if step_x > 0 else behind_ref
            shift = (0, 16, 8)[step_y]
            values = jnp.where(kind == 2, crossed[start + shift : stop + shift, :], values)
        return jnp.where(kind > 0, values, 0.0)

    own = [line[0:24, :] for line in lines]
    own_mass = [unfold_line(line[48:56, :]) for line in lines]
    near = [message(side, 0, 24) for side in range(4)]
    change = [message(side, 24, 48) for side in range(4)]
    extra = [message(side, 48, 56) for side in range(4)]
    mass = [unfold_line(extra[side]) for side in range(4)]
    shared_mass = [share_lanes(mass[side]) for side in range(4)]
    total = [own[side] + near[side] for side in range(4)]
    total_mass = [share_lanes(own_mass[side]) + shared_mass[side] for side in range(4)]
    corners = []
    for along in (UPPER, LOWER):
        for across in (RIGHT, LEFT):
            corner = 4 + 2 * (along - UPPER) + across
            at_x = 127 if across == RIGHT else 0
            at_y = 127 if along == UPPER else 0
            tile = message(corner, 48, 56)
            end_x = 0 if across == RIGHT else 3

            def spread_out(packed, start, at_x=at_x):
                return jnp.concatenate(
                    [turn(packed, at_x - start - 4 * part) for part in range(3)], 0
                )

            far = spread_out(tile, end_x)
            far_mass = turn(tile, at_x - 24 - end_x)[0:1]
            corners.append((along, across, at_x, at_y, tile, far_mass, spread_out))
            on_x, on_y = lane == at_x, lane == at_y
            total[along] = total[along] + jnp.where(
                on_x, turn(near[across], at_x - at_y) + far, 0.0
            )
            total_mass[along] = total_mass[along] + jnp.where(
                on_x, turn(mass[across], at_x - at_y) + far_mass, 0.0
            )
            total[across] = total[across] + jnp.where(
                on_y, turn(near[along] + far, at_y - at_x), 0.0
            )
            total_mass[across] = total_mass[across] + jnp.where(
                on_y, turn(mass[along] + far_mass, at_y - at_x), 0.0
            )
    smooth = [total[side] / total_mass[side] for side in range(4)]
    curve = [second_lanes(smooth[side], tiles_ref) for side in range(4)]
    added = [
        change[side]
        - hyper_coef
        * (shared_mass[side] * CENTRE * smooth[side] + share_lanes(mass[side] * curve[side]))
        for side in range(4)
    ]

    def arm(beside, diagonal, coefs):
        both = beside + diagonal
        weight = jnp.broadcast_to(turn(both, -24)[0:1], (8, 128))
        value = jnp.where(weight > 0.0, both / jnp.where(weight > 0.0, weight, 1.0), 0.0) * coefs
        value = value + turn(value, -1)
        return value + turn(value, -2)

    for along, across, at_x, at_y, tile, far_mass, spread_out in corners:
        beside = extra[across] if along == UPPER else turn(extra[across], -12)
        arm_x = spread_out(arm(beside, tile, tiles_ref[21 if across == RIGHT else 22]), 0)
        beside = extra[along] if across == LEFT else turn(extra[along], -12)
        arm_y = spread_out(
            arm(beside, turn(tile, -12), tiles_ref[21 if along == UPPER else 22]), 0
        )
        middle = CENTRE * smooth[along]
        arm_x, arm_y = arm_x + middle, arm_y + middle
        own_x = curve[along]
        own_y = turn(curve[across], at_x - at_y)
        mass_x = turn(mass[across], at_x - at_y)
        end_x = 0 if across == RIGHT else 3
        value = (
            turn(change[across], at_x - at_y) + change[along] + spread_out(tile, 48 + end_x)
        ) - hyper_coef * (
            mass_x * (arm_x + own_y) + mass[along] * (own_x + arm_y) + far_mass * (arm_x + arm_y)
        )
        added[along] = jnp.where(lane == at_x, value, added[along])
    ends = (lane == 0) | (lane == 127)
    plain, edge = [], []
    for side in range(4):
        line = smooth[side] if side >= UPPER else jnp.where(ends, 0.0, smooth[side])
        outside = added[side] if side >= UPPER else jnp.where(ends, 0.0, added[side])
        bend = curve[side] if side >= UPPER else second_lanes(line, tiles_ref)
        plain.append(share_lanes(own_mass[side] * line))
        edge.append(outside - hyper_coef * share_lanes(own_mass[side] * bend))
    return plain, edge, total_mass


def last_kernel(
    table_ref, lines_ref, received_ref, ahead_ref, behind_ref, tops_ref, tiles_ref, widen_ref,
    velocity_far, height_far, partial_far, new_velocity_far, new_height_far,
    rows, velocity_ref, height_ref, partial_ref, arrived, left_off,
):
    lane = lane_index(128)
    mass_in = pltpu.make_async_copy(partial_far.at[24], partial_ref.at[24], arrived.at[3, 0])
    mass_in.start()
    incoming = []
    for group in range(GROUPS):
        part = pl.ds(LEVELS_EACH * group, LEVELS_EACH)
        incoming.append(
            (
                pltpu.make_async_copy(
                    partial_far.at[pl.ds(3 * LEVELS_EACH * group, 3 * LEVELS_EACH)],
                    partial_ref.at[pl.ds(3 * LEVELS_EACH * group, 3 * LEVELS_EACH)],
                    arrived.at[0, group],
                ),
                pltpu.make_async_copy(
                    velocity_far.at[:, part], velocity_ref.at[:, part], arrived.at[1, group]
                ),
                pltpu.make_async_copy(
                    height_far.at[part], height_ref.at[part], arrived.at[2, group]
                ),
            )
        )
        for copy in incoming[-1]:
            copy.start()

    lines = [lines_ref.at[pl.ds(STARTS[side], 56)] for side in range(4)]
    plain, edge, total_mass = edge_terms(
        table_ref, lines, received_ref, ahead_ref, behind_ref, tiles_ref
    )
    rows[0] = plain[UPPER]
    rows[1] = plain[LOWER]
    rows[2] = edge[UPPER]
    rows[3] = edge[LOWER]
    stacked = jnp.concatenate(
        [plain[LEFT], plain[RIGHT], edge[LEFT], edge[RIGHT]]
        + [jnp.broadcast_to(total_mass[side], (16, 128)) for side in (LEFT, RIGHT)],
        0,
    )
    columns = jnp.transpose(stacked)
    mass_in.wait()
    mass = partial_ref[24]
    mass = jnp.where(lane == 0, columns[:, 96:97], mass)
    mass = jnp.where(lane == 127, columns[:, 112:113], mass)
    row = lax.broadcasted_iota(jnp.int32, (128, 128), 0)
    mass = jnp.where(row == 127, total_mass[UPPER], mass)
    mass = jnp.where(row == 0, total_mass[LOWER], mass)
    top = jnp.max(tops_ref[...], axis=(0, 1), keepdims=True)
    factor = (courant / top) / mass
    near_edge = (lane < 5) | (lane > 122)
    widened = product(columns, widen_ref[...])
    row = lax.broadcasted_iota(jnp.int32, (8, 128), 0)
    outgoing = []
    for group in range(GROUPS):
        for copy in incoming[group]:
            copy.wait()
        for level in range(LEVELS_EACH * group, LEVELS_EACH * (group + 1)):
            for part in range(3):
                at = 8 * part + level
                half = 128 * (at // 12)
                beside = turn(widened[:, half : half + 128], 123 - 10 * (at % 12))
                value = partial_ref[3 * level + part] + jnp.where(near_edge, beside, 0.0)
                upper = tiles_ref[23] * rows[0, at : at + 1, :]
                lower = tiles_ref[24] * rows[1, at : at + 1, :]
                upper = upper + jnp.where(row == 7, rows[2, at : at + 1, :], 0.0)
                lower = lower + jnp.where(row == 0, rows[3, at : at + 1, :], 0.0)
                value = jnp.concatenate([value[:8] + lower, value[8:120], value[120:] + upper], 0)
                if part < 2:
                    velocity_ref[part, level] = velocity_ref[part, level] + factor * value
                else:
                    height_ref[level] = height_ref[level] + factor * value
        part = pl.ds(LEVELS_EACH * group, LEVELS_EACH)
        for copy in (
            pltpu.make_async_copy(
                velocity_ref.at[:, part], new_velocity_far.at[:, part], left_off.at[0, group]
            ),
            pltpu.make_async_copy(
                height_ref.at[part], new_height_far.at[part], left_off.at[1, group]
            ),
        ):
            copy.start()
            outgoing.append(copy)
    for copy in outgoing:
        copy.wait()


def whole(shape, space=None):
    if space is None:
        return pl.BlockSpec(shape, lambda level: (0,) * len(shape))
    return pl.BlockSpec(memory_space=space)


def per_device(velocity, thickness, coriolis, elem_mass, block_owner):
    cols_b = block_owner.shape[1]
    count = 4 * cols_b
    velocity = velocity[:, :, 0]
    thickness = thickness[:, 0]
    widen, along_x, tiles = constant_tables()
    device = (lax.axis_index("elem") * lax.axis_size("sub") + lax.axis_index("sub")).reshape(1)
    if cols_b < 128:
        block_owner = jnp.pad(block_owner, ((0, 0), (0, 128 - cols_b)), constant_values=-1)
    shape = jax.ShapeDtypeStruct
    params = pltpu.CompilerParams(
        dimension_semantics=("arbitrary",), vmem_limit_bytes=BLOCK_VMEM
    )
    vmem = pltpu.VMEM
    far = pl.BlockSpec(memory_space=pltpu.HBM)
    held = pl.BlockSpec(memory_space=vmem)
    small = pl.BlockSpec(memory_space=pltpu.SMEM)
    arrays = (block_owner, velocity, thickness, coriolis, elem_mass, along_x, tiles)
    lines, send, table = pl.pallas_call(
        functools.partial(edge_kernel, cols_b),
        in_specs=[small] + [far] * 7,
        out_specs=[held] * 3,
        out_shape=[
            shape((256, 128), f32), shape((16, 104, 128), f32), shape((1, 128), jnp.int32),
        ],
        scratch_shapes=[
            pltpu.VMEM((2, 3, 128, 128), f32), pltpu.VMEM((2, 3, 128, 128), f32),
            pltpu.VMEM(block_owner.shape, jnp.int32), pltpu.SMEM((1, 128), jnp.int32),
        ]
        + [pltpu.VMEM(array.shape, array.dtype) for array in arrays[1:]]
        + [pltpu.SemaphoreType.DMA((8,))],
        compiler_params=pltpu.CompilerParams(vmem_limit_bytes=EDGE_VMEM),
        name="edge",
    )(device, *arrays)
    squares = count // 16
    same_place = [[16 * s + i for s in range(squares)] for i in range(16)]
    same_square = [[16 * s + i for i in range(16)] for s in range(squares)]
    received = lax.all_to_all(
        send, axes, 0, 0, axis_index_groups=same_square, tiled=True
    )
    pair = pl.BlockSpec((2, 1, 128, 128), lambda step: (0, jnp.minimum(step, 7), 0, 0))
    single = pl.BlockSpec((1, 128, 128), lambda step: (jnp.minimum(step, 7), 0, 0))
    partial = pl.pallas_call(
        block_kernel,
        grid=(9,),
        in_specs=[
            pair, single, whole((1, 128, 128)), whole((1, 32, 32)), whole((2, 384, 128)),
            whole((45, 8, 128)), whole((1, 8, 128)),
        ],
        out_specs=pl.BlockSpec((3, 128, 128), lambda step: (step, 0, 0)),
        out_shape=shape((27, 128, 128), f32),
        scratch_shapes=[pltpu.VMEM((128, 128), f32), pltpu.VMEM((128, 128), f32)],
        compiler_params=params,
        cost_estimate=pl.CostEstimate(
            flops=2_000_000_000, bytes_accessed=3_200_000, transcendentals=0
        ),
        name="block",
    )(velocity, thickness, coriolis, elem_mass, along_x, tiles, send)
    to_ahead, to_behind, top = pl.pallas_call(
        pack_kernel,
        grid=(1,),
        in_specs=[
            whole((1, 128), pltpu.SMEM), whole((16, 104, 128)),
            pl.BlockSpec((1, 8, 128), lambda step: (0, 0, 0)),
        ],
        out_specs=[
            whole((72, 128)), whole((72, 128)), whole((squares * TOP_ROWS, 128)),
        ],
        out_shape=[
            shape((72, 128), f32), shape((72, 128), f32), shape((squares * TOP_ROWS, 128), f32),
        ],
        compiler_params=pltpu.CompilerParams(vmem_limit_bytes=PACK_VMEM),
        name="pack",
    )(table, received, partial)
    tops = lax.all_to_all(top, axes, 0, 0, axis_index_groups=same_place, tiled=True)
    ahead = lax.ppermute(to_behind, axes, [(b, (b - 16) % count) for b in range(count)])
    behind = lax.ppermute(to_ahead, axes, [(b, (b + 16) % count) for b in range(count)])
    new_velocity, new_thickness = pl.pallas_call(
        last_kernel,
        in_specs=[small] + [held] * 7 + [far] * 3,
        out_specs=[far] * 2,
        out_shape=[shape((2, 8, 128, 128), f32), shape((8, 128, 128), f32)],
        scratch_shapes=[
            pltpu.VMEM((4, 24, 128), f32), pltpu.VMEM((2, 8, 128, 128), f32),
            pltpu.VMEM((8, 128, 128), f32), pltpu.VMEM((25, 128, 128), f32),
            pltpu.SemaphoreType.DMA((4, GROUPS)), pltpu.SemaphoreType.DMA((2, GROUPS)),
        ],
        compiler_params=pltpu.CompilerParams(vmem_limit_bytes=LAST_VMEM),
        name="last",
    )(table, lines, received, ahead, behind, tops, tiles, widen, velocity, thickness, partial)
    return new_velocity[:, :, None], new_thickness[:, None]


def solution(mesh):
    return jax.shard_map(
        per_device,
        mesh=mesh,
        in_specs=(
            P(None, None, axes, None, None),
            P(None, axes, None, None),
            P(axes, None, None),
            P(axes, None, None),
            P(),
        ),
        out_specs=(
            P(None, None, axes, None, None),
            P(None, axes, None, None),
        ),
        check_vma=False,
    )
```

```python
import functools
import math

import jax
import jax.numpy as jnp
import numpy as np
from jax import lax
from jax.experimental import pallas as pl
from jax.experimental.pallas import tpu as pltpu
from jax.sharding import PartitionSpec as P

courant = 0.1
hyper_coef = 0.002
TOP_ROWS = 3
MIB = 1024 * 1024
EDGE_VMEM = 60 * MIB
PACK_VMEM = 52 * MIB
BLOCK_VMEM = 60 * MIB
LAST_VMEM = 51 * MIB
GROUPS = 2
LEVELS_EACH = 8 // GROUPS
axes = ("elem", "sub")
f32 = jnp.float32
HIGH = lax.Precision.HIGHEST
RIGHT, LEFT, UPPER, LOWER = range(4)
STARTS = (0, 72, 144, 200, 8, 80, 16, 88)
steps8 = ((0, 1), (0, -1), (1, 0), (-1, 0), (1, 1), (1, -1), (-1, 1), (-1, -1))


def gll_tables():
    points = [-1.0, -1.0 / math.sqrt(5.0), 1.0 / math.sqrt(5.0), 1.0]
    weights = np.array([1.0 / 6.0, 5.0 / 6.0, 5.0 / 6.0, 1.0 / 6.0])
    spread = [
        math.prod([points[target] - points[others] for others in range(4) if others != target])
        for target in range(4)
    ]
    derivative = np.zeros((4, 4))
    for target in range(4):
        for source in range(4):
            if target == source:
                derivative[target, source] = sum(
                    1.0 / (points[target] - points[others]) for others in range(4) if others != target
                )
            else:
                derivative[target, source] = spread[target] / (
                    spread[source] * (points[target] - points[source])
                )
    return weights, 2.0 * derivative


WEIGHTS, FIRST = gll_tables()
SECOND = FIRST @ FIRST
CENTRE = float(SECOND[0, 0])


def offset_rows(table):
    rows = np.zeros((7, 4))
    for shift in range(-3, 4):
        for target in range(4):
            if 0 <= target + shift < 4:
                rows[shift + 3, target] = table[target, target + shift]
    return rows


def constant_tables():
    along_x = np.stack([np.kron(np.eye(32), FIRST.T), np.kron(np.eye(32), SECOND.T)])
    expand = np.kron(np.eye(32), WEIGHTS[:, None])
    tiles = np.zeros((25, 8, 128))
    expand_tiles = np.zeros((128, 128))
    expand_tiles[:, :32] = expand
    for base, table in ((0, FIRST), (7, SECOND)):
        tiles[base : base + 7] = np.tile(offset_rows(table), (1, 2))[:, :, None]
    tiles[14:21] = np.tile(offset_rows(SECOND), (1, 32))[:, None, :]
    arm_low = np.array([0.0, SECOND[0, 1], SECOND[0, 2], SECOND[0, 3]])
    arm_high = np.array([SECOND[3, 0], SECOND[3, 1], SECOND[3, 2], 0.0])
    tiles[21] = np.tile(arm_low, 32)[None]
    tiles[22] = np.tile(arm_high, 32)[None]
    high = np.array([-hyper_coef * WEIGHTS[a] / WEIGHTS[3] * SECOND[a, 3] for a in range(4)])
    low = np.array([-hyper_coef * WEIGHTS[a] / WEIGHTS[0] * SECOND[a, 0] for a in range(4)])
    tiles[23] = np.concatenate([[0.0, 0.0, 0.0, high[0]], high])[:, None]
    tiles[24] = np.concatenate([low, [low[3], 0.0, 0.0, 0.0]])[:, None]
    across = np.zeros(128)
    across[:5] = [*low, low[3]]
    across[123:] = [high[0], *high]
    widen = np.zeros((128, 256))
    for plane in range(24):
        start = 128 * (plane // 12) + 10 * (plane % 12)
        for lane in range(10):
            widen[24 * (lane < 5) + plane, start + lane] = across[(123 + lane) % 128]
        widen[72 + plane, start + 4] = 1.0
        widen[48 + plane, start + 5] = 1.0
    return (
        split_matrix(widen),
        split_matrix(along_x),
        jnp.asarray(
            np.concatenate([tiles, expand_tiles.reshape(16, 8, 128), expand.T.reshape(4, 8, 128)]), f32
        ),
    )


def lane_index(rows):
    return lax.broadcasted_iota(jnp.int32, (rows, 128), 1)


def turn(values, steps, axis=1):
    steps = steps % values.shape[axis]
    return values if steps == 0 else pltpu.roll(values, steps, axis)


def share_lanes(values):
    lane = lane_index(values.shape[0])
    first = (lane % 4 == 0) & (lane > 0)
    last = (lane % 4 == 3) & (lane < 127)
    return values + jnp.where(first, turn(values, 1), jnp.where(last, turn(values, 127), 0.0))


def share_rows(values):
    row = lax.broadcasted_iota(jnp.int32, values.shape, 0)
    first = (row % 4 == 0) & (row > 0)
    last = (row % 4 == 3) & (row < 127)
    return values + jnp.where(
        first, turn(values, 1, 0), jnp.where(last, turn(values, 127, 0), 0.0)
    )


def share_block(values):
    return share_rows(share_lanes(values))


def split_matrix(table):
    high = jnp.asarray(table, f32).astype(jnp.bfloat16)
    low = (jnp.asarray(table, f32) - high.astype(f32)).astype(jnp.bfloat16)
    return jnp.concatenate([high, high, low], -2)


def product(values, matrix):
    high = values.astype(jnp.bfloat16)
    low = (values - high.astype(f32)).astype(jnp.bfloat16)
    return jnp.dot(
        jnp.concatenate([high, low, high], 1), matrix, preferred_element_type=f32
    )


def along_rows(values, tiles_ref, base):
    grouped = values.reshape(16, 8, 128)
    total = grouped * tiles_ref[base + 3][None]
    for shift in (-3, -2, -1, 1, 2, 3):
        total = total + pltpu.roll(grouped, (-shift) % 8, 1) * tiles_ref[base + 3 + shift][None]
    return total.reshape(128, 128)


def second_lanes(values, tiles_ref):
    total = values * tiles_ref[17, 0:1]
    for shift in (-3, -2, -1, 1, 2, 3):
        total = total + turn(values, -shift) * tiles_ref[17 + shift, 0:1]
    return total


def pack_end(lines, at_high):
    lane = lane_index(8)
    start = 124 if at_high else 0
    packed = jnp.zeros((8, 128), f32)
    for part in range(3):
        moved = turn(lines[8 * part : 8 * part + 8], 4 * part - start)
        packed = jnp.where(lane // 4 == part, moved, packed)
    return packed


def pack_mass(line, at_high):
    lane = lane_index(8)
    start = 124 if at_high else 0
    wide = jnp.broadcast_to(line, (8, 128))
    packed = jnp.zeros((8, 128), f32)
    for part in range(3):
        packed = jnp.where(lane // 4 == 6 + part, turn(wide, 24 + 4 * part - start), packed)
    return packed


def fold_line(line):
    lane = lane_index(8)
    row = lax.broadcasted_iota(jnp.int32, (8, 128), 0)
    wide = jnp.broadcast_to(line, (8, 128))
    folded = jnp.zeros((8, 128), f32)
    for part in range(8):
        folded = jnp.where((row == part) & (lane // 16 == 3), turn(wide, 48 - 16 * part), folded)
    return folded


def unfold_line(tile):
    lane = lane_index(8)
    row = lax.broadcasted_iota(jnp.int32, (8, 128), 0)
    moved = pltpu.roll(turn(tile, -48), 0, 1, stride=16, stride_axis=0)
    return jnp.sum(jnp.where(lane // 16 == row, moved, 0.0), axis=0, keepdims=True)


def top_lanes():
    lane = lane_index(8)
    row = lax.broadcasted_iota(jnp.int32, (8, 128), 0)
    return (row == 7) & (lane >= 24) & (lane < 48)


def mass_of_nodes(elem_mass, tiles_ref):
    wide = tiles_ref[25:41].reshape(128, 128)[:, :32]
    rows = jnp.dot(wide, elem_mass, precision=HIGH, preferred_element_type=f32)
    return jnp.dot(
        rows, tiles_ref[41:45].reshape(32, 128), precision=HIGH, preferred_element_type=f32
    )


def find_tables(device, owner_ref, table_ref, cols_b):
    square = device // 16
    squares = cols_b // 4
    place = jnp.zeros((48, 128), f32)
    index = lax.broadcasted_iota(jnp.int32, (48, 1), 0)
    wanted = ((square + index // 16 + squares - 1) % squares) * 16 + index % 16
    lane = lane_index(1)
    own = jnp.zeros((1, 128), f32)
    for row in range(4):
        line = owner_ref[row : row + 1, :]
        code = (128 * row + lane).astype(f32)
        place = place + jnp.where(line == wanted, code, 0.0)
        own = own + jnp.where(line == device, code, 0.0)
    place = jnp.sum(place, axis=1, keepdims=True).astype(jnp.int32)
    own = jnp.sum(own, axis=1, keepdims=True).astype(jnp.int32)
    own_row, own_col = own // 128, own % 128
    rows, cols = place // 128, place % 128
    member = device % 16
    here_rows, here_cols = rows[16:32], cols[16:32]
    down, over = here_rows - own_row, here_cols - own_col
    inside = jnp.full((16, 1), -1, jnp.int32)
    for start, (step_y, step_x) in zip(STARTS, steps8):
        inside = jnp.where((down == step_y) & (over == step_x), start, inside)
    crossing = jnp.full((16, 1), -1, jnp.int32)
    sixteen = lax.broadcasted_iota(jnp.int32, (16, 1), 0)
    sources = []
    for side, begin, step_x in ((RIGHT, 32, 1), (LEFT, 0, -1)):
        there_rows, there_cols = rows[begin : begin + 16], cols[begin : begin + 16]
        beside = there_cols == (own_col + step_x + cols_b) % cols_b
        picked = sixteen == member
        their = jnp.sum(
            jnp.where(picked, place[begin : begin + 16], 0).astype(f32), axis=0, keepdims=True
        ).astype(jnp.int32)
        their_row, their_col = their // 128, their % 128
        facing = here_cols == (their_col - step_x + cols_b) % cols_b
        for number, step_y in enumerate((0, 1, -1)):
            start = STARTS[side] if step_y == 0 else STARTS[side] + 8 * number
            crossing = jnp.where(beside & (there_rows - own_row == step_y), start, crossing)
            found = facing & (their_row - here_rows == step_y)
            sources.append(
                jnp.sum(jnp.where(found, sixteen, 0).astype(f32), axis=0, keepdims=True).astype(
                    jnp.int32
                )
            )
    way = lax.broadcasted_iota(jnp.int32, (8, 1), 0)
    step_y = jnp.zeros((8, 1), jnp.int32)
    step_x = jnp.zeros((8, 1), jnp.int32)
    for number, (along_y, along_x) in enumerate(steps8):
        step_y = jnp.where(way == number, along_y, step_y)
        step_x = jnp.where(way == number, along_x, step_x)
    near_row = own_row + step_y
    near_col = (own_col + step_x + cols_b) % cols_b
    found = jnp.zeros((8, 128), f32)
    for row in range(4):
        line = owner_ref[row : row + 1, :].astype(f32)
        found = found + jnp.where((near_row == row) & (near_col == lane), line, 0.0)
    found = jnp.sum(found, axis=1, keepdims=True).astype(jnp.int32)
    there = (near_row >= 0) & (near_row < 4)
    slot = found % 16
    kind = jnp.where(there, jnp.where(found // 16 == square, 1, 2), 0)
    ahead_of = jnp.where(way == 0, sources[0], 0)
    for number in range(1, 6):
        ahead_of = jnp.where(way == number, sources[number], ahead_of)
    column = jnp.concatenate([inside, crossing, slot, kind, ahead_of], 0).astype(f32)
    picked = lax.broadcasted_iota(jnp.int32, (56, 128), 0) == lane_index(56)
    table_ref[...] = jnp.sum(jnp.where(picked, column, 0.0), axis=0, keepdims=True).astype(
        jnp.int32
    )


def share_band(values):
    across = share_lanes(values).reshape(16, 8, 128)
    row = lax.broadcasted_iota(jnp.int32, (1, 8, 128), 1)
    above = pltpu.roll(across, 1, 1)
    below = pltpu.roll(across, 7, 1)
    shared = across + jnp.where(row == 4, above, jnp.where(row == 3, below, 0.0))
    return shared.reshape(128, 128)


def changes(east, north, height, coriolis, mass, inverse, share, along_x_ref, tiles_ref):
    energy = 0.5 * (east * east + north * north) + height
    flux_x, flux_y = height * east, height * north
    first_x = product(jnp.concatenate([north, energy, flux_x], 0), along_x_ref[0])
    second_x = product(jnp.concatenate([east, north, height], 0), along_x_ref[1])
    absolute = first_x[:128] - along_rows(east, tiles_ref, 0) + coriolis
    tendencies = (
        absolute * north - first_x[128:256],
        -absolute * east - along_rows(energy, tiles_ref, 0),
        -(first_x[256:] + along_rows(flux_y, tiles_ref, 0)),
    )
    locals_, smoothed = [], []
    for part, values in enumerate((east, north, height)):
        lap = second_x[128 * part : 128 * part + 128] + along_rows(values, tiles_ref, 7)
        local = share(lap * mass)
        locals_.append(local)
        smoothed.append(local * inverse)
    second_x = product(jnp.concatenate(smoothed, 0), along_x_ref[1])
    changed = []
    for part in range(3):
        lap = second_x[128 * part : 128 * part + 128] + along_rows(smoothed[part], tiles_ref, 7)
        changed.append(share((tendencies[part] - hyper_coef * lap) * mass))
    return locals_, changed


def edge_kernel(
    cols_b, device_ref, owner_far,
    velocity_far, height_far, coriolis_far, elem_mass_far, along_x_far, tiles_far,
    lines_ref, send_ref, table_ref,
    smooth, change, owner_ref, near_ref, velocity_ref, height_ref, coriolis_ref, elem_mass_ref,
    along_x_ref, tiles_ref, arrived,
):
    far = (
        owner_far, elem_mass_far, tiles_far, height_far, velocity_far, coriolis_far, along_x_far,
    )
    near = (
        owner_ref, elem_mass_ref, tiles_ref, height_ref, velocity_ref, coriolis_ref, along_x_ref,
    )
    copies = [
        pltpu.make_async_copy(far[k], near[k], arrived.at[k]) for k in range(len(far))
    ]
    for copy in copies:
        copy.start()
    lane = lane_index(128)
    copies[0].wait()
    find_tables(device_ref[0], owner_ref, table_ref, cols_b)
    table_copy = pltpu.make_async_copy(table_ref, near_ref, arrived.at[7])
    table_copy.start()
    copies[1].wait()
    copies[2].wait()
    mass = mass_of_nodes(elem_mass_ref[0], tiles_ref)
    mass_t = jnp.transpose(mass)
    for copy in copies[3:]:
        copy.wait()
    coriolis = coriolis_ref[0]

    def upright_band(ref_value):
        return jnp.concatenate([ref_value[120:128], ref_value[0:8]], 0)

    def upright_plane(read):
        return jnp.concatenate(
            [piece for level in range(8) for piece in (read(level, 120), read(level, 0))], 0
        )

    def sideways_plane(read):
        packed = jnp.zeros((128, 128), f32)
        for level in range(8):
            packed = jnp.where(lane // 16 == level, turn(read(level), 8 + 16 * level), packed)
        return jnp.transpose(packed)

    def repeat(band):
        return jnp.concatenate([band] * 8, 0)

    row = lax.broadcasted_iota(jnp.int32, (128, 128), 0) % 16
    inner = (row != 7) & (row != 8) & (lane > 0) & (lane < 127)
    for way in range(2):
        if way == 0:
            planes = [
                upright_plane(lambda level, at, c=c: velocity_ref[c, level, at : at + 8, :])
                for c in range(2)
            ] + [upright_plane(lambda level, at: height_ref[level, at : at + 8, :])]
            turning = repeat(upright_band(coriolis))
            band_mass = repeat(upright_band(mass))
        else:
            top = jnp.zeros((128, 128), f32)
            for level in range(8):
                east, north = velocity_ref[0, level], velocity_ref[1, level]
                top = jnp.maximum(
                    top, jnp.sqrt(east * east + north * north) + jnp.sqrt(height_ref[level])
                )
            top = jnp.max(top, axis=(0, 1), keepdims=True)
            planes = [
                sideways_plane(lambda level, c=c: velocity_ref[c, level]) for c in (1, 0)
            ] + [sideways_plane(lambda level: height_ref[level])]
            turning = -sideways_plane(lambda level: coriolis)
            band_mass = repeat(upright_band(mass_t))
        inverse = jnp.where(inner, 1.0 / share_band(band_mass), 0.0)
        locals_, changed = changes(
            *planes, turning, band_mass, inverse, share_band, along_x_ref, tiles_ref
        )
        for part in range(3):
            target = part if way == 0 or part == 2 else 1 - part
            smooth[way, target] = locals_[part]
            change[way, target] = changed[part]

    sizes = (72, 72, 56, 56)
    targets = [lines_ref.at[pl.ds(STARTS[side], sizes[side])] for side in range(4)]
    for way in range(2):
        for end in range(2):
            target = targets[2 * (1 - way) + end]
            for part in range(3):
                place = pl.ds(7 + end, 8, stride=16)
                target[8 * part : 8 * part + 8, :] = smooth.at[way, part][place, :]
                target[24 + 8 * part : 32 + 8 * part, :] = change.at[way, part][place, :]
    mass_lines = (mass_t[127:128], mass_t[0:1], mass[127:128], mass[0:1])
    lines = [targets[side][0:48, :] for side in range(4)]
    ends = {}
    for side in range(4):
        local_mass = share_lanes(mass_lines[side])
        for high in (False, True):
            ends[side, high] = pack_end(lines[side][0:24], high) + pack_mass(local_mass, high)
    extras = (
        ends[UPPER, True] + turn(ends[LOWER, True], 12),
        ends[UPPER, False] + turn(ends[LOWER, False], 12),
        ends[LEFT, True] + turn(ends[RIGHT, True], 12),
        ends[LEFT, False] + turn(ends[RIGHT, False], 12),
    )
    for side in range(4):
        targets[side][48:56, :] = extras[side] + fold_line(mass_lines[side])
    for number, (along, upward) in enumerate(((UPPER, True), (LOWER, False))):
        for across, sideways in ((RIGHT, True), (LEFT, False)):
            tile = ends[along, sideways] + turn(ends[across, upward], 12)
            tile = tile + turn(pack_end(lines[along][24:48], sideways), 48)
            targets[across][56 + 8 * number : 64 + 8 * number, :] = tile
    table_copy.wait()
    starts = [
        [pl.multiple_of(jnp.maximum(near_ref[0, 16 * part + place], 0), 8) for part in range(2)]
        for place in range(16)
    ]
    for place in range(16):
        for part in range(2):
            rows = pl.ds(starts[place][part], 48)
            send_ref[place, 48 * part : 48 * part + 48, :] = lines_ref[rows, :]
    for place in range(16):
        tiles = [lines_ref[pl.ds(starts[place][part] + 48, 8), :] for part in range(2)]
        tile = jnp.where(lane_index(8) < 64, tiles[0], turn(tiles[1], 64))
        send_ref[place, 96:104, :] = jnp.where(top_lanes(), top, tile)


def block_kernel(
    velocity_ref, height_ref, coriolis_ref, elem_mass_ref, along_x_ref, tiles_ref, after_ref,
    partial_ref, node_mass, inner_inverse,
):
    lane = lane_index(128)
    step = pl.program_id(0)

    @pl.when(step == 0)
    def _():
        node_mass[...] = mass_of_nodes(elem_mass_ref[0], tiles_ref)
        local_mass = share_block(node_mass[...])
        row = lax.broadcasted_iota(jnp.int32, (128, 128), 0)
        inner = (row > 0) & (row < 127) & (lane > 0) & (lane < 127)
        inner_inverse[...] = jnp.where(inner, 1.0 / local_mass, 0.0)

    @pl.when(step < 8)
    def _():
        _, changed = changes(
            velocity_ref[0, 0], velocity_ref[1, 0], height_ref[0], coriolis_ref[0],
            node_mass[...], inner_inverse[...], share_block, along_x_ref, tiles_ref,
        )
        for part in range(3):
            partial_ref[part] = changed[part]

    @pl.when(step == 8)
    def _():
        partial_ref[0] = share_block(node_mass[...])


def pack_kernel(table_ref, received_ref, after_ref, ahead_ref, behind_ref, top_ref):
    top = jnp.zeros((8, 128), f32)
    for place in range(16):
        top = jnp.maximum(top, received_ref[place, 96:104, :])
    top = jnp.max(jnp.where(top_lanes(), top, 0.0), axis=(0, 1), keepdims=True)
    top_ref[...] = jnp.broadcast_to(top, top_ref.shape)
    for base, ref in ((48, ahead_ref), (51, behind_ref)):
        ref[0:48, :] = received_ref[table_ref[0, base], 48:96, :]
        for number in range(3):
            tile = received_ref[table_ref[0, base + number], 96:104, :]
            ref[48 + 8 * number : 56 + 8 * number, :] = turn(tile, 64)


def edge_terms(table_ref, lines, received_ref, ahead_ref, behind_ref, tiles_ref):
    lane = lane_index(1)

    def message(way, start, stop):
        kind = table_ref[0, 40 + way]
        skip = 48 if start == 48 else 0
        values = received_ref[table_ref[0, 32 + way], start + skip : stop + skip, :]
        step_y, step_x = steps8[way]
        if step_x != 0:
            crossed = ahead_ref if step_x > 0 else behind_ref
            shift = (0, 16, 8)[step_y]
            values = jnp.where(kind == 2, crossed[start + shift : stop + shift, :], values)
        return jnp.where(kind > 0, values, 0.0)

    own = [line[0:24, :] for line in lines]
    own_mass = [unfold_line(line[48:56, :]) for line in lines]
    near = [message(side, 0, 24) for side in range(4)]
    change = [message(side, 24, 48) for side in range(4)]
    extra = [message(side, 48, 56) for side in range(4)]
    mass = [unfold_line(extra[side]) for side in range(4)]
    shared_mass = [share_lanes(mass[side]) for side in range(4)]
    total = [own[side] + near[side] for side in range(4)]
    total_mass = [share_lanes(own_mass[side]) + shared_mass[side] for side in range(4)]
    corners = []
    for along in (UPPER, LOWER):
        for across in (RIGHT, LEFT):
            corner = 4 + 2 * (along - UPPER) + across
            at_x = 127 if across == RIGHT else 0
            at_y = 127 if along == UPPER else 0
            tile = message(corner, 48, 56)
            end_x = 0 if across == RIGHT else 3

            def spread_out(packed, start, at_x=at_x):
                return jnp.concatenate(
                    [turn(packed, at_x - start - 4 * part) for part in range(3)], 0
                )

            far = spread_out(tile, end_x)
            far_mass = turn(tile, at_x - 24 - end_x)[0:1]
            corners.append((along, across, at_x, at_y, tile, far_mass, spread_out))
            on_x, on_y = lane == at_x, lane == at_y
            total[along] = total[along] + jnp.where(
                on_x, turn(near[across], at_x - at_y) + far, 0.0
            )
            total_mass[along] = total_mass[along] + jnp.where(
                on_x, turn(mass[across], at_x - at_y) + far_mass, 0.0
            )
            total[across] = total[across] + jnp.where(
                on_y, turn(near[along] + far, at_y - at_x), 0.0
            )
            total_mass[across] = total_mass[across] + jnp.where(
                on_y, turn(mass[along] + far_mass, at_y - at_x), 0.0
            )
    smooth = [total[side] / total_mass[side] for side in range(4)]
    curve = [second_lanes(smooth[side], tiles_ref) for side in range(4)]
    added = [
        change[side]
        - hyper_coef
        * (shared_mass[side] * CENTRE * smooth[side] + share_lanes(mass[side] * curve[side]))
        for side in range(4)
    ]

    def arm(beside, diagonal, coefs):
        both = beside + diagonal
        weight = jnp.broadcast_to(turn(both, -24)[0:1], (8, 128))
        value = jnp.where(weight > 0.0, both / jnp.where(weight > 0.0, weight, 1.0), 0.0) * coefs
        value = value + turn(value, -1)
        return value + turn(value, -2)

    for along, across, at_x, at_y, tile, far_mass, spread_out in corners:
        beside = extra[across] if along == UPPER else turn(extra[across], -12)
        arm_x = spread_out(arm(beside, tile, tiles_ref[21 if across == RIGHT else 22]), 0)
        beside = extra[along] if across == LEFT else turn(extra[along], -12)
        arm_y = spread_out(
            arm(beside, turn(tile, -12), tiles_ref[21 if along == UPPER else 22]), 0
        )
        middle = CENTRE * smooth[along]
        arm_x, arm_y = arm_x + middle, arm_y + middle
        own_x = curve[along]
        own_y = turn(curve[across], at_x - at_y)
        mass_x = turn(mass[across], at_x - at_y)
        end_x = 0 if across == RIGHT else 3
        value = (
            turn(change[across], at_x - at_y) + change[along] + spread_out(tile, 48 + end_x)
        ) - hyper_coef * (
            mass_x * (arm_x + own_y) + mass[along] * (own_x + arm_y) + far_mass * (arm_x + arm_y)
        )
        added[along] = jnp.where(lane == at_x, value, added[along])
    ends = (lane == 0) | (lane == 127)
    plain, edge = [], []
    for side in range(4):
        line = smooth[side] if side >= UPPER else jnp.where(ends, 0.0, smooth[side])
        outside = added[side] if side >= UPPER else jnp.where(ends, 0.0, added[side])
        bend = curve[side] if side >= UPPER else second_lanes(line, tiles_ref)
        plain.append(share_lanes(own_mass[side] * line))
        edge.append(outside - hyper_coef * share_lanes(own_mass[side] * bend))
    return plain, edge, total_mass


def last_kernel(
    table_ref, lines_ref, received_ref, ahead_ref, behind_ref, tops_ref, tiles_ref, widen_ref,
    velocity_far, height_far, partial_far, new_velocity_far, new_height_far,
    rows, velocity_ref, height_ref, partial_ref, arrived, left_off,
):
    lane = lane_index(128)
    mass_in = pltpu.make_async_copy(partial_far.at[24], partial_ref.at[24], arrived.at[3, 0])
    mass_in.start()
    incoming = []
    for group in range(GROUPS):
        part = pl.ds(LEVELS_EACH * group, LEVELS_EACH)
        incoming.append(
            (
                pltpu.make_async_copy(
                    partial_far.at[pl.ds(3 * LEVELS_EACH * group, 3 * LEVELS_EACH)],
                    partial_ref.at[pl.ds(3 * LEVELS_EACH * group, 3 * LEVELS_EACH)],
                    arrived.at[0, group],
                ),
                pltpu.make_async_copy(
                    velocity_far.at[:, part], velocity_ref.at[:, part], arrived.at[1, group]
                ),
                pltpu.make_async_copy(
                    height_far.at[part], height_ref.at[part], arrived.at[2, group]
                ),
            )
        )
        for copy in incoming[-1]:
            copy.start()

    lines = [lines_ref.at[pl.ds(STARTS[side], 56)] for side in range(4)]
    plain, edge, total_mass = edge_terms(
        table_ref, lines, received_ref, ahead_ref, behind_ref, tiles_ref
    )
    rows[0] = plain[UPPER]
    rows[1] = plain[LOWER]
    rows[2] = edge[UPPER]
    rows[3] = edge[LOWER]
    stacked = jnp.concatenate(
        [plain[LEFT], plain[RIGHT], edge[LEFT], edge[RIGHT]]
        + [jnp.broadcast_to(total_mass[side], (16, 128)) for side in (LEFT, RIGHT)],
        0,
    )
    columns = jnp.transpose(stacked)
    mass_in.wait()
    mass = partial_ref[24]
    mass = jnp.where(lane == 0, columns[:, 96:97], mass)
    mass = jnp.where(lane == 127, columns[:, 112:113], mass)
    row = lax.broadcasted_iota(jnp.int32, (128, 128), 0)
    mass = jnp.where(row == 127, total_mass[UPPER], mass)
    mass = jnp.where(row == 0, total_mass[LOWER], mass)
    top = jnp.max(tops_ref[...], axis=(0, 1), keepdims=True)
    factor = (courant / top) / mass
    near_edge = (lane < 5) | (lane > 122)
    widened = product(columns, widen_ref[...])
    row = lax.broadcasted_iota(jnp.int32, (8, 128), 0)
    outgoing = []
    for group in range(GROUPS):
        for copy in incoming[group]:
            copy.wait()
        for level in range(LEVELS_EACH * group, LEVELS_EACH * (group + 1)):
            for part in range(3):
                at = 8 * part + level
                half = 128 * (at // 12)
                beside = turn(widened[:, half : half + 128], 123 - 10 * (at % 12))
                value = partial_ref[3 * level + part] + jnp.where(near_edge, beside, 0.0)
                upper = tiles_ref[23] * rows[0, at : at + 1, :]
                lower = tiles_ref[24] * rows[1, at : at + 1, :]
                upper = upper + jnp.where(row == 7, rows[2, at : at + 1, :], 0.0)
                lower = lower + jnp.where(row == 0, rows[3, at : at + 1, :], 0.0)
                value = jnp.concatenate([value[:8] + lower, value[8:120], value[120:] + upper], 0)
                if part < 2:
                    velocity_ref[part, level] = velocity_ref[part, level] + factor * value
                else:
                    height_ref[level] = height_ref[level] + factor * value
        part = pl.ds(LEVELS_EACH * group, LEVELS_EACH)
        for copy in (
            pltpu.make_async_copy(
                velocity_ref.at[:, part], new_velocity_far.at[:, part], left_off.at[0, group]
            ),
            pltpu.make_async_copy(
                height_ref.at[part], new_height_far.at[part], left_off.at[1, group]
            ),
        ):
            copy.start()
            outgoing.append(copy)
    for copy in outgoing:
        copy.wait()


def whole(shape, space=None):
    if space is None:
        return pl.BlockSpec(shape, lambda level: (0,) * len(shape))
    return pl.BlockSpec(memory_space=space)


def per_device(velocity, thickness, coriolis, elem_mass, block_owner):
    cols_b = block_owner.shape[1]
    count = 4 * cols_b
    velocity = velocity[:, :, 0]
    thickness = thickness[:, 0]
    widen, along_x, tiles = constant_tables()
    device = (lax.axis_index("elem") * lax.axis_size("sub") + lax.axis_index("sub")).reshape(1)
    if cols_b < 128:
        block_owner = jnp.pad(block_owner, ((0, 0), (0, 128 - cols_b)), constant_values=-1)
    shape = jax.ShapeDtypeStruct
    params = pltpu.CompilerParams(
        dimension_semantics=("arbitrary",), vmem_limit_bytes=BLOCK_VMEM
    )
    vmem = pltpu.VMEM
    far = pl.BlockSpec(memory_space=pltpu.HBM)
    held = pl.BlockSpec(memory_space=vmem)
    small = pl.BlockSpec(memory_space=pltpu.SMEM)
    arrays = (block_owner, velocity, thickness, coriolis, elem_mass, along_x, tiles)
    lines, send, table = pl.pallas_call(
        functools.partial(edge_kernel, cols_b),
        in_specs=[small] + [far] * 7,
        out_specs=[held] * 3,
        out_shape=[
            shape((256, 128), f32), shape((16, 104, 128), f32), shape((1, 128), jnp.int32),
        ],
        scratch_shapes=[
            pltpu.VMEM((2, 3, 128, 128), f32), pltpu.VMEM((2, 3, 128, 128), f32),
            pltpu.VMEM(block_owner.shape, jnp.int32), pltpu.SMEM((1, 128), jnp.int32),
        ]
        + [pltpu.VMEM(array.shape, array.dtype) for array in arrays[1:]]
        + [pltpu.SemaphoreType.DMA((8,))],
        compiler_params=pltpu.CompilerParams(vmem_limit_bytes=EDGE_VMEM),
        name="edge",
    )(device, *arrays)
    squares = count // 16
    same_place = [[16 * s + i for s in range(squares)] for i in range(16)]
    same_square = [[16 * s + i for i in range(16)] for s in range(squares)]
    received = lax.all_to_all(
        send, axes, 0, 0, axis_index_groups=same_square, tiled=True
    )
    pair = pl.BlockSpec((2, 1, 128, 128), lambda step: (0, jnp.minimum(step, 7), 0, 0))
    single = pl.BlockSpec((1, 128, 128), lambda step: (jnp.minimum(step, 7), 0, 0))
    partial = pl.pallas_call(
        block_kernel,
        grid=(9,),
        in_specs=[
            pair, single, whole((1, 128, 128)), whole((1, 32, 32)), whole((2, 384, 128)),
            whole((45, 8, 128)), whole((1, 8, 128)),
        ],
        out_specs=pl.BlockSpec((3, 128, 128), lambda step: (step, 0, 0)),
        out_shape=shape((27, 128, 128), f32),
        scratch_shapes=[pltpu.VMEM((128, 128), f32), pltpu.VMEM((128, 128), f32)],
        compiler_params=params,
        cost_estimate=pl.CostEstimate(
            flops=2_000_000_000, bytes_accessed=3_200_000, transcendentals=0
        ),
        name="block",
    )(velocity, thickness, coriolis, elem_mass, along_x, tiles, send)
    to_ahead, to_behind, top = pl.pallas_call(
        pack_kernel,
        grid=(1,),
        in_specs=[
            whole((1, 128), pltpu.SMEM), whole((16, 104, 128)),
            pl.BlockSpec((1, 8, 128), lambda step: (0, 0, 0)),
        ],
        out_specs=[
            whole((72, 128)), whole((72, 128)), whole((squares * TOP_ROWS, 128)),
        ],
        out_shape=[
            shape((72, 128), f32), shape((72, 128), f32), shape((squares * TOP_ROWS, 128), f32),
        ],
        compiler_params=pltpu.CompilerParams(vmem_limit_bytes=PACK_VMEM),
        name="pack",
    )(table, received, partial)
    tops = lax.all_to_all(top, axes, 0, 0, axis_index_groups=same_place, tiled=True)
    ahead = lax.ppermute(to_behind, axes, [(b, (b - 16) % count) for b in range(count)])
    behind = lax.ppermute(to_ahead, axes, [(b, (b + 16) % count) for b in range(count)])
    new_velocity, new_thickness = pl.pallas_call(
        last_kernel,
        in_specs=[small] + [held] * 7 + [far] * 3,
        out_specs=[far] * 2,
        out_shape=[shape((2, 8, 128, 128), f32), shape((8, 128, 128), f32)],
        scratch_shapes=[
            pltpu.VMEM((4, 24, 128), f32), pltpu.VMEM((2, 8, 128, 128), f32),
            pltpu.VMEM((8, 128, 128), f32), pltpu.VMEM((25, 128, 128), f32),
            pltpu.SemaphoreType.DMA((4, GROUPS)), pltpu.SemaphoreType.DMA((2, GROUPS)),
        ],
        compiler_params=pltpu.CompilerParams(vmem_limit_bytes=LAST_VMEM),
        name="last",
    )(table, lines, received, ahead, behind, tops, tiles, widen, velocity, thickness, partial)
    return new_velocity[:, :, None], new_thickness[:, None]


def solution(mesh):
    return jax.shard_map(
        per_device,
        mesh=mesh,
        in_specs=(
            P(None, None, axes, None, None),
            P(None, axes, None, None),
            P(axes, None, None),
            P(axes, None, None),
            P(),
        ),
        out_specs=(
            P(None, None, axes, None, None),
            P(None, axes, None, None),
        ),
        check_vma=False,
    )
```

```python
import functools
import math

import jax
import jax.numpy as jnp
import numpy as np
from jax import lax
from jax.experimental import pallas as pl
from jax.experimental.pallas import tpu as pltpu
from jax.sharding import PartitionSpec as P

courant = 0.1
hyper_coef = 0.002
TOP_ROWS = 2
MIB = 1024 * 1024
EDGE_VMEM = 60 * MIB
PACK_VMEM = 52 * MIB
BLOCK_VMEM = 60 * MIB
LAST_VMEM = 51 * MIB
GROUPS = 2
LEVELS_EACH = 8 // GROUPS
axes = ("elem", "sub")
f32 = jnp.float32
HIGH = lax.Precision.HIGHEST
RIGHT, LEFT, UPPER, LOWER = range(4)
STARTS = (0, 72, 144, 200, 8, 80, 16, 88)
steps8 = ((0, 1), (0, -1), (1, 0), (-1, 0), (1, 1), (1, -1), (-1, 1), (-1, -1))


def gll_tables():
    points = [-1.0, -1.0 / math.sqrt(5.0), 1.0 / math.sqrt(5.0), 1.0]
    weights = np.array([1.0 / 6.0, 5.0 / 6.0, 5.0 / 6.0, 1.0 / 6.0])
    spread = [
        math.prod([points[target] - points[others] for others in range(4) if others != target])
        for target in range(4)
    ]
    derivative = np.zeros((4, 4))
    for target in range(4):
        for source in range(4):
            if target == source:
                derivative[target, source] = sum(
                    1.0 / (points[target] - points[others]) for others in range(4) if others != target
                )
            else:
                derivative[target, source] = spread[target] / (
                    spread[source] * (points[target] - points[source])
                )
    return weights, 2.0 * derivative


WEIGHTS, FIRST = gll_tables()
SECOND = FIRST @ FIRST
CENTRE = float(SECOND[0, 0])


def offset_rows(table):
    rows = np.zeros((7, 4))
    for shift in range(-3, 4):
        for target in range(4):
            if 0 <= target + shift < 4:
                rows[shift + 3, target] = table[target, target + shift]
    return rows


def constant_tables():
    along_x = np.stack([np.kron(np.eye(32), FIRST.T), np.kron(np.eye(32), SECOND.T)])
    expand = np.kron(np.eye(32), WEIGHTS[:, None])
    tiles = np.zeros((25, 8, 128))
    expand_tiles = np.zeros((128, 128))
    expand_tiles[:, :32] = expand
    for base, table in ((0, FIRST), (7, SECOND)):
        tiles[base : base + 7] = np.tile(offset_rows(table), (1, 2))[:, :, None]
    tiles[14:21] = np.tile(offset_rows(SECOND), (1, 32))[:, None, :]
    arm_low = np.array([0.0, SECOND[0, 1], SECOND[0, 2], SECOND[0, 3]])
    arm_high = np.array([SECOND[3, 0], SECOND[3, 1], SECOND[3, 2], 0.0])
    tiles[21] = np.tile(arm_low, 32)[None]
    tiles[22] = np.tile(arm_high, 32)[None]
    high = np.array([-hyper_coef * WEIGHTS[a] / WEIGHTS[3] * SECOND[a, 3] for a in range(4)])
    low = np.array([-hyper_coef * WEIGHTS[a] / WEIGHTS[0] * SECOND[a, 0] for a in range(4)])
    tiles[23] = np.concatenate([[0.0, 0.0, 0.0, high[0]], high])[:, None]
    tiles[24] = np.concatenate([low, [low[3], 0.0, 0.0, 0.0]])[:, None]
    across = np.zeros(128)
    across[:5] = [*low, low[3]]
    across[123:] = [high[0], *high]
    widen = np.zeros((128, 256))
    for plane in range(24):
        start = 128 * (plane // 12) + 10 * (plane % 12)
        for lane in range(10):
            widen[24 * (lane < 5) + plane, start + lane] = across[(123 + lane) % 128]
        widen[72 + plane, start + 4] = 1.0
        widen[48 + plane, start + 5] = 1.0
    return (
        split_matrix(widen),
        split_matrix(along_x),
        jnp.asarray(
            np.concatenate([tiles, expand_tiles.reshape(16, 8, 128), expand.T.reshape(4, 8, 128)]), f32
        ),
    )


def lane_index(rows):
    return lax.broadcasted_iota(jnp.int32, (rows, 128), 1)


def turn(values, steps, axis=1):
    steps = steps % values.shape[axis]
    return values if steps == 0 else pltpu.roll(values, steps, axis)


def share_lanes(values):
    lane = lane_index(values.shape[0])
    first = (lane % 4 == 0) & (lane > 0)
    last = (lane % 4 == 3) & (lane < 127)
    return values + jnp.where(first, turn(values, 1), jnp.where(last, turn(values, 127), 0.0))


def share_rows(values):
    row = lax.broadcasted_iota(jnp.int32, values.shape, 0)
    first = (row % 4 == 0) & (row > 0)
    last = (row % 4 == 3) & (row < 127)
    return values + jnp.where(
        first, turn(values, 1, 0), jnp.where(last, turn(values, 127, 0), 0.0)
    )


def share_block(values):
    return share_rows(share_lanes(values))


def split_matrix(table):
    high = jnp.asarray(table, f32).astype(jnp.bfloat16)
    low = (jnp.asarray(table, f32) - high.astype(f32)).astype(jnp.bfloat16)
    return jnp.concatenate([high, high, low], -2)


def product(values, matrix):
    high = values.astype(jnp.bfloat16)
    low = (values - high.astype(f32)).astype(jnp.bfloat16)
    return jnp.dot(
        jnp.concatenate([high, low, high], 1), matrix, preferred_element_type=f32
    )


def along_rows(values, tiles_ref, base):
    grouped = values.reshape(16, 8, 128)
    total = grouped * tiles_ref[base + 3][None]
    for shift in (-3, -2, -1, 1, 2, 3):
        total = total + pltpu.roll(grouped, (-shift) % 8, 1) * tiles_ref[base + 3 + shift][None]
    return total.reshape(128, 128)


def second_lanes(values, tiles_ref):
    total = values * tiles_ref[17, 0:1]
    for shift in (-3, -2, -1, 1, 2, 3):
        total = total + turn(values, -shift) * tiles_ref[17 + shift, 0:1]
    return total


def pack_end(lines, at_high):
    lane = lane_index(8)
    start = 124 if at_high else 0
    packed = jnp.zeros((8, 128), f32)
    for part in range(3):
        moved = turn(lines[8 * part : 8 * part + 8], 4 * part - start)
        packed = jnp.where(lane // 4 == part, moved, packed)
    return packed


def pack_mass(line, at_high):
    lane = lane_index(8)
    start = 124 if at_high else 0
    wide = jnp.broadcast_to(line, (8, 128))
    packed = jnp.zeros((8, 128), f32)
    for part in range(3):
        packed = jnp.where(lane // 4 == 6 + part, turn(wide, 24 + 4 * part - start), packed)
    return packed


def fold_line(line):
    lane = lane_index(8)
    row = lax.broadcasted_iota(jnp.int32, (8, 128), 0)
    wide = jnp.broadcast_to(line, (8, 128))
    folded = jnp.zeros((8, 128), f32)
    for part in range(8):
        folded = jnp.where((row == part) & (lane // 16 == 3), turn(wide, 48 - 16 * part), folded)
    return folded


def unfold_line(tile):
    lane = lane_index(8)
    row = lax.broadcasted_iota(jnp.int32, (8, 128), 0)
    moved = pltpu.roll(turn(tile, -48), 0, 1, stride=16, stride_axis=0)
    return jnp.sum(jnp.where(lane // 16 == row, moved, 0.0), axis=0, keepdims=True)


def top_lanes():
    lane = lane_index(8)
    row = lax.broadcasted_iota(jnp.int32, (8, 128), 0)
    return (row == 7) & (lane >= 24) & (lane < 48)


def mass_of_nodes(elem_mass, tiles_ref):
    wide = tiles_ref[25:41].reshape(128, 128)[:, :32]
    rows = jnp.dot(wide, elem_mass, precision=HIGH, preferred_element_type=f32)
    return jnp.dot(
        rows, tiles_ref[41:45].reshape(32, 128), precision=HIGH, preferred_element_type=f32
    )


def find_tables(device, owner_ref, table_ref, cols_b):
    square = device // 16
    squares = cols_b // 4
    place = jnp.zeros((48, 128), f32)
    index = lax.broadcasted_iota(jnp.int32, (48, 1), 0)
    wanted = ((square + index // 16 + squares - 1) % squares) * 16 + index % 16
    lane = lane_index(1)
    own = jnp.zeros((1, 128), f32)
    for row in range(4):
        line = owner_ref[row : row + 1, :]
        code = (128 * row + lane).astype(f32)
        place = place + jnp.where(line == wanted, code, 0.0)
        own = own + jnp.where(line == device, code, 0.0)
    place = jnp.sum(place, axis=1, keepdims=True).astype(jnp.int32)
    own = jnp.sum(own, axis=1, keepdims=True).astype(jnp.int32)
    own_row, own_col = own // 128, own % 128
    rows, cols = place // 128, place % 128
    member = device % 16
    here_rows, here_cols = rows[16:32], cols[16:32]
    down, over = here_rows - own_row, here_cols - own_col
    inside = jnp.full((16, 1), -1, jnp.int32)
    for start, (step_y, step_x) in zip(STARTS, steps8):
        inside = jnp.where((down == step_y) & (over == step_x), start, inside)
    crossing = jnp.full((16, 1), -1, jnp.int32)
    sixteen = lax.broadcasted_iota(jnp.int32, (16, 1), 0)
    sources = []
    for side, begin, step_x in ((RIGHT, 32, 1), (LEFT, 0, -1)):
        there_rows, there_cols = rows[begin : begin + 16], cols[begin : begin + 16]
        beside = there_cols == (own_col + step_x + cols_b) % cols_b
        picked = sixteen == member
        their = jnp.sum(
            jnp.where(picked, place[begin : begin + 16], 0).astype(f32), axis=0, keepdims=True
        ).astype(jnp.int32)
        their_row, their_col = their // 128, their % 128
        facing = here_cols == (their_col - step_x + cols_b) % cols_b
        for number, step_y in enumerate((0, 1, -1)):
            start = STARTS[side] if step_y == 0 else STARTS[side] + 8 * number
            crossing = jnp.where(beside & (there_rows - own_row == step_y), start, crossing)
            found = facing & (their_row - here_rows == step_y)
            sources.append(
                jnp.sum(jnp.where(found, sixteen, 0).astype(f32), axis=0, keepdims=True).astype(
                    jnp.int32
                )
            )
    way = lax.broadcasted_iota(jnp.int32, (8, 1), 0)
    step_y = jnp.zeros((8, 1), jnp.int32)
    step_x = jnp.zeros((8, 1), jnp.int32)
    for number, (along_y, along_x) in enumerate(steps8):
        step_y = jnp.where(way == number, along_y, step_y)
        step_x = jnp.where(way == number, along_x, step_x)
    near_row = own_row + step_y
    near_col = (own_col + step_x + cols_b) % cols_b
    found = jnp.zeros((8, 128), f32)
    for row in range(4):
        line = owner_ref[row : row + 1, :].astype(f32)
        found = found + jnp.where((near_row == row) & (near_col == lane), line, 0.0)
    found = jnp.sum(found, axis=1, keepdims=True).astype(jnp.int32)
    there = (near_row >= 0) & (near_row < 4)
    slot = found % 16
    kind = jnp.where(there, jnp.where(found // 16 == square, 1, 2), 0)
    ahead_of = jnp.where(way == 0, sources[0], 0)
    for number in range(1, 6):
        ahead_of = jnp.where(way == number, sources[number], ahead_of)
    column = jnp.concatenate([inside, crossing, slot, kind, ahead_of], 0).astype(f32)
    picked = lax.broadcasted_iota(jnp.int32, (56, 128), 0) == lane_index(56)
    table_ref[...] = jnp.sum(jnp.where(picked, column, 0.0), axis=0, keepdims=True).astype(
        jnp.int32
    )


def share_band(values):
    across = share_lanes(values).reshape(16, 8, 128)
    row = lax.broadcasted_iota(jnp.int32, (1, 8, 128), 1)
    above = pltpu.roll(across, 1, 1)
    below = pltpu.roll(across, 7, 1)
    shared = across + jnp.where(row == 4, above, jnp.where(row == 3, below, 0.0))
    return shared.reshape(128, 128)


def changes(east, north, height, coriolis, mass, inverse, share, along_x_ref, tiles_ref):
    energy = 0.5 * (east * east + north * north) + height
    flux_x, flux_y = height * east, height * north
    first_x = product(jnp.concatenate([north, energy, flux_x], 0), along_x_ref[0])
    second_x = product(jnp.concatenate([east, north, height], 0), along_x_ref[1])
    absolute = first_x[:128] - along_rows(east, tiles_ref, 0) + coriolis
    tendencies = (
        absolute * north - first_x[128:256],
        -absolute * east - along_rows(energy, tiles_ref, 0),
        -(first_x[256:] + along_rows(flux_y, tiles_ref, 0)),
    )
    locals_, smoothed = [], []
    for part, values in enumerate((east, north, height)):
        lap = second_x[128 * part : 128 * part + 128] + along_rows(values, tiles_ref, 7)
        local = share(lap * mass)
        locals_.append(local)
        smoothed.append(local * inverse)
    second_x = product(jnp.concatenate(smoothed, 0), along_x_ref[1])
    changed = []
    for part in range(3):
        lap = second_x[128 * part : 128 * part + 128] + along_rows(smoothed[part], tiles_ref, 7)
        changed.append(share((tendencies[part] - hyper_coef * lap) * mass))
    return locals_, changed


def edge_kernel(
    cols_b, device_ref, owner_far,
    velocity_far, height_far, coriolis_far, elem_mass_far, along_x_far, tiles_far,
    lines_ref, send_ref, table_ref,
    smooth, change, owner_ref, near_ref, velocity_ref, height_ref, coriolis_ref, elem_mass_ref,
    along_x_ref, tiles_ref, arrived,
):
    far = (
        owner_far, elem_mass_far, tiles_far, height_far, velocity_far, coriolis_far, along_x_far,
    )
    near = (
        owner_ref, elem_mass_ref, tiles_ref, height_ref, velocity_ref, coriolis_ref, along_x_ref,
    )
    copies = [
        pltpu.make_async_copy(far[k], near[k], arrived.at[k]) for k in range(len(far))
    ]
    for copy in copies:
        copy.start()
    lane = lane_index(128)
    copies[0].wait()
    find_tables(device_ref[0], owner_ref, table_ref, cols_b)
    table_copy = pltpu.make_async_copy(table_ref, near_ref, arrived.at[7])
    table_copy.start()
    copies[1].wait()
    copies[2].wait()
    mass = mass_of_nodes(elem_mass_ref[0], tiles_ref)
    mass_t = jnp.transpose(mass)
    for copy in copies[3:]:
        copy.wait()
    coriolis = coriolis_ref[0]

    def upright_band(ref_value):
        return jnp.concatenate([ref_value[120:128], ref_value[0:8]], 0)

    def upright_plane(read):
        return jnp.concatenate(
            [piece for level in range(8) for piece in (read(level, 120), read(level, 0))], 0
        )

    def sideways_plane(read):
        packed = jnp.zeros((128, 128), f32)
        for level in range(8):
            packed = jnp.where(lane // 16 == level, turn(read(level), 8 + 16 * level), packed)
        return jnp.transpose(packed)

    def repeat(band):
        return jnp.concatenate([band] * 8, 0)

    row = lax.broadcasted_iota(jnp.int32, (128, 128), 0) % 16
    inner = (row != 7) & (row != 8) & (lane > 0) & (lane < 127)
    for way in range(2):
        if way == 0:
            planes = [
                upright_plane(lambda level, at, c=c: velocity_ref[c, level, at : at + 8, :])
                for c in range(2)
            ] + [upright_plane(lambda level, at: height_ref[level, at : at + 8, :])]
            turning = repeat(upright_band(coriolis))
            band_mass = repeat(upright_band(mass))
        else:
            top = jnp.zeros((128, 128), f32)
            for level in range(8):
                east, north = velocity_ref[0, level], velocity_ref[1, level]
                top = jnp.maximum(
                    top, jnp.sqrt(east * east + north * north) + jnp.sqrt(height_ref[level])
                )
            top = jnp.max(top, axis=(0, 1), keepdims=True)
            planes = [
                sideways_plane(lambda level, c=c: velocity_ref[c, level]) for c in (1, 0)
            ] + [sideways_plane(lambda level: height_ref[level])]
            turning = -sideways_plane(lambda level: coriolis)
            band_mass = repeat(upright_band(mass_t))
        inverse = jnp.where(inner, 1.0 / share_band(band_mass), 0.0)
        locals_, changed = changes(
            *planes, turning, band_mass, inverse, share_band, along_x_ref, tiles_ref
        )
        for part in range(3):
            target = part if way == 0 or part == 2 else 1 - part
            smooth[way, target] = locals_[part]
            change[way, target] = changed[part]

    sizes = (72, 72, 56, 56)
    targets = [lines_ref.at[pl.ds(STARTS[side], sizes[side])] for side in range(4)]
    for way in range(2):
        for end in range(2):
            target = targets[2 * (1 - way) + end]
            for part in range(3):
                place = pl.ds(7 + end, 8, stride=16)
                target[8 * part : 8 * part + 8, :] = smooth.at[way, part][place, :]
                target[24 + 8 * part : 32 + 8 * part, :] = change.at[way, part][place, :]
    mass_lines = (mass_t[127:128], mass_t[0:1], mass[127:128], mass[0:1])
    lines = [targets[side][0:48, :] for side in range(4)]
    ends = {}
    for side in range(4):
        local_mass = share_lanes(mass_lines[side])
        for high in (False, True):
            ends[side, high] = pack_end(lines[side][0:24], high) + pack_mass(local_mass, high)
    extras = (
        ends[UPPER, True] + turn(ends[LOWER, True], 12),
        ends[UPPER, False] + turn(ends[LOWER, False], 12),
        ends[LEFT, True] + turn(ends[RIGHT, True], 12),
        ends[LEFT, False] + turn(ends[RIGHT, False], 12),
    )
    for side in range(4):
        targets[side][48:56, :] = extras[side] + fold_line(mass_lines[side])
    for number, (along, upward) in enumerate(((UPPER, True), (LOWER, False))):
        for across, sideways in ((RIGHT, True), (LEFT, False)):
            tile = ends[along, sideways] + turn(ends[across, upward], 12)
            tile = tile + turn(pack_end(lines[along][24:48], sideways), 48)
            targets[across][56 + 8 * number : 64 + 8 * number, :] = tile
    table_copy.wait()
    starts = [
        [pl.multiple_of(jnp.maximum(near_ref[0, 16 * part + place], 0), 8) for part in range(2)]
        for place in range(16)
    ]
    for place in range(16):
        for part in range(2):
            rows = pl.ds(starts[place][part], 48)
            send_ref[place, 48 * part : 48 * part + 48, :] = lines_ref[rows, :]
    for place in range(16):
        tiles = [lines_ref[pl.ds(starts[place][part] + 48, 8), :] for part in range(2)]
        tile = jnp.where(lane_index(8) < 64, tiles[0], turn(tiles[1], 64))
        send_ref[place, 96:104, :] = jnp.where(top_lanes(), top, tile)


def block_kernel(
    velocity_ref, height_ref, coriolis_ref, elem_mass_ref, along_x_ref, tiles_ref, after_ref,
    partial_ref, node_mass, inner_inverse,
):
    lane = lane_index(128)
    step = pl.program_id(0)

    @pl.when(step == 0)
    def _():
        node_mass[...] = mass_of_nodes(elem_mass_ref[0], tiles_ref)
        local_mass = share_block(node_mass[...])
        row = lax.broadcasted_iota(jnp.int32, (128, 128), 0)
        inner = (row > 0) & (row < 127) & (lane > 0) & (lane < 127)
        inner_inverse[...] = jnp.where(inner, 1.0 / local_mass, 0.0)

    @pl.when(step < 8)
    def _():
        _, changed = changes(
            velocity_ref[0, 0], velocity_ref[1, 0], height_ref[0], coriolis_ref[0],
            node_mass[...], inner_inverse[...], share_block, along_x_ref, tiles_ref,
        )
        for part in range(3):
            partial_ref[part] = changed[part]

    @pl.when(step == 8)
    def _():
        partial_ref[0] = share_block(node_mass[...])


def pack_kernel(table_ref, received_ref, after_ref, ahead_ref, behind_ref, top_ref):
    top = jnp.zeros((8, 128), f32)
    for place in range(16):
        top = jnp.maximum(top, received_ref[place, 96:104, :])
    top = jnp.max(jnp.where(top_lanes(), top, 0.0), axis=(0, 1), keepdims=True)
    top_ref[...] = jnp.broadcast_to(top, top_ref.shape)
    for base, ref in ((48, ahead_ref), (51, behind_ref)):
        ref[0:48, :] = received_ref[table_ref[0, base], 48:96, :]
        for number in range(3):
            tile = received_ref[table_ref[0, base + number], 96:104, :]
            ref[48 + 8 * number : 56 + 8 * number, :] = turn(tile, 64)


def edge_terms(table_ref, lines, received_ref, ahead_ref, behind_ref, tiles_ref):
    lane = lane_index(1)

    def message(way, start, stop):
        kind = table_ref[0, 40 + way]
        skip = 48 if start == 48 else 0
        values = received_ref[table_ref[0, 32 + way], start + skip : stop + skip, :]
        step_y, step_x = steps8[way]
        if step_x != 0:
            crossed = ahead_ref if step_x > 0 else behind_ref
            shift = (0, 16, 8)[step_y]
            values = jnp.where(kind == 2, crossed[start + shift : stop + shift, :], values)
        return jnp.where(kind > 0, values, 0.0)

    own = [line[0:24, :] for line in lines]
    own_mass = [unfold_line(line[48:56, :]) for line in lines]
    near = [message(side, 0, 24) for side in range(4)]
    change = [message(side, 24, 48) for side in range(4)]
    extra = [message(side, 48, 56) for side in range(4)]
    mass = [unfold_line(extra[side]) for side in range(4)]
    shared_mass = [share_lanes(mass[side]) for side in range(4)]
    total = [own[side] + near[side] for side in range(4)]
    total_mass = [share_lanes(own_mass[side]) + shared_mass[side] for side in range(4)]
    corners = []
    for along in (UPPER, LOWER):
        for across in (RIGHT, LEFT):
            corner = 4 + 2 * (along - UPPER) + across
            at_x = 127 if across == RIGHT else 0
            at_y = 127 if along == UPPER else 0
            tile = message(corner, 48, 56)
            end_x = 0 if across == RIGHT else 3

            def spread_out(packed, start, at_x=at_x):
                return jnp.concatenate(
                    [turn(packed, at_x - start - 4 * part) for part in range(3)], 0
                )

            far = spread_out(tile, end_x)
            far_mass = turn(tile, at_x - 24 - end_x)[0:1]
            corners.append((along, across, at_x, at_y, tile, far_mass, spread_out))
            on_x, on_y = lane == at_x, lane == at_y
            total[along] = total[along] + jnp.where(
                on_x, turn(near[across], at_x - at_y) + far, 0.0
            )
            total_mass[along] = total_mass[along] + jnp.where(
                on_x, turn(mass[across], at_x - at_y) + far_mass, 0.0
            )
            total[across] = total[across] + jnp.where(
                on_y, turn(near[along] + far, at_y - at_x), 0.0
            )
            total_mass[across] = total_mass[across] + jnp.where(
                on_y, turn(mass[along] + far_mass, at_y - at_x), 0.0
            )
    smooth = [total[side] / total_mass[side] for side in range(4)]
    curve = [second_lanes(smooth[side], tiles_ref) for side in range(4)]
    added = [
        change[side]
        - hyper_coef
        * (shared_mass[side] * CENTRE * smooth[side] + share_lanes(mass[side] * curve[side]))
        for side in range(4)
    ]

    def arm(beside, diagonal, coefs):
        both = beside + diagonal
        weight = jnp.broadcast_to(turn(both, -24)[0:1], (8, 128))
        value = jnp.where(weight > 0.0, both / jnp.where(weight > 0.0, weight, 1.0), 0.0) * coefs
        value = value + turn(value, -1)
        return value + turn(value, -2)

    for along, across, at_x, at_y, tile, far_mass, spread_out in corners:
        beside = extra[across] if along == UPPER else turn(extra[across], -12)
        arm_x = spread_out(arm(beside, tile, tiles_ref[21 if across == RIGHT else 22]), 0)
        beside = extra[along] if across == LEFT else turn(extra[along], -12)
        arm_y = spread_out(
            arm(beside, turn(tile, -12), tiles_ref[21 if along == UPPER else 22]), 0
        )
        middle = CENTRE * smooth[along]
        arm_x, arm_y = arm_x + middle, arm_y + middle
        own_x = curve[along]
        own_y = turn(curve[across], at_x - at_y)
        mass_x = turn(mass[across], at_x - at_y)
        end_x = 0 if across == RIGHT else 3
        value = (
            turn(change[across], at_x - at_y) + change[along] + spread_out(tile, 48 + end_x)
        ) - hyper_coef * (
            mass_x * (arm_x + own_y) + mass[along] * (own_x + arm_y) + far_mass * (arm_x + arm_y)
        )
        added[along] = jnp.where(lane == at_x, value, added[along])
    ends = (lane == 0) | (lane == 127)
    plain, edge = [], []
    for side in range(4):
        line = smooth[side] if side >= UPPER else jnp.where(ends, 0.0, smooth[side])
        outside = added[side] if side >= UPPER else jnp.where(ends, 0.0, added[side])
        bend = curve[side] if side >= UPPER else second_lanes(line, tiles_ref)
        plain.append(share_lanes(own_mass[side] * line))
        edge.append(outside - hyper_coef * share_lanes(own_mass[side] * bend))
    return plain, edge, total_mass


def last_kernel(
    table_ref, lines_ref, received_ref, ahead_ref, behind_ref, tops_ref, tiles_ref, widen_ref,
    velocity_far, height_far, partial_far, new_velocity_far, new_height_far,
    rows, velocity_ref, height_ref, partial_ref, arrived, left_off,
):
    lane = lane_index(128)
    mass_in = pltpu.make_async_copy(partial_far.at[24], partial_ref.at[24], arrived.at[3, 0])
    mass_in.start()
    incoming = []
    for group in range(GROUPS):
        part = pl.ds(LEVELS_EACH * group, LEVELS_EACH)
        incoming.append(
            (
                pltpu.make_async_copy(
                    partial_far.at[pl.ds(3 * LEVELS_EACH * group, 3 * LEVELS_EACH)],
                    partial_ref.at[pl.ds(3 * LEVELS_EACH * group, 3 * LEVELS_EACH)],
                    arrived.at[0, group],
                ),
                pltpu.make_async_copy(
                    velocity_far.at[:, part], velocity_ref.at[:, part], arrived.at[1, group]
                ),
                pltpu.make_async_copy(
                    height_far.at[part], height_ref.at[part], arrived.at[2, group]
                ),
            )
        )
        for copy in incoming[-1]:
            copy.start()

    lines = [lines_ref.at[pl.ds(STARTS[side], 56)] for side in range(4)]
    plain, edge, total_mass = edge_terms(
        table_ref, lines, received_ref, ahead_ref, behind_ref, tiles_ref
    )
    rows[0] = plain[UPPER]
    rows[1] = plain[LOWER]
    rows[2] = edge[UPPER]
    rows[3] = edge[LOWER]
    stacked = jnp.concatenate(
        [plain[LEFT], plain[RIGHT], edge[LEFT], edge[RIGHT]]
        + [jnp.broadcast_to(total_mass[side], (16, 128)) for side in (LEFT, RIGHT)],
        0,
    )
    columns = jnp.transpose(stacked)
    mass_in.wait()
    mass = partial_ref[24]
    mass = jnp.where(lane == 0, columns[:, 96:97], mass)
    mass = jnp.where(lane == 127, columns[:, 112:113], mass)
    row = lax.broadcasted_iota(jnp.int32, (128, 128), 0)
    mass = jnp.where(row == 127, total_mass[UPPER], mass)
    mass = jnp.where(row == 0, total_mass[LOWER], mass)
    top = jnp.max(tops_ref[...], axis=(0, 1), keepdims=True)
    factor = (courant / top) / mass
    near_edge = (lane < 5) | (lane > 122)
    widened = product(columns, widen_ref[...])
    row = lax.broadcasted_iota(jnp.int32, (8, 128), 0)
    outgoing = []
    for group in range(GROUPS):
        for copy in incoming[group]:
            copy.wait()
        for level in range(LEVELS_EACH * group, LEVELS_EACH * (group + 1)):
            for part in range(3):
                at = 8 * part + level
                half = 128 * (at // 12)
                beside = turn(widened[:, half : half + 128], 123 - 10 * (at % 12))
                value = partial_ref[3 * level + part] + jnp.where(near_edge, beside, 0.0)
                upper = tiles_ref[23] * rows[0, at : at + 1, :]
                lower = tiles_ref[24] * rows[1, at : at + 1, :]
                upper = upper + jnp.where(row == 7, rows[2, at : at + 1, :], 0.0)
                lower = lower + jnp.where(row == 0, rows[3, at : at + 1, :], 0.0)
                value = jnp.concatenate([value[:8] + lower, value[8:120], value[120:] + upper], 0)
                if part < 2:
                    velocity_ref[part, level] = velocity_ref[part, level] + factor * value
                else:
                    height_ref[level] = height_ref[level] + factor * value
        part = pl.ds(LEVELS_EACH * group, LEVELS_EACH)
        for copy in (
            pltpu.make_async_copy(
                velocity_ref.at[:, part], new_velocity_far.at[:, part], left_off.at[0, group]
            ),
            pltpu.make_async_copy(
                height_ref.at[part], new_height_far.at[part], left_off.at[1, group]
            ),
        ):
            copy.start()
            outgoing.append(copy)
    for copy in outgoing:
        copy.wait()


def whole(shape, space=None):
    if space is None:
        return pl.BlockSpec(shape, lambda level: (0,) * len(shape))
    return pl.BlockSpec(memory_space=space)


def per_device(velocity, thickness, coriolis, elem_mass, block_owner):
    cols_b = block_owner.shape[1]
    count = 4 * cols_b
    velocity = velocity[:, :, 0]
    thickness = thickness[:, 0]
    widen, along_x, tiles = constant_tables()
    device = (lax.axis_index("elem") * lax.axis_size("sub") + lax.axis_index("sub")).reshape(1)
    if cols_b < 128:
        block_owner = jnp.pad(block_owner, ((0, 0), (0, 128 - cols_b)), constant_values=-1)
    shape = jax.ShapeDtypeStruct
    params = pltpu.CompilerParams(
        dimension_semantics=("arbitrary",), vmem_limit_bytes=BLOCK_VMEM
    )
    vmem = pltpu.VMEM
    far = pl.BlockSpec(memory_space=pltpu.HBM)
    held = pl.BlockSpec(memory_space=vmem)
    small = pl.BlockSpec(memory_space=pltpu.SMEM)
    arrays = (block_owner, velocity, thickness, coriolis, elem_mass, along_x, tiles)
    lines, send, table = pl.pallas_call(
        functools.partial(edge_kernel, cols_b),
        in_specs=[small] + [far] * 7,
        out_specs=[held] * 3,
        out_shape=[
            shape((256, 128), f32), shape((16, 104, 128), f32), shape((1, 128), jnp.int32),
        ],
        scratch_shapes=[
            pltpu.VMEM((2, 3, 128, 128), f32), pltpu.VMEM((2, 3, 128, 128), f32),
            pltpu.VMEM(block_owner.shape, jnp.int32), pltpu.SMEM((1, 128), jnp.int32),
        ]
        + [pltpu.VMEM(array.shape, array.dtype) for array in arrays[1:]]
        + [pltpu.SemaphoreType.DMA((8,))],
        compiler_params=pltpu.CompilerParams(vmem_limit_bytes=EDGE_VMEM),
        name="edge",
    )(device, *arrays)
    squares = count // 16
    same_place = [[16 * s + i for s in range(squares)] for i in range(16)]
    same_square = [[16 * s + i for i in range(16)] for s in range(squares)]
    received = lax.all_to_all(
        send, axes, 0, 0, axis_index_groups=same_square, tiled=True
    )
    pair = pl.BlockSpec((2, 1, 128, 128), lambda step: (0, jnp.minimum(step, 7), 0, 0))
    single = pl.BlockSpec((1, 128, 128), lambda step: (jnp.minimum(step, 7), 0, 0))
    partial = pl.pallas_call(
        block_kernel,
        grid=(9,),
        in_specs=[
            pair, single, whole((1, 128, 128)), whole((1, 32, 32)), whole((2, 384, 128)),
            whole((45, 8, 128)), whole((1, 8, 128)),
        ],
        out_specs=pl.BlockSpec((3, 128, 128), lambda step: (step, 0, 0)),
        out_shape=shape((27, 128, 128), f32),
        scratch_shapes=[pltpu.VMEM((128, 128), f32), pltpu.VMEM((128, 128), f32)],
        compiler_params=params,
        cost_estimate=pl.CostEstimate(
            flops=2_000_000_000, bytes_accessed=3_200_000, transcendentals=0
        ),
        name="block",
    )(velocity, thickness, coriolis, elem_mass, along_x, tiles, send)
    to_ahead, to_behind, top = pl.pallas_call(
        pack_kernel,
        grid=(1,),
        in_specs=[
            whole((1, 128), pltpu.SMEM), whole((16, 104, 128)),
            pl.BlockSpec((1, 8, 128), lambda step: (0, 0, 0)),
        ],
        out_specs=[
            whole((72, 128)), whole((72, 128)), whole((squares * TOP_ROWS, 128)),
        ],
        out_shape=[
            shape((72, 128), f32), shape((72, 128), f32), shape((squares * TOP_ROWS, 128), f32),
        ],
        compiler_params=pltpu.CompilerParams(vmem_limit_bytes=PACK_VMEM),
        name="pack",
    )(table, received, partial)
    tops = lax.all_to_all(top, axes, 0, 0, axis_index_groups=same_place, tiled=True)
    ahead = lax.ppermute(to_behind, axes, [(b, (b - 16) % count) for b in range(count)])
    behind = lax.ppermute(to_ahead, axes, [(b, (b + 16) % count) for b in range(count)])
    new_velocity, new_thickness = pl.pallas_call(
        last_kernel,
        in_specs=[small] + [held] * 7 + [far] * 3,
        out_specs=[far] * 2,
        out_shape=[shape((2, 8, 128, 128), f32), shape((8, 128, 128), f32)],
        scratch_shapes=[
            pltpu.VMEM((4, 24, 128), f32), pltpu.VMEM((2, 8, 128, 128), f32),
            pltpu.VMEM((8, 128, 128), f32), pltpu.VMEM((25, 128, 128), f32),
            pltpu.SemaphoreType.DMA((4, GROUPS)), pltpu.SemaphoreType.DMA((2, GROUPS)),
        ],
        compiler_params=pltpu.CompilerParams(vmem_limit_bytes=LAST_VMEM),
        name="last",
    )(table, lines, received, ahead, behind, tops, tiles, widen, velocity, thickness, partial)
    return new_velocity[:, :, None], new_thickness[:, None]


def solution(mesh):
    return jax.shard_map(
        per_device,
        mesh=mesh,
        in_specs=(
            P(None, None, axes, None, None),
            P(None, axes, None, None),
            P(axes, None, None),
            P(axes, None, None),
            P(),
        ),
        out_specs=(
            P(None, None, axes, None, None),
            P(None, axes, None, None),
        ),
        check_vma=False,
    )
```
